32 devices in a mesh: blk: 2 (over y), tiles: 16 (over z, x, core).
Axes of the slice: x: 2, y: 2, z: 4, core: 2. Of those that a mesh axis runs over, the one named last changes fastest.
Arguments:
- tensor_tiles: bfloat16 [2, 32, 64, 4096], P('blk', 'tiles'), may hold values from -6 to 6
- tile_iblock: int32 [2, 32], P('blk', 'tiles'), may hold values from 0 to 1
- tile_jslot: int32 [2, 32], P('blk', 'tiles'), may hold values from 0 to 1, as said below
- tile_kslot: int32 [2, 32], P('blk', 'tiles'), may hold values from 0 to 1, as said below
- block_jlist: int32 [2, 32], P('blk', 'tiles'), may hold values from 0 to 255, as said below
- block_klist: int32 [2, 32], P('blk', 'tiles'), may hold values from 0 to 63, as said below
- factor_b: bfloat16 [256, 64, 512], P(None, 'tiles'), may hold values from -0.5 to 0.5
- factor_c: bfloat16 [64, 64, 512], P(None, 'tiles'), may hold values from -0.75 to 0.75
Outputs:
- mttkrp: float32 [2048, 512], P(('blk', 'tiles'))
The draws below stay inside these ranges and needn't reach their ends.
Inputs may be any that keep to these rules, and one draw needn't show every extreme that they name: `block_jlist`: the 2 entries of one device's list are distinct. `block_klist`: the 2 entries of one device's list are distinct. `tile_jslot`: one device's tiles use between 1 and 2 distinct positions, and all 2 on some device. `tile_kslot`: one device's tiles use between 1 and 2 distinct positions, and all 2 on some device.
All inputs are finite; a program needn't handle non-finite values.
Results may differ from the reference program's by a relative error of at most 0.011.
Values may be sent and summed in bfloat16 or wider, within the bound.
No kernel may reach another device: no remote copies, remote signals or barrier semaphores. Data moves between devices by JAX's collectives and lax.ppermute only.
A program may use at most 64 MiB of HBM per device.

```python
import jax
import jax.numpy as jnp
from jax import lax

TI = 64
TJ = 64
TK = 64
RANK = 512
TPD = 2
DIST = 2
JB = 256
KB = 64
TILE_COLS = 32
N_BLK = 2
N_TILES = 16


def slot_positions(key):
    devices = N_BLK * N_TILES
    key_count, key_top, key_fill, key_order = jax.random.split(key, 4)
    counts = jax.random.randint(key_count, (devices,), 1, DIST + 1)
    chosen = jax.random.randint(key_top, (), 0, devices)
    counts = jnp.where(jnp.arange(devices) == chosen, DIST, counts)
    position = jnp.arange(TPD)
    filler = jax.random.randint(key_fill, (devices, TPD), 0, 65536) % counts[:, None]
    slots = jnp.where(position[None, :] < counts[:, None], position[None, :], filler)
    scores = jax.random.randint(key_order, (devices, TPD), 0, 65536) * TPD + position[None, :]
    order = jnp.argsort(scores, axis=1)
    slots = jnp.take_along_axis(slots, order, axis=1)
    return slots.reshape(N_BLK, N_TILES * TPD).astype(jnp.int32)


def distinct_lists(key, total):
    devices = N_BLK * N_TILES
    scores = jax.random.randint(key, (devices, total), 0, 65536) * total + jnp.arange(total)[None, :]
    order = jnp.argsort(scores, axis=1)[:, :DIST]
    return order.reshape(N_BLK, N_TILES * DIST).astype(jnp.int32)


def draw_tile_jslot(key, part):
    return slot_positions(jax.random.fold_in(key, 11))


def draw_tile_kslot(key, part):
    return slot_positions(jax.random.fold_in(key, 23))


def draw_block_jlist(key, part):
    return distinct_lists(jax.random.fold_in(key, 37), JB)


def draw_block_klist(key, part):
    return distinct_lists(jax.random.fold_in(key, 41), KB)


def plant(entries, key, smallest, high):
    extent = entries.shape
    place = [jax.random.randint(jax.random.fold_in(key, axis), (), 0, extent[axis]) for axis in range(len(extent))]
    entries = entries.at[tuple(place)].set(smallest)
    longest = extent.index(max(extent))
    place[longest] = (place[longest] + 1) % extent[longest]
    return entries.at[tuple(place)].set(high)


def level_of(key, dims, shards, least, largest):
    def one(dim, parts):
        steps = jax.random.uniform(jax.random.fold_in(jax.random.fold_in(key, 6), dim), (parts,), jnp.float32, least / len(shards), largest / len(shards))
        return jnp.repeat(jnp.exp(steps), dims[dim] // parts).reshape((-1,) + (1,) * (len(dims) - dim - 1))

    gain = one(*shards[0])
    for cut in shards[1:]:
        gain = gain * one(*cut)
    return gain


def noise(key, extent, width, most, cuts=(), kind=jnp.bfloat16):
    factor_of = level_of(key, extent, cuts, -0.22, 0.18) if cuts else 1.0
    values = jax.random.normal(key, extent, jnp.float32) * width * factor_of
    return jnp.minimum(jnp.maximum(values, -most), most).astype(kind)


def setup_inputs(seed: int = 0) -> dict:
    keys = jax.random.split(jax.random.key(seed), 9)
    return {
        "tensor_tiles": noise(keys[0], (N_BLK, TILE_COLS, TI, TJ * TK), 1.0, 6.0, ((0, 2), (1, 16))),
        "tile_iblock": plant(jax.random.randint(keys[1], (N_BLK, TILE_COLS), 0, N_BLK), jax.random.fold_in(keys[1], 1), 0, N_BLK - 1).astype(jnp.int32),
        "tile_jslot": draw_tile_jslot(jax.random.fold_in(keys[8], 71), 0),
        "tile_kslot": draw_tile_kslot(jax.random.fold_in(keys[8], 71), 0),
        "block_jlist": draw_block_jlist(jax.random.fold_in(keys[8], 71), 0),
        "block_klist": draw_block_klist(jax.random.fold_in(keys[8], 71), 0),
        "factor_b": noise(keys[6], (JB, TJ, RANK), (TJ * TPD) ** -0.5, 0.5, ((1, 16),)),
        "factor_c": noise(keys[7], (KB, TK, RANK), TK ** -0.5, 0.75, ((1, 16),)),
    }


def device_partial(tiles, iblock, jslot, kslot, jlist, klist, factor_b, factor_c):
    def accumulate(which, partial_value):
        tile_block = tiles[which].astype(jnp.float32)
        mode_two = factor_b[jlist[jslot[which]]].astype(jnp.float32)
        mode_three = factor_c[klist[kslot[which]]].astype(jnp.float32)
        contracted = jnp.dot(tile_block.reshape(TI * TJ, TK), mode_three, precision=lax.Precision.HIGHEST)
        term = jnp.sum(contracted.reshape(TI, TJ, RANK) * mode_two[None], axis=1)
        target = iblock[which]
        current = lax.dynamic_index_in_dim(partial_value, target, 0, keepdims=False)
        return lax.dynamic_update_index_in_dim(partial_value, current + term, target, 0)

    partial_value = lax.fori_loop(0, TPD, accumulate, jnp.zeros((N_BLK, TI, RANK), jnp.float32))
    return lax.optimization_barrier(partial_value.astype(jnp.bfloat16)).astype(jnp.float32)


def reference(tensor_tiles, tile_iblock, tile_jslot, tile_kslot, block_jlist, block_klist, factor_b, factor_c):
    def column(column_index):
        tile_start = (column_index * TPD).astype(jnp.int32)
        list_start = (column_index * DIST).astype(jnp.int32)

        def row_partial(row_index):
            tiles = lax.dynamic_slice_in_dim(tensor_tiles[row_index], tile_start, TPD, 0)
            iblock = lax.dynamic_slice_in_dim(tile_iblock[row_index], tile_start, TPD, 0)
            jslot = lax.dynamic_slice_in_dim(tile_jslot[row_index], tile_start, TPD, 0)
            kslot = lax.dynamic_slice_in_dim(tile_kslot[row_index], tile_start, TPD, 0)
            jlist = lax.dynamic_slice_in_dim(block_jlist[row_index], list_start, DIST, 0)
            klist = lax.dynamic_slice_in_dim(block_klist[row_index], list_start, DIST, 0)
            return device_partial(tiles, iblock, jslot, kslot, jlist, klist, factor_b, factor_c)

        def add_row(total, row_index):
            return total + row_partial(row_index), None

        total, unused = lax.scan(add_row, jnp.zeros((N_BLK, TI, RANK), jnp.float32), jnp.arange(N_BLK, dtype=jnp.int32))
        return total

    blocks = lax.map(column, jnp.arange(N_TILES, dtype=jnp.int32))
    return jnp.transpose(blocks, (1, 0, 2, 3)).reshape(N_BLK * N_TILES * TI, RANK)
```

```python
import functools

import jax
import jax.numpy as jnp
from jax import lax
from jax.experimental import pallas as pl
from jax.experimental.pallas import tpu as pltpu
from jax.sharding import PartitionSpec as P


def pick(table, slots):
    entries = jnp.arange(table.shape[0], dtype=jnp.int32)
    return jnp.sum(jnp.where(slots[:, None] == entries[None, :], table[None, :], 0), axis=1)


def gather_rows(asked, factor_b, factor_c):
    peers, wants = asked.shape
    rows, rank = factor_b.shape[1:]

    def kernel(asked_ref, b_ref, c_ref, out_ref):
        for peer in range(peers):
            for want in range(wants):
                source = b_ref if want < wants // 2 else c_ref
                out_ref[peer, want] = source[asked_ref[peer, want]]

    return pl.pallas_call(
        kernel,
        out_shape=jax.ShapeDtypeStruct((peers, wants, rows, rank), factor_b.dtype),
        in_specs=[
            pl.BlockSpec(memory_space=pltpu.SMEM),
            pl.BlockSpec(memory_space=pltpu.VMEM),
            pl.BlockSpec(memory_space=pltpu.VMEM),
        ],
        out_specs=pl.BlockSpec(memory_space=pltpu.VMEM),
        compiler_params=pltpu.CompilerParams(vmem_limit_bytes=8 * 1024 * 1024),
        name="gather_rows",
    )(asked, factor_b, factor_c)


def contract(owners, fetched, tiles, groups):
    peers, wants, rows, rank = fetched.shape
    count, inner, width = tiles.shape
    across = peers * rows
    depth = width // across
    step = max(1, 256 // depth)

    def kernel(owners_ref, fetched_ref, tiles_ref, own_ref, send_ref, factor_ref):
        me = lax.axis_index("blk")
        for want in range(wants):
            for peer in range(peers):
                factor_ref[want, peer * rows : (peer + 1) * rows, :] = fetched_ref[peer, want].astype(jnp.float32)
        terms = []
        for which in range(count):
            mode_three = factor_ref[count + which].astype(jnp.bfloat16)
            term = jnp.zeros((inner, rank), jnp.float32)
            for start in range(0, across, step):
                product = jnp.concatenate(
                    [
                        jnp.broadcast_to(factor_ref[which, j : j + 1, :], (depth, rank)).astype(jnp.bfloat16)
                        * mode_three
                        for j in range(start, start + step)
                    ],
                    axis=0,
                )
                term = term + jnp.dot(
                    tiles_ref[which, :, start * depth : (start + step) * depth],
                    product,
                    preferred_element_type=jnp.float32,
                )
            terms.append(term)
        for shift in range(groups):
            group = lax.rem(me + shift, groups)
            total = jnp.zeros((inner, rank), jnp.float32)
            for which in range(count):
                total = total + jnp.where(owners_ref[0, which] == group, terms[which], 0.0)
            rounded = total.astype(jnp.bfloat16)
            if shift == 0:
                own_ref[...] = rounded
            else:
                send_ref[shift - 1] = rounded

    return pl.pallas_call(
        kernel,
        out_shape=(
            jax.ShapeDtypeStruct((inner, rank), jnp.bfloat16),
            jax.ShapeDtypeStruct((groups - 1, inner, rank), jnp.bfloat16),
        ),
        in_specs=[
            pl.BlockSpec(memory_space=pltpu.SMEM),
            pl.BlockSpec(memory_space=pltpu.VMEM),
            pl.BlockSpec(memory_space=pltpu.VMEM),
        ],
        out_specs=(pl.BlockSpec(memory_space=pltpu.VMEM), pl.BlockSpec(memory_space=pltpu.VMEM)),
        scratch_shapes=[pltpu.VMEM((wants, across, rank), jnp.float32)],
        compiler_params=pltpu.CompilerParams(vmem_limit_bytes=16 * 1024 * 1024),
        name="contract",
    )(owners, fetched, tiles)


def per_device(
    tensor_tiles, tile_iblock, tile_jslot, tile_kslot, block_jlist, block_klist, factor_b, factor_c
):
    groups = lax.axis_size("blk")
    wanted = jnp.concatenate([pick(block_jlist[0], tile_jslot[0]), pick(block_klist[0], tile_kslot[0])])
    asked = lax.all_gather(wanted, "tiles", axis=0)
    rows = gather_rows(asked, factor_b, factor_c)
    fetched = lax.all_to_all(rows, "tiles", split_axis=0, concat_axis=0, tiled=True)
    own, send = contract(tile_iblock, fetched, tensor_tiles[0], groups)
    total = own.astype(jnp.float32)
    for shift in range(1, groups):
        arrived = lax.ppermute(
            send[shift - 1], "blk", [(i, (i + shift) % groups) for i in range(groups)]
        )
        total = total + arrived.astype(jnp.float32)
    return total


def solution(mesh):
    placed = (
        P("blk", "tiles", None, None),
        P("blk", "tiles"),
        P("blk", "tiles"),
        P("blk", "tiles"),
        P("blk", "tiles"),
        P("blk", "tiles"),
        P(None, "tiles", None),
        P(None, "tiles", None),
    )
    return jax.shard_map(
        per_device, mesh=mesh, in_specs=placed, out_specs=P(("blk", "tiles"), None), check_vma=False
    )
```

```python
import jax
import jax.numpy as jnp
from jax import lax
from jax.experimental import pallas as pl
from jax.experimental.pallas import tpu as pltpu
from jax.sharding import PartitionSpec as P

MIB = 1024 * 1024


def pick(table, slots):
    entries = jnp.arange(table.shape[0], dtype=jnp.int32)
    return jnp.sum(jnp.where(slots[:, None] == entries[None, :], table[None, :], 0), axis=1)


def across_tiles(array, distance):
    size = lax.axis_size("tiles")
    return lax.ppermute(array, "tiles", [(at, at ^ distance) for at in range(size)])


def gather_rows(asked, count, mine, paired):
    chips = len(asked)
    wants = 2 * count
    rows, rank = mine[0].shape[1:]
    words = asked[0].shape[0]

    def kernel(*refs):
        asked_refs, (mine_b, mine_c, pair_b, pair_c) = refs[:chips], refs[chips : chips + 4]
        outs, (index_ref, sem, row_sem) = refs[chips + 4 : -3], refs[-3:]
        copies = [
            pltpu.make_async_copy(asked_refs[chip], index_ref.at[chip], sem.at[chip]) for chip in range(chips)
        ]
        for copy in copies:
            copy.start()
        side = lax.rem(lax.axis_index("tiles"), 2)
        pending = []
        for chip in range(chips):
            copies[chip].wait()
            for want in range(wants):
                own = mine_b if want < count else mine_c
                pending.append(
                    pltpu.make_async_copy(
                        own.at[index_ref[chip, want]], outs[chip].at[want, side], row_sem.at[chip, want]
                    )
                )
                pending[-1].start()
        for chip in range(chips):
            for want in range(wants):
                other = pair_b if want < count else pair_c
                outs[chip][want, 1 - side] = other[index_ref[chip, want]]
        for copy in pending:
            copy.wait()

    return pl.pallas_call(
        kernel,
        out_shape=[jax.ShapeDtypeStruct((wants, 2, rows, rank), mine[0].dtype)] * chips,
        in_specs=[pl.BlockSpec(memory_space=pl.ANY)] * (chips + 2) + [pl.BlockSpec(memory_space=pltpu.VMEM)] * 2,
        out_specs=[pl.BlockSpec(memory_space=pltpu.VMEM)] * chips,
        scratch_shapes=[
            pltpu.SMEM((chips, words), jnp.int32),
            pltpu.SemaphoreType.DMA((chips,)),
            pltpu.SemaphoreType.DMA((chips, wants)),
        ],
        compiler_params=pltpu.CompilerParams(vmem_limit_bytes=8 * MIB),
        name="gather_rows",
    )(*asked, *mine, *paired)


def contract(wanted, fetched, tiles, groups):
    chips = len(fetched)
    wants, halves, rows, rank = fetched[0].shape
    count, inner, width = tiles.shape
    chunk = halves * rows
    across = chips * chunk
    depth = width // across
    step = max(1, 256 // depth)

    def kernel(wanted_ref, *refs):
        fetched_refs, (tiles_ref, own_ref, send_ref, piece_ref, factor_ref, index_ref, sem) = refs[:chips], refs[chips:]
        copy = pltpu.make_async_copy(wanted_ref, index_ref, sem)
        copy.start()
        me = lax.axis_index("blk")
        here = lax.axis_index("tiles") // 2
        for apart in range(chips):
            chip = jnp.bitwise_xor(here, apart)
            for want in range(wants):
                for half in range(halves):
                    piece_ref[want, chip, half] = fetched_refs[apart][want, half].astype(jnp.float32)
        for want in range(wants):
            for at in range(chips * halves):
                factor_ref[want, at * rows : (at + 1) * rows, :] = piece_ref[want, at // halves, at % halves]
        terms = []
        for which in range(count):
            mode_three = factor_ref[count + which].astype(jnp.bfloat16)
            term = jnp.zeros((inner, rank), jnp.float32)
            for start in range(0, across, step):
                product = jnp.concatenate(
                    [
                        jnp.broadcast_to(factor_ref[which, j : j + 1, :], (depth, rank)).astype(jnp.bfloat16)
                        * mode_three
                        for j in range(start, start + step)
                    ],
                    axis=0,
                )
                term = term + jnp.dot(
                    tiles_ref[which, :, start * depth : (start + step) * depth],
                    product,
                    preferred_element_type=jnp.float32,
                )
            terms.append(term)
        copy.wait()
        for shift in range(groups):
            group = lax.rem(me + shift, groups)
            total = jnp.zeros((inner, rank), jnp.float32)
            for which in range(count):
                total = total + jnp.where(index_ref[2 * count + which] == group, terms[which], 0.0)
            rounded = total.astype(jnp.bfloat16)
            if shift == 0:
                own_ref[...] = rounded
            else:
                send_ref[shift - 1] = rounded

    return pl.pallas_call(
        kernel,
        out_shape=(
            jax.ShapeDtypeStruct((inner, rank), jnp.bfloat16),
            jax.ShapeDtypeStruct((groups - 1, inner, rank), jnp.bfloat16),
        ),
        in_specs=[pl.BlockSpec(memory_space=pl.ANY)] + [pl.BlockSpec(memory_space=pltpu.VMEM)] * (chips + 1),
        out_specs=(pl.BlockSpec(memory_space=pltpu.VMEM), pl.BlockSpec(memory_space=pltpu.VMEM)),
        scratch_shapes=[
            pltpu.VMEM((wants, chips, halves, rows, rank), jnp.float32),
            pltpu.VMEM((wants, across, rank), jnp.float32),
            pltpu.SMEM(wanted.shape, jnp.int32),
            pltpu.SemaphoreType.DMA,
        ],
        compiler_params=pltpu.CompilerParams(vmem_limit_bytes=16 * MIB),
        name="contract",
    )(wanted, *fetched, tiles)


def per_device(
    tensor_tiles, tile_iblock, tile_jslot, tile_kslot, block_jlist, block_klist, factor_b, factor_c
):
    groups = lax.axis_size("blk")
    chips = lax.axis_size("tiles") // 2
    count = tensor_tiles.shape[1]
    mine = (factor_b, factor_c)
    paired = [across_tiles(factor, 1) for factor in mine]
    wanted = jnp.concatenate(
        [pick(block_jlist[0], tile_jslot[0]), pick(block_klist[0], tile_kslot[0]), tile_iblock[0]]
    )
    order = list(range(chips - 1, 0, -1))
    asked = {apart: across_tiles(wanted, 2 * apart) for apart in order}
    rows = gather_rows([wanted] + [asked[apart] for apart in range(1, chips)], count, mine, paired)
    fetched = {apart: across_tiles(rows[apart], 2 * apart) for apart in order}
    own, send = contract(
        wanted, [rows[0]] + [fetched[apart] for apart in range(1, chips)], tensor_tiles[0], groups
    )
    total = own.astype(jnp.float32)
    for shift in range(1, groups):
        arrived = lax.ppermute(
            send[shift - 1], "blk", [(i, (i + shift) % groups) for i in range(groups)]
        )
        total = total + arrived.astype(jnp.float32)
    return total


def solution(mesh):
    placed = (
        P("blk", "tiles", None, None),
        P("blk", "tiles"),
        P("blk", "tiles"),
        P("blk", "tiles"),
        P("blk", "tiles"),
        P("blk", "tiles"),
        P(None, "tiles", None),
        P(None, "tiles", None),
    )
    return jax.shard_map(
        per_device, mesh=mesh, in_specs=placed, out_specs=P(("blk", "tiles"), None), check_vma=False
    )
```

```python
import jax
import jax.numpy as jnp
from jax import lax
from jax.experimental import pallas as pl
from jax.experimental.pallas import tpu as pltpu
from jax.sharding import PartitionSpec as P

MIB = 1024 * 1024
LANES = 128


def in_hbm(*arrays):
    return [pltpu.with_memory_space_constraint(array, pltpu.HBM) for array in arrays]


def make_requests(peers, owners, slots_two, slots_three, list_two, list_three):
    count = owners.shape[1]
    listed = list_two.shape[1]

    def kernel(owners_hbm, *refs):
        hbm, out_ref, held, sem = (owners_hbm, *refs[:4]), refs[4], refs[5:10], refs[10]
        copies = [pltpu.make_async_copy(source, target, sem.at[at]) for at, (source, target) in enumerate(zip(hbm, held))]
        for copy in copies:
            copy.start()
        for copy in copies:
            copy.wait()
        own, slot_two, slot_three, two, three = held
        words = []
        for slot, table in ((slot_two, two), (slot_three, three)):
            for which in range(count):
                word = table[0, 0]
                for entry in range(1, listed):
                    word = jnp.where(slot[0, which] == entry, table[0, entry], word)
                words.append(word)
        words.extend(own[0, which] for which in range(count))
        lane = lax.broadcasted_iota(jnp.int32, (1, LANES), 1)
        row = jnp.zeros((1, LANES), jnp.int32)
        for at, word in enumerate(words):
            row = jnp.where(lane == at, word, row)
        for peer in range(peers):
            out_ref[peer] = row

    small = (owners, slots_two, slots_three, list_two, list_three)
    return pl.pallas_call(
        kernel,
        out_shape=jax.ShapeDtypeStruct((peers, 1, LANES), jnp.int32),
        in_specs=[pl.BlockSpec(memory_space=pltpu.HBM)] * 5,
        out_specs=pl.BlockSpec(memory_space=pltpu.VMEM),
        scratch_shapes=[pltpu.SMEM(array.shape, jnp.int32) for array in small] + [pltpu.SemaphoreType.DMA((5,))],
        name="make_requests",
    )(*small)


def gather_rows(asked, count, factor_b, factor_c):
    peers = asked.shape[0]
    wants = 2 * count
    rows, rank = factor_b.shape[1:]

    def kernel(asked_ref, b_ref, c_ref, out_ref, index_ref, sem, row_sem):
        copy = pltpu.make_async_copy(asked_ref, index_ref, sem)
        copy.start()
        copy.wait()
        pending = []
        for peer in range(peers):
            for want in range(wants):
                source = b_ref if want < count else c_ref
                pending.append(
                    pltpu.make_async_copy(
                        source.at[index_ref[peer, 0, want]], out_ref.at[peer, want], row_sem.at[peer, want]
                    )
                )
                pending[-1].start()
        for copy in pending:
            copy.wait()

    return pl.pallas_call(
        kernel,
        out_shape=jax.ShapeDtypeStruct((peers, wants, rows, rank), factor_b.dtype),
        in_specs=[
            pl.BlockSpec(memory_space=pl.ANY),
            pl.BlockSpec(memory_space=pltpu.HBM),
            pl.BlockSpec(memory_space=pltpu.HBM),
        ],
        out_specs=pl.BlockSpec(memory_space=pltpu.VMEM),
        scratch_shapes=[
            pltpu.SMEM(asked.shape, jnp.int32),
            pltpu.SemaphoreType.DMA,
            pltpu.SemaphoreType.DMA((peers, wants)),
        ],
        compiler_params=pltpu.CompilerParams(vmem_limit_bytes=8 * MIB),
        name="gather_rows",
    )(asked, factor_b, factor_c)


def contract(requests, fetched, tiles, groups):
    peers, wants, rows, rank = fetched.shape
    count, inner, width = tiles.shape
    across = peers * rows
    depth = width // across
    step = max(1, 256 // depth)

    def kernel(requests_ref, fetched_ref, tiles_ref, own_ref, send_ref, factor_ref, index_ref, sem):
        copy = pltpu.make_async_copy(requests_ref.at[0], index_ref, sem)
        copy.start()
        me = lax.axis_index("blk")
        for want in range(wants):
            for peer in range(peers):
                factor_ref[want, peer * rows : (peer + 1) * rows, :] = fetched_ref[peer, want].astype(jnp.float32)
        terms = []
        for which in range(count):
            mode_three = factor_ref[count + which].astype(jnp.bfloat16)
            term = jnp.zeros((inner, rank), jnp.float32)
            for start in range(0, across, step):
                product = jnp.concatenate(
                    [
                        jnp.broadcast_to(factor_ref[which, j : j + 1, :], (depth, rank)).astype(jnp.bfloat16)
                        * mode_three
                        for j in range(start, start + step)
                    ],
                    axis=0,
                )
                term = term + jnp.dot(
                    tiles_ref[which, :, start * depth : (start + step) * depth],
                    product,
                    preferred_element_type=jnp.float32,
                )
            terms.append(term)
        copy.wait()
        for shift in range(groups):
            group = lax.rem(me + shift, groups)
            total = jnp.zeros((inner, rank), jnp.float32)
            for which in range(count):
                total = total + jnp.where(index_ref[0, 2 * count + which] == group, terms[which], 0.0)
            rounded = total.astype(jnp.bfloat16)
            if shift == 0:
                own_ref[...] = rounded
            else:
                send_ref[shift - 1] = rounded

    return pl.pallas_call(
        kernel,
        out_shape=(
            jax.ShapeDtypeStruct((inner, rank), jnp.bfloat16),
            jax.ShapeDtypeStruct((groups - 1, inner, rank), jnp.bfloat16),
        ),
        in_specs=[
            pl.BlockSpec(memory_space=pl.ANY),
            pl.BlockSpec(memory_space=pltpu.VMEM),
            pl.BlockSpec(memory_space=pltpu.VMEM),
        ],
        out_specs=(pl.BlockSpec(memory_space=pltpu.VMEM), pl.BlockSpec(memory_space=pltpu.VMEM)),
        scratch_shapes=[
            pltpu.VMEM((wants, across, rank), jnp.float32),
            pltpu.SMEM((1, LANES), jnp.int32),
            pltpu.SemaphoreType.DMA,
        ],
        compiler_params=pltpu.CompilerParams(vmem_limit_bytes=16 * MIB),
        name="contract",
    )(requests, fetched, tiles)


def per_device(
    tensor_tiles, tile_iblock, tile_jslot, tile_kslot, block_jlist, block_klist, factor_b, factor_c
):
    groups = lax.axis_size("blk")
    peers = lax.axis_size("tiles")
    count = tensor_tiles.shape[1]
    requests = make_requests(
        peers, *in_hbm(tile_iblock, tile_jslot, tile_kslot, block_jlist, block_klist)
    )
    asked = lax.all_to_all(requests, "tiles", split_axis=0, concat_axis=0, tiled=True)
    rows = gather_rows(asked, count, *in_hbm(factor_b, factor_c))
    fetched = lax.all_to_all(rows, "tiles", split_axis=0, concat_axis=0, tiled=True)
    own, send = contract(requests, fetched, tensor_tiles[0], groups)
    total = own.astype(jnp.float32)
    for shift in range(1, groups):
        arrived = lax.ppermute(
            send[shift - 1], "blk", [(i, (i + shift) % groups) for i in range(groups)]
        )
        total = total + arrived.astype(jnp.float32)
    return total


def solution(mesh):
    placed = (
        P("blk", "tiles", None, None),
        P("blk", "tiles"),
        P("blk", "tiles"),
        P("blk", "tiles"),
        P("blk", "tiles"),
        P("blk", "tiles"),
        P(None, "tiles", None),
        P(None, "tiles", None),
    )
    return jax.shard_map(
        per_device, mesh=mesh, in_specs=placed, out_specs=P(("blk", "tiles"), None), check_vma=False
    )
```

```python
import jax
import jax.numpy as jnp
from jax import lax
from jax.experimental import pallas as pl
from jax.experimental.pallas import tpu as pltpu
from jax.sharding import PartitionSpec as P

MIB = 1024 * 1024
LANES = 128


def in_hbm(*arrays):
    return [pltpu.with_memory_space_constraint(array, pltpu.HBM) for array in arrays]


def make_requests(chips, owners, slots_two, slots_three, list_two, list_three, factor_b, factor_c):
    count = owners.shape[1]
    listed = list_two.shape[1]
    small = (owners, slots_two, slots_three, list_two, list_three)
    factors = (factor_b, factor_c)

    def kernel(*refs):
        sources, outs, held, sem = refs[:7], refs[7:10], refs[10:15], refs[15]
        copies = [
            pltpu.make_async_copy(source, target, sem.at[at])
            for at, (source, target) in enumerate(zip(sources, (*held, *outs[1:])))
        ]
        for copy in copies:
            copy.start()
        for copy in copies[:5]:
            copy.wait()
        own, slot_two, slot_three, two, three = held
        words = []
        for slot, table in ((slot_two, two), (slot_three, three)):
            for which in range(count):
                word = table[0, 0]
                for entry in range(1, listed):
                    word = jnp.where(slot[0, which] == entry, table[0, entry], word)
                words.append(word)
        words.extend(own[0, which] for which in range(count))
        lane = lax.broadcasted_iota(jnp.int32, (1, LANES), 1)
        row = jnp.zeros((1, LANES), jnp.int32)
        for at, word in enumerate(words):
            row = jnp.where(lane == at, word, row)
        for chip in range(chips):
            outs[0][chip] = row
        for copy in copies[5:]:
            copy.wait()

    return pl.pallas_call(
        kernel,
        out_shape=[jax.ShapeDtypeStruct((chips, 1, LANES), jnp.int32)]
        + [jax.ShapeDtypeStruct(factor.shape, factor.dtype) for factor in factors],
        in_specs=[pl.BlockSpec(memory_space=pltpu.HBM)] * 7,
        out_specs=[pl.BlockSpec(memory_space=pltpu.VMEM)] * 3,
        scratch_shapes=[pltpu.SMEM(array.shape, jnp.int32) for array in small] + [pltpu.SemaphoreType.DMA((7,))],
        compiler_params=pltpu.CompilerParams(vmem_limit_bytes=8 * MIB),
        name="make_requests",
    )(*in_hbm(*small, *factors))


def gather_rows(asked, count, mine, paired):
    chips = asked.shape[0]
    wants = 2 * count
    rows, rank = mine[0].shape[1:]

    def kernel(asked_ref, mine_b, mine_c, pair_b, pair_c, out_ref, index_ref, sem):
        copy = pltpu.make_async_copy(asked_ref, index_ref, sem)
        copy.start()
        side = lax.rem(lax.axis_index("tiles"), 2)
        copy.wait()
        for chip in range(chips):
            for want in range(wants):
                own, other = (mine_b, pair_b) if want < count else (mine_c, pair_c)
                block = index_ref[chip, 0, want]
                out_ref[chip, want, side] = own[block]
                out_ref[chip, want, 1 - side] = other[block]

    return pl.pallas_call(
        kernel,
        out_shape=jax.ShapeDtypeStruct((chips, wants, 2, rows, rank), mine[0].dtype),
        in_specs=[pl.BlockSpec(memory_space=pl.ANY)] + [pl.BlockSpec(memory_space=pltpu.VMEM)] * 4,
        out_specs=pl.BlockSpec(memory_space=pltpu.VMEM),
        scratch_shapes=[pltpu.SMEM(asked.shape, jnp.int32), pltpu.SemaphoreType.DMA],
        compiler_params=pltpu.CompilerParams(vmem_limit_bytes=8 * MIB),
        name="gather_rows",
    )(asked, *mine, *paired)


def contract(requests, fetched, tiles, groups):
    chips, wants, halves, rows, rank = fetched.shape
    count, inner, width = tiles.shape
    pieces = chips * halves
    across = pieces * rows
    depth = width // across
    step = max(1, 256 // depth)

    def kernel(requests_ref, fetched_ref, tiles_ref, own_ref, send_ref, factor_ref, index_ref, sem):
        copy = pltpu.make_async_copy(requests_ref.at[0], index_ref, sem)
        copy.start()
        me = lax.axis_index("blk")
        for want in range(wants):
            for at in range(pieces):
                piece = fetched_ref[at // halves, want, at % halves]
                factor_ref[want, at * rows : (at + 1) * rows, :] = piece.astype(jnp.float32)
        terms = []
        for which in range(count):
            mode_three = factor_ref[count + which].astype(jnp.bfloat16)
            term = jnp.zeros((inner, rank), jnp.float32)
            for start in range(0, across, step):
                product = jnp.concatenate(
                    [
                        jnp.broadcast_to(factor_ref[which, j : j + 1, :], (depth, rank)).astype(jnp.bfloat16)
                        * mode_three
                        for j in range(start, start + step)
                    ],
                    axis=0,
                )
                term = term + jnp.dot(
                    tiles_ref[which, :, start * depth : (start + step) * depth],
                    product,
                    preferred_element_type=jnp.float32,
                )
            terms.append(term)
        copy.wait()
        for shift in range(groups):
            group = lax.rem(me + shift, groups)
            total = jnp.zeros((inner, rank), jnp.float32)
            for which in range(count):
                total = total + jnp.where(index_ref[0, 2 * count + which] == group, terms[which], 0.0)
            rounded = total.astype(jnp.bfloat16)
            if shift == 0:
                own_ref[...] = rounded
            else:
                send_ref[shift - 1] = rounded

    return pl.pallas_call(
        kernel,
        out_shape=(
            jax.ShapeDtypeStruct((inner, rank), jnp.bfloat16),
            jax.ShapeDtypeStruct((groups - 1, inner, rank), jnp.bfloat16),
        ),
        in_specs=[
            pl.BlockSpec(memory_space=pl.ANY),
            pl.BlockSpec(memory_space=pltpu.VMEM),
            pl.BlockSpec(memory_space=pltpu.VMEM),
        ],
        out_specs=(pl.BlockSpec(memory_space=pltpu.VMEM), pl.BlockSpec(memory_space=pltpu.VMEM)),
        scratch_shapes=[
            pltpu.VMEM((wants, across, rank), jnp.float32),
            pltpu.SMEM((1, LANES), jnp.int32),
            pltpu.SemaphoreType.DMA,
        ],
        compiler_params=pltpu.CompilerParams(vmem_limit_bytes=16 * MIB),
        name="contract",
    )(requests, fetched, tiles)


def per_device(
    tensor_tiles, tile_iblock, tile_jslot, tile_kslot, block_jlist, block_klist, factor_b, factor_c
):
    groups = lax.axis_size("blk")
    size = lax.axis_size("tiles")
    chips = size // 2
    same_side = [[2 * chip + side for chip in range(chips)] for side in range(2)]
    count = tensor_tiles.shape[1]

    def exchange(array):
        return lax.all_to_all(
            array, "tiles", split_axis=0, concat_axis=0, tiled=True, axis_index_groups=same_side
        )

    requests, *mine = make_requests(
        chips, tile_iblock, tile_jslot, tile_kslot, block_jlist, block_klist, factor_b, factor_c
    )
    paired = [lax.ppermute(factor, "tiles", [(at, at ^ 1) for at in range(size)]) for factor in mine]
    rows = gather_rows(exchange(requests), count, mine, paired)
    fetched = exchange(rows)
    own, send = contract(requests, fetched, tensor_tiles[0], groups)
    total = own.astype(jnp.float32)
    for shift in range(1, groups):
        arrived = lax.ppermute(
            send[shift - 1], "blk", [(i, (i + shift) % groups) for i in range(groups)]
        )
        total = total + arrived.astype(jnp.float32)
    return total


def solution(mesh):
    placed = (
        P("blk", "tiles", None, None),
        P("blk", "tiles"),
        P("blk", "tiles"),
        P("blk", "tiles"),
        P("blk", "tiles"),
        P("blk", "tiles"),
        P(None, "tiles", None),
        P(None, "tiles", None),
    )
    return jax.shard_map(
        per_device, mesh=mesh, in_specs=placed, out_specs=P(("blk", "tiles"), None), check_vma=False
    )
```

```python
import jax
import jax.numpy as jnp
from jax import lax
from jax.experimental import pallas as pl
from jax.experimental.pallas import tpu as pltpu
from jax.sharding import PartitionSpec as P

MIB = 1024 * 1024
LANES = 128


def in_hbm(*arrays):
    return [pltpu.with_memory_space_constraint(array, pltpu.HBM) for array in arrays]


def make_requests(chips, owners, slots_two, slots_three, list_two, list_three, factor_b, factor_c):
    count = owners.shape[1]
    listed = list_two.shape[1]
    small = (owners, slots_two, slots_three, list_two, list_three)
    factors = (factor_b, factor_c)

    def kernel(*refs):
        sources, outs, held, sem = refs[:7], refs[7:10], refs[10:15], refs[15]
        copies = [
            pltpu.make_async_copy(source, target, sem.at[at])
            for at, (source, target) in enumerate(zip(sources, (*held, *outs[1:])))
        ]
        for copy in copies:
            copy.start()
        for copy in copies[:5]:
            copy.wait()
        own, slot_two, slot_three, two, three = held
        words = []
        for slot, table in ((slot_two, two), (slot_three, three)):
            for which in range(count):
                word = table[0, 0]
                for entry in range(1, listed):
                    word = jnp.where(slot[0, which] == entry, table[0, entry], word)
                words.append(word)
        words.extend(own[0, which] for which in range(count))
        lane = lax.broadcasted_iota(jnp.int32, (1, LANES), 1)
        row = jnp.zeros((1, LANES), jnp.int32)
        for at, word in enumerate(words):
            row = jnp.where(lane == at, word, row)
        for chip in range(chips):
            outs[0][chip] = row
        for copy in copies[5:]:
            copy.wait()

    return pl.pallas_call(
        kernel,
        out_shape=[jax.ShapeDtypeStruct((chips, 1, LANES), jnp.int32)]
        + [jax.ShapeDtypeStruct(factor.shape, factor.dtype) for factor in factors],
        in_specs=[pl.BlockSpec(memory_space=pltpu.HBM)] * 7,
        out_specs=[pl.BlockSpec(memory_space=pltpu.VMEM)] * 3,
        scratch_shapes=[pltpu.SMEM(array.shape, jnp.int32) for array in small] + [pltpu.SemaphoreType.DMA((7,))],
        compiler_params=pltpu.CompilerParams(vmem_limit_bytes=8 * MIB),
        name="make_requests",
    )(*in_hbm(*small, *factors))


def gather_rows(asked, count, mine, paired):
    chips = asked.shape[0]
    wants = 2 * count
    rows, rank = mine[0].shape[1:]

    def kernel(asked_ref, mine_b, mine_c, pair_b, pair_c, out_ref, index_ref, sem):
        copy = pltpu.make_async_copy(asked_ref, index_ref, sem)
        copy.start()
        side = lax.rem(lax.axis_index("tiles"), 2)
        copy.wait()
        for chip in range(chips):
            for want in range(wants):
                own, other = (mine_b, pair_b) if want < count else (mine_c, pair_c)
                block = index_ref[chip, 0, want]
                out_ref[chip, want, side] = own[block]
                out_ref[chip, want, 1 - side] = other[block]

    return pl.pallas_call(
        kernel,
        out_shape=jax.ShapeDtypeStruct((chips, wants, 2, rows, rank), mine[0].dtype),
        in_specs=[pl.BlockSpec(memory_space=pl.ANY)] + [pl.BlockSpec(memory_space=pltpu.VMEM)] * 4,
        out_specs=pl.BlockSpec(memory_space=pltpu.VMEM),
        scratch_shapes=[pltpu.SMEM(asked.shape, jnp.int32), pltpu.SemaphoreType.DMA],
        compiler_params=pltpu.CompilerParams(vmem_limit_bytes=8 * MIB),
        name="gather_rows",
    )(asked, *mine, *paired)


def contract(requests, fetched, tiles, groups):
    chips, wants, halves, rows, rank = fetched.shape
    count, inner, width = tiles.shape
    pieces = chips * halves
    across = pieces * rows
    depth = width // across
    step = max(1, 256 // depth)

    def kernel(requests_ref, fetched_ref, tiles_ref, own_ref, send_ref, factor_ref, index_ref, sem):
        copy = pltpu.make_async_copy(requests_ref.at[0], index_ref, sem)
        copy.start()
        me = lax.axis_index("blk")
        for want in range(wants):
            for at in range(pieces):
                piece = fetched_ref[at // halves, want, at % halves]
                factor_ref[want, at * rows : (at + 1) * rows, :] = piece.astype(jnp.float32)
        terms = []
        for which in range(count):
            mode_three = factor_ref[count + which].astype(jnp.bfloat16)
            term = jnp.zeros((inner, rank), jnp.float32)
            for start in range(0, across, step):
                product = jnp.concatenate(
                    [
                        jnp.broadcast_to(factor_ref[which, j : j + 1, :], (depth, rank)).astype(jnp.bfloat16)
                        * mode_three
                        for j in range(start, start + step)
                    ],
                    axis=0,
                )
                term = term + jnp.dot(
                    tiles_ref[which, :, start * depth : (start + step) * depth],
                    product,
                    preferred_element_type=jnp.float32,
                )
            terms.append(term)
        copy.wait()
        for shift in range(groups):
            group = lax.rem(me + shift, groups)
            total = jnp.zeros((inner, rank), jnp.float32)
            for which in range(count):
                total = total + jnp.where(index_ref[0, 2 * count + which] == group, terms[which], 0.0)
            rounded = total.astype(jnp.bfloat16)
            if shift == 0:
                own_ref[...] = rounded
            else:
                send_ref[shift - 1] = rounded

    return pl.pallas_call(
        kernel,
        out_shape=(
            jax.ShapeDtypeStruct((inner, rank), jnp.bfloat16),
            jax.ShapeDtypeStruct((groups - 1, inner, rank), jnp.bfloat16),
        ),
        in_specs=[
            pl.BlockSpec(memory_space=pl.ANY),
            pl.BlockSpec(memory_space=pltpu.VMEM),
            pl.BlockSpec(memory_space=pltpu.VMEM),
        ],
        out_specs=(pl.BlockSpec(memory_space=pltpu.VMEM), pl.BlockSpec(memory_space=pltpu.VMEM)),
        scratch_shapes=[
            pltpu.VMEM((wants, across, rank), jnp.float32),
            pltpu.SMEM((1, LANES), jnp.int32),
            pltpu.SemaphoreType.DMA,
        ],
        compiler_params=pltpu.CompilerParams(vmem_limit_bytes=16 * MIB),
        name="contract",
    )(requests, fetched, tiles)


def per_device(
    tensor_tiles, tile_iblock, tile_jslot, tile_kslot, block_jlist, block_klist, factor_b, factor_c
):
    groups = lax.axis_size("blk")
    size = lax.axis_size("tiles")
    chips = size // 2
    mixed = [[2 * chip + (side + chip.bit_count()) % 2 for chip in range(chips)] for side in range(2)]
    count = tensor_tiles.shape[1]

    def exchange(array):
        return lax.all_to_all(
            array, "tiles", split_axis=0, concat_axis=0, tiled=True, axis_index_groups=mixed
        )

    requests, *mine = make_requests(
        chips, tile_iblock, tile_jslot, tile_kslot, block_jlist, block_klist, factor_b, factor_c
    )
    paired = [lax.ppermute(factor, "tiles", [(at, at ^ 1) for at in range(size)]) for factor in mine]
    rows = gather_rows(exchange(requests), count, mine, paired)
    fetched = exchange(rows)
    own, send = contract(requests, fetched, tensor_tiles[0], groups)
    total = own.astype(jnp.float32)
    for shift in range(1, groups):
        arrived = lax.ppermute(
            send[shift - 1], "blk", [(i, (i + shift) % groups) for i in range(groups)]
        )
        total = total + arrived.astype(jnp.float32)
    return total


def solution(mesh):
    placed = (
        P("blk", "tiles", None, None),
        P("blk", "tiles"),
        P("blk", "tiles"),
        P("blk", "tiles"),
        P("blk", "tiles"),
        P("blk", "tiles"),
        P(None, "tiles", None),
        P(None, "tiles", None),
    )
    return jax.shard_map(
        per_device, mesh=mesh, in_specs=placed, out_specs=P(("blk", "tiles"), None), check_vma=False
    )
```

```python
import jax
import jax.numpy as jnp
from jax import lax
from jax.experimental import pallas as pl
from jax.experimental.pallas import tpu as pltpu
from jax.sharding import PartitionSpec as P

MIB = 1024 * 1024
LANES = 128


def in_hbm(*arrays):
    return [pltpu.with_memory_space_constraint(array, pltpu.HBM) for array in arrays]


def make_requests(chips, owners, slots_two, slots_three, list_two, list_three, factor_b, factor_c):
    count = owners.shape[1]
    listed = list_two.shape[1]
    small = (owners, slots_two, slots_three, list_two, list_three)
    factors = (factor_b, factor_c)

    def kernel(*refs):
        sources, outs, held, sem = refs[:7], refs[7:10], refs[10:15], refs[15]
        copies = [
            pltpu.make_async_copy(source, target, sem.at[at])
            for at, (source, target) in enumerate(zip(sources, (*held, *outs[1:])))
        ]
        for copy in copies:
            copy.start()
        for copy in copies[:5]:
            copy.wait()
        own, slot_two, slot_three, two, three = held
        words = []
        for slot, table in ((slot_two, two), (slot_three, three)):
            for which in range(count):
                word = table[0, 0]
                for entry in range(1, listed):
                    word = jnp.where(slot[0, which] == entry, table[0, entry], word)
                words.append(word)
        words.extend(own[0, which] for which in range(count))
        lane = lax.broadcasted_iota(jnp.int32, (1, LANES), 1)
        row = jnp.zeros((1, LANES), jnp.int32)
        for at, word in enumerate(words):
            row = jnp.where(lane == at, word, row)
        outs[0][...] = jnp.zeros((chips, 1, LANES), jnp.int32)
        outs[0][lax.axis_index("tiles") // 2] = row
        for copy in copies[5:]:
            copy.wait()

    return pl.pallas_call(
        kernel,
        out_shape=[jax.ShapeDtypeStruct((chips, 1, LANES), jnp.int32)]
        + [jax.ShapeDtypeStruct(factor.shape, factor.dtype) for factor in factors],
        in_specs=[pl.BlockSpec(memory_space=pltpu.HBM)] * 7,
        out_specs=[pl.BlockSpec(memory_space=pltpu.VMEM)] * 3,
        scratch_shapes=[pltpu.SMEM(array.shape, jnp.int32) for array in small] + [pltpu.SemaphoreType.DMA((7,))],
        compiler_params=pltpu.CompilerParams(vmem_limit_bytes=8 * MIB),
        name="make_requests",
    )(*in_hbm(*small, *factors))


def gather_rows(asked, count, mine, paired):
    chips = asked.shape[0]
    wants = 2 * count
    rows, rank = mine[0].shape[1:]

    def kernel(asked_ref, mine_b, mine_c, pair_b, pair_c, out_ref, index_ref, sem):
        copy = pltpu.make_async_copy(asked_ref, index_ref, sem)
        copy.start()
        side = lax.rem(lax.axis_index("tiles"), 2)
        copy.wait()
        for chip in range(chips):
            for want in range(wants):
                own, other = (mine_b, pair_b) if want < count else (mine_c, pair_c)
                block = index_ref[chip, 0, want]
                out_ref[chip, want, side] = own[block]
                out_ref[chip, want, 1 - side] = other[block]

    return pl.pallas_call(
        kernel,
        out_shape=jax.ShapeDtypeStruct((chips, wants, 2, rows, rank), mine[0].dtype),
        in_specs=[pl.BlockSpec(memory_space=pl.ANY)] + [pl.BlockSpec(memory_space=pltpu.VMEM)] * 4,
        out_specs=pl.BlockSpec(memory_space=pltpu.VMEM),
        scratch_shapes=[pltpu.SMEM(asked.shape, jnp.int32), pltpu.SemaphoreType.DMA],
        compiler_params=pltpu.CompilerParams(vmem_limit_bytes=8 * MIB),
        name="gather_rows",
    )(asked, *mine, *paired)


def contract(requests, fetched, tiles, groups):
    chips, wants, halves, rows, rank = fetched.shape
    count, inner, width = tiles.shape
    pieces = chips * halves
    across = pieces * rows
    depth = width // across
    step = max(1, 256 // depth)

    def kernel(requests_ref, fetched_ref, tiles_ref, own_ref, send_ref, factor_ref, index_ref, sem):
        copy = pltpu.make_async_copy(requests_ref.at[lax.axis_index("tiles") // 2], index_ref, sem)
        copy.start()
        me = lax.axis_index("blk")
        for want in range(wants):
            for at in range(pieces):
                piece = fetched_ref[at // halves, want, at % halves]
                factor_ref[want, at * rows : (at + 1) * rows, :] = piece.astype(jnp.float32)
        terms = []
        for which in range(count):
            mode_three = factor_ref[count + which].astype(jnp.bfloat16)
            term = jnp.zeros((inner, rank), jnp.float32)
            for start in range(0, across, step):
                product = jnp.concatenate(
                    [
                        jnp.broadcast_to(factor_ref[which, j : j + 1, :], (depth, rank)).astype(jnp.bfloat16)
                        * mode_three
                        for j in range(start, start + step)
                    ],
                    axis=0,
                )
                term = term + jnp.dot(
                    tiles_ref[which, :, start * depth : (start + step) * depth],
                    product,
                    preferred_element_type=jnp.float32,
                )
            terms.append(term)
        copy.wait()
        for shift in range(groups):
            group = lax.rem(me + shift, groups)
            total = jnp.zeros((inner, rank), jnp.float32)
            for which in range(count):
                total = total + jnp.where(index_ref[0, 2 * count + which] == group, terms[which], 0.0)
            rounded = total.astype(jnp.bfloat16)
            if shift == 0:
                own_ref[...] = rounded
            else:
                send_ref[shift - 1] = rounded

    return pl.pallas_call(
        kernel,
        out_shape=(
            jax.ShapeDtypeStruct((inner, rank), jnp.bfloat16),
            jax.ShapeDtypeStruct((groups - 1, inner, rank), jnp.bfloat16),
        ),
        in_specs=[
            pl.BlockSpec(memory_space=pl.ANY),
            pl.BlockSpec(memory_space=pltpu.VMEM),
            pl.BlockSpec(memory_space=pltpu.VMEM),
        ],
        out_specs=(pl.BlockSpec(memory_space=pltpu.VMEM), pl.BlockSpec(memory_space=pltpu.VMEM)),
        scratch_shapes=[
            pltpu.VMEM((wants, across, rank), jnp.float32),
            pltpu.SMEM((1, LANES), jnp.int32),
            pltpu.SemaphoreType.DMA,
        ],
        compiler_params=pltpu.CompilerParams(vmem_limit_bytes=16 * MIB),
        name="contract",
    )(requests, fetched, tiles)


def per_device(
    tensor_tiles, tile_iblock, tile_jslot, tile_kslot, block_jlist, block_klist, factor_b, factor_c
):
    groups = lax.axis_size("blk")
    size = lax.axis_size("tiles")
    chips = size // 2
    same_side = [[2 * chip + side for chip in range(chips)] for side in range(2)]
    count = tensor_tiles.shape[1]

    requests, *mine = make_requests(
        chips, tile_iblock, tile_jslot, tile_kslot, block_jlist, block_klist, factor_b, factor_c
    )
    paired = [lax.ppermute(factor, "tiles", [(at, at ^ 1) for at in range(size)]) for factor in mine]
    asked = lax.psum(requests, "tiles", axis_index_groups=same_side)
    rows = gather_rows(asked, count, mine, paired)
    fetched = lax.all_to_all(
        rows, "tiles", split_axis=0, concat_axis=0, tiled=True, axis_index_groups=same_side
    )
    own, send = contract(requests, fetched, tensor_tiles[0], groups)
    total = own.astype(jnp.float32)
    for shift in range(1, groups):
        arrived = lax.ppermute(
            send[shift - 1], "blk", [(i, (i + shift) % groups) for i in range(groups)]
        )
        total = total + arrived.astype(jnp.float32)
    return total


def solution(mesh):
    placed = (
        P("blk", "tiles", None, None),
        P("blk", "tiles"),
        P("blk", "tiles"),
        P("blk", "tiles"),
        P("blk", "tiles"),
        P("blk", "tiles"),
        P(None, "tiles", None),
        P(None, "tiles", None),
    )
    return jax.shard_map(
        per_device, mesh=mesh, in_specs=placed, out_specs=P(("blk", "tiles"), None), check_vma=False
    )
```

```python
import jax
import jax.numpy as jnp
from jax import lax
from jax.experimental import pallas as pl
from jax.experimental.pallas import tpu as pltpu
from jax.sharding import PartitionSpec as P

MIB = 1024 * 1024
LANES = 128


def in_hbm(*arrays):
    return [pltpu.with_memory_space_constraint(array, pltpu.HBM) for array in arrays]


def make_requests(chips, owners, slots_two, slots_three, list_two, list_three):
    count = owners.shape[1]
    listed = list_two.shape[1]
    small = (owners, slots_two, slots_three, list_two, list_three)

    def kernel(*refs):
        sources, out_ref, held, sem = refs[:5], refs[5], refs[6:11], refs[11]
        copies = [
            pltpu.make_async_copy(source, target, sem.at[at]) for at, (source, target) in enumerate(zip(sources, held))
        ]
        for copy in copies:
            copy.start()
        for copy in copies:
            copy.wait()
        own, slot_two, slot_three, two, three = held
        words = []
        for slot, table in ((slot_two, two), (slot_three, three)):
            for which in range(count):
                word = table[0, 0]
                for entry in range(1, listed):
                    word = jnp.where(slot[0, which] == entry, table[0, entry], word)
                words.append(word)
        words.extend(own[0, which] for which in range(count))
        lane = lax.broadcasted_iota(jnp.int32, (1, LANES), 1)
        row = jnp.zeros((1, LANES), jnp.int32)
        for at, word in enumerate(words):
            row = jnp.where(lane == at, word, row)
        for chip in range(chips):
            out_ref[chip] = row

    return pl.pallas_call(
        kernel,
        out_shape=jax.ShapeDtypeStruct((chips, 1, LANES), jnp.int32),
        in_specs=[pl.BlockSpec(memory_space=pltpu.HBM)] * 5,
        out_specs=pl.BlockSpec(memory_space=pltpu.VMEM),
        scratch_shapes=[pltpu.SMEM(array.shape, jnp.int32) for array in small] + [pltpu.SemaphoreType.DMA((5,))],
        compiler_params=pltpu.CompilerParams(vmem_limit_bytes=8 * MIB),
        name="make_requests",
    )(*in_hbm(*small))


def stage_factors(requests, *factors):
    def kernel(requests_ref, *refs):
        sources, outs, sem = refs[:2], refs[2:4], refs[4]
        copies = [
            pltpu.make_async_copy(source, target, sem.at[at]) for at, (source, target) in enumerate(zip(sources, outs))
        ]
        for copy in copies:
            copy.start()
        for copy in copies:
            copy.wait()

    moved = 2 * sum(factor.size * factor.dtype.itemsize for factor in factors)
    return pl.pallas_call(
        kernel,
        out_shape=[jax.ShapeDtypeStruct(factor.shape, factor.dtype) for factor in factors],
        in_specs=[pl.BlockSpec(memory_space=pl.ANY)] + [pl.BlockSpec(memory_space=pltpu.HBM)] * 2,
        out_specs=[pl.BlockSpec(memory_space=pltpu.VMEM)] * 2,
        scratch_shapes=[pltpu.SemaphoreType.DMA((2,))],
        compiler_params=pltpu.CompilerParams(vmem_limit_bytes=8 * MIB),
        cost_estimate=pl.CostEstimate(flops=0, bytes_accessed=moved, transcendentals=0),
        name="stage_factors",
    )(requests, *in_hbm(*factors))


def gather_rows(asked, count, mine, paired):
    chips = asked.shape[0]
    wants = 2 * count
    rows, rank = mine[0].shape[1:]

    def kernel(asked_ref, mine_b, mine_c, pair_b, pair_c, out_ref, index_ref, sem):
        copy = pltpu.make_async_copy(asked_ref, index_ref, sem)
        copy.start()
        side = lax.rem(lax.axis_index("tiles"), 2)
        copy.wait()
        for chip in range(chips):
            for want in range(wants):
                own, other = (mine_b, pair_b) if want < count else (mine_c, pair_c)
                block = index_ref[chip, 0, want]
                out_ref[chip, want, side] = own[block]
                out_ref[chip, want, 1 - side] = other[block]

    return pl.pallas_call(
        kernel,
        out_shape=jax.ShapeDtypeStruct((chips, wants, 2, rows, rank), mine[0].dtype),
        in_specs=[pl.BlockSpec(memory_space=pl.ANY)] + [pl.BlockSpec(memory_space=pltpu.VMEM)] * 4,
        out_specs=pl.BlockSpec(memory_space=pltpu.VMEM),
        scratch_shapes=[pltpu.SMEM(asked.shape, jnp.int32), pltpu.SemaphoreType.DMA],
        compiler_params=pltpu.CompilerParams(vmem_limit_bytes=8 * MIB),
        name="gather_rows",
    )(asked, *mine, *paired)


def contract(requests, fetched, tiles, groups):
    chips, wants, halves, rows, rank = fetched.shape
    count, inner, width = tiles.shape
    pieces = chips * halves
    across = pieces * rows
    depth = width // across
    step = max(1, 256 // depth)

    def kernel(requests_ref, fetched_ref, tiles_ref, own_ref, send_ref, factor_ref, index_ref, sem):
        copy = pltpu.make_async_copy(requests_ref.at[0], index_ref, sem)
        copy.start()
        me = lax.axis_index("blk")
        for want in range(wants):
            for at in range(pieces):
                piece = fetched_ref[at // halves, want, at % halves]
                factor_ref[want, at * rows : (at + 1) * rows, :] = piece.astype(jnp.float32)
        terms = []
        for which in range(count):
            mode_three = factor_ref[count + which].astype(jnp.bfloat16)
            term = jnp.zeros((inner, rank), jnp.float32)
            for start in range(0, across, step):
                product = jnp.concatenate(
                    [
                        jnp.broadcast_to(factor_ref[which, j : j + 1, :], (depth, rank)).astype(jnp.bfloat16)
                        * mode_three
                        for j in range(start, start + step)
                    ],
                    axis=0,
                )
                term = term + jnp.dot(
                    tiles_ref[which, :, start * depth : (start + step) * depth],
                    product,
                    preferred_element_type=jnp.float32,
                )
            terms.append(term)
        copy.wait()
        for shift in range(groups):
            group = lax.rem(me + shift, groups)
            total = jnp.zeros((inner, rank), jnp.float32)
            for which in range(count):
                total = total + jnp.where(index_ref[0, 2 * count + which] == group, terms[which], 0.0)
            rounded = total.astype(jnp.bfloat16)
            if shift == 0:
                own_ref[...] = rounded
            else:
                send_ref[shift - 1] = rounded

    return pl.pallas_call(
        kernel,
        out_shape=(
            jax.ShapeDtypeStruct((inner, rank), jnp.bfloat16),
            jax.ShapeDtypeStruct((groups - 1, inner, rank), jnp.bfloat16),
        ),
        in_specs=[
            pl.BlockSpec(memory_space=pl.ANY),
            pl.BlockSpec(memory_space=pltpu.VMEM),
            pl.BlockSpec(memory_space=pltpu.VMEM),
        ],
        out_specs=(pl.BlockSpec(memory_space=pltpu.VMEM), pl.BlockSpec(memory_space=pltpu.VMEM)),
        scratch_shapes=[
            pltpu.VMEM((wants, across, rank), jnp.float32),
            pltpu.SMEM((1, LANES), jnp.int32),
            pltpu.SemaphoreType.DMA,
        ],
        compiler_params=pltpu.CompilerParams(vmem_limit_bytes=16 * MIB),
        name="contract",
    )(requests, fetched, tiles)


def per_device(
    tensor_tiles, tile_iblock, tile_jslot, tile_kslot, block_jlist, block_klist, factor_b, factor_c
):
    groups = lax.axis_size("blk")
    size = lax.axis_size("tiles")
    chips = size // 2
    same_side = [[2 * chip + side for chip in range(chips)] for side in range(2)]
    count = tensor_tiles.shape[1]

    def exchange(array):
        return lax.all_to_all(
            array, "tiles", split_axis=0, concat_axis=0, tiled=True, axis_index_groups=same_side
        )

    paired = [
        lax.ppermute(factor, "tiles", [(at, at ^ 1) for at in range(size)]) for factor in (factor_b, factor_c)
    ]
    requests = make_requests(chips, tile_iblock, tile_jslot, tile_kslot, block_jlist, block_klist)
    asked = exchange(requests)
    mine = stage_factors(requests, factor_b, factor_c)
    rows = gather_rows(asked, count, mine, paired)
    fetched = exchange(rows)
    own, send = contract(requests, fetched, tensor_tiles[0], groups)
    total = own.astype(jnp.float32)
    for shift in range(1, groups):
        arrived = lax.ppermute(
            send[shift - 1], "blk", [(i, (i + shift) % groups) for i in range(groups)]
        )
        total = total + arrived.astype(jnp.float32)
    return total


def solution(mesh):
    placed = (
        P("blk", "tiles", None, None),
        P("blk", "tiles"),
        P("blk", "tiles"),
        P("blk", "tiles"),
        P("blk", "tiles"),
        P("blk", "tiles"),
        P(None, "tiles", None),
        P(None, "tiles", None),
    )
    return jax.shard_map(
        per_device, mesh=mesh, in_specs=placed, out_specs=P(("blk", "tiles"), None), check_vma=False
    )
```

```python
import jax
import jax.numpy as jnp
from jax import lax
from jax.experimental import pallas as pl
from jax.experimental.pallas import tpu as pltpu
from jax.sharding import PartitionSpec as P

MIB = 1024 * 1024
LANES = 128


def in_hbm(*arrays):
    return [pltpu.with_memory_space_constraint(array, pltpu.HBM) for array in arrays]


def make_requests(chips, owners, slots_two, slots_three, list_two, list_three, factor_b, factor_c):
    count = owners.shape[1]
    listed = list_two.shape[1]
    small = (owners, slots_two, slots_three, list_two, list_three)
    factors = (factor_b, factor_c)

    def kernel(*refs):
        sources, outs, held, sem = refs[:7], refs[7:10], refs[10:15], refs[15]
        copies = [
            pltpu.make_async_copy(source, target, sem.at[at])
            for at, (source, target) in enumerate(zip(sources, (*held, *outs[1:])))
        ]
        for copy in copies:
            copy.start()
        for copy in copies[:5]:
            copy.wait()
        own, slot_two, slot_three, two, three = held
        words = []
        for slot, table in ((slot_two, two), (slot_three, three)):
            for which in range(count):
                word = table[0, 0]
                for entry in range(1, listed):
                    word = jnp.where(slot[0, which] == entry, table[0, entry], word)
                words.append(word)
        words.extend(own[0, which] for which in range(count))
        lane = lax.broadcasted_iota(jnp.int32, (1, LANES), 1)
        row = jnp.zeros((1, LANES), jnp.int32)
        for at, word in enumerate(words):
            row = jnp.where(lane == at, word, row)
        for chip in range(chips):
            outs[0][chip] = row
        for copy in copies[5:]:
            copy.wait()

    return pl.pallas_call(
        kernel,
        out_shape=[jax.ShapeDtypeStruct((chips, 1, LANES), jnp.int32)]
        + [jax.ShapeDtypeStruct(factor.shape, factor.dtype) for factor in factors],
        in_specs=[pl.BlockSpec(memory_space=pltpu.HBM)] * 7,
        out_specs=[pl.BlockSpec(memory_space=pltpu.VMEM)] * 3,
        scratch_shapes=[pltpu.SMEM(array.shape, jnp.int32) for array in small] + [pltpu.SemaphoreType.DMA((7,))],
        compiler_params=pltpu.CompilerParams(vmem_limit_bytes=8 * MIB),
        name="make_requests",
    )(*in_hbm(*small, *factors))


def gather_rows(asked, count, mine, paired):
    chips = asked.shape[0]
    wants = 2 * count
    rows, rank = mine[0].shape[1:]

    def kernel(asked_ref, mine_b, mine_c, pair_b, pair_c, out_ref, index_ref, sem):
        copy = pltpu.make_async_copy(asked_ref, index_ref, sem)
        copy.start()
        side = lax.rem(lax.axis_index("tiles"), 2)
        copy.wait()
        for chip in range(chips):
            for want in range(wants):
                own, other = (mine_b, pair_b) if want < count else (mine_c, pair_c)
                block = index_ref[chip, 0, want]
                out_ref[chip, want, side] = own[block]
                out_ref[chip, want, 1 - side] = other[block]

    return pl.pallas_call(
        kernel,
        out_shape=jax.ShapeDtypeStruct((chips, wants, 2, rows, rank), mine[0].dtype),
        in_specs=[pl.BlockSpec(memory_space=pl.ANY)] + [pl.BlockSpec(memory_space=pltpu.VMEM)] * 4,
        out_specs=pl.BlockSpec(memory_space=pltpu.VMEM),
        scratch_shapes=[pltpu.SMEM(asked.shape, jnp.int32), pltpu.SemaphoreType.DMA],
        compiler_params=pltpu.CompilerParams(vmem_limit_bytes=8 * MIB),
        name="gather_rows",
    )(asked, *mine, *paired)


def contract(requests, fetched, order, tiles, groups):
    chips, wants, halves, rows, rank = fetched.shape
    count, inner, width = tiles.shape
    across = chips * halves * rows
    depth = width // across
    step = max(1, 256 // depth)

    def kernel(requests_ref, fetched_ref, tiles_ref, own_ref, send_ref, factor_ref, index_ref, sem):
        copy = pltpu.make_async_copy(requests_ref.at[0], index_ref, sem)
        copy.start()
        me = lax.axis_index("blk")
        for want in range(wants):
            for came, chip in enumerate(order):
                for half in range(halves):
                    at = (chip * halves + half) * rows
                    factor_ref[want, at : at + rows, :] = fetched_ref[came, want, half].astype(jnp.float32)
        terms = []
        for which in range(count):
            mode_three = factor_ref[count + which].astype(jnp.bfloat16)
            term = jnp.zeros((inner, rank), jnp.float32)
            for start in range(0, across, step):
                product = jnp.concatenate(
                    [
                        jnp.broadcast_to(factor_ref[which, j : j + 1, :], (depth, rank)).astype(jnp.bfloat16)
                        * mode_three
                        for j in range(start, start + step)
                    ],
                    axis=0,
                )
                term = term + jnp.dot(
                    tiles_ref[which, :, start * depth : (start + step) * depth],
                    product,
                    preferred_element_type=jnp.float32,
                )
            terms.append(term)
        copy.wait()
        for shift in range(groups):
            group = lax.rem(me + shift, groups)
            total = jnp.zeros((inner, rank), jnp.float32)
            for which in range(count):
                total = total + jnp.where(index_ref[0, 2 * count + which] == group, terms[which], 0.0)
            rounded = total.astype(jnp.bfloat16)
            if shift == 0:
                own_ref[...] = rounded
            else:
                send_ref[shift - 1] = rounded

    return pl.pallas_call(
        kernel,
        out_shape=(
            jax.ShapeDtypeStruct((inner, rank), jnp.bfloat16),
            jax.ShapeDtypeStruct((groups - 1, inner, rank), jnp.bfloat16),
        ),
        in_specs=[
            pl.BlockSpec(memory_space=pl.ANY),
            pl.BlockSpec(memory_space=pltpu.VMEM),
            pl.BlockSpec(memory_space=pltpu.VMEM),
        ],
        out_specs=(pl.BlockSpec(memory_space=pltpu.VMEM), pl.BlockSpec(memory_space=pltpu.VMEM)),
        scratch_shapes=[
            pltpu.VMEM((wants, across, rank), jnp.float32),
            pltpu.SMEM((1, LANES), jnp.int32),
            pltpu.SemaphoreType.DMA,
        ],
        compiler_params=pltpu.CompilerParams(vmem_limit_bytes=16 * MIB),
        name="contract",
    )(requests, fetched, tiles)


def per_device(
    tensor_tiles, tile_iblock, tile_jslot, tile_kslot, block_jlist, block_klist, factor_b, factor_c
):
    groups = lax.axis_size("blk")
    size = lax.axis_size("tiles")
    chips = size // 2
    order = [(chip + chips // 2) % chips for chip in range(chips)]
    same_side = [[2 * chip + side for chip in order] for side in range(2)]
    count = tensor_tiles.shape[1]

    def exchange(array):
        return lax.all_to_all(
            array, "tiles", split_axis=0, concat_axis=0, tiled=True, axis_index_groups=same_side
        )

    requests, *mine = make_requests(
        chips, tile_iblock, tile_jslot, tile_kslot, block_jlist, block_klist, factor_b, factor_c
    )
    paired = [lax.ppermute(factor, "tiles", [(at, at ^ 1) for at in range(size)]) for factor in mine]
    rows = gather_rows(exchange(requests), count, mine, paired)
    fetched = exchange(rows)
    own, send = contract(requests, fetched, order, tensor_tiles[0], groups)
    total = own.astype(jnp.float32)
    for shift in range(1, groups):
        arrived = lax.ppermute(
            send[shift - 1], "blk", [(i, (i + shift) % groups) for i in range(groups)]
        )
        total = total + arrived.astype(jnp.float32)
    return total


def solution(mesh):
    placed = (
        P("blk", "tiles", None, None),
        P("blk", "tiles"),
        P("blk", "tiles"),
        P("blk", "tiles"),
        P("blk", "tiles"),
        P("blk", "tiles"),
        P(None, "tiles", None),
        P(None, "tiles", None),
    )
    return jax.shard_map(
        per_device, mesh=mesh, in_specs=placed, out_specs=P(("blk", "tiles"), None), check_vma=False
    )
```

```python
import jax
import jax.numpy as jnp
from jax import lax
from jax.experimental import pallas as pl
from jax.experimental.pallas import tpu as pltpu
from jax.sharding import PartitionSpec as P

MIB = 1024 * 1024


def in_hbm(*arrays):
    return [pltpu.with_memory_space_constraint(array, pltpu.HBM) for array in arrays]


def make_requests(chips, *small):
    width = small[0].shape[1]

    def kernel(*refs):
        sources, out_ref, held, sem = refs[:4], refs[4], refs[5:9], refs[9]
        copies = [
            pltpu.make_async_copy(source, target, sem.at[at]) for at, (source, target) in enumerate(zip(sources, held))
        ]
        for copy in copies:
            copy.start()
        for at, copy in enumerate(copies):
            copy.wait()
            row = held[at][...]
            for chip in range(chips):
                out_ref[chip, at : at + 1, :] = row

    return pl.pallas_call(
        kernel,
        out_shape=jax.ShapeDtypeStruct((chips, 4, width), jnp.int32),
        in_specs=[pl.BlockSpec(memory_space=pltpu.HBM)] * 4,
        out_specs=pl.BlockSpec(memory_space=pltpu.VMEM),
        scratch_shapes=[pltpu.VMEM((1, width), jnp.int32)] * 4 + [pltpu.SemaphoreType.DMA((4,))],
        compiler_params=pltpu.CompilerParams(vmem_limit_bytes=8 * MIB),
        name="make_requests",
    )(*in_hbm(*small))


def stage_factors(requests, *factors):
    def kernel(requests_ref, *refs):
        sources, outs, sem = refs[:2], refs[2:4], refs[4]
        copies = [
            pltpu.make_async_copy(source, target, sem.at[at]) for at, (source, target) in enumerate(zip(sources, outs))
        ]
        for copy in copies:
            copy.start()
        for copy in copies:
            copy.wait()

    moved = 2 * sum(factor.size * factor.dtype.itemsize for factor in factors)
    return pl.pallas_call(
        kernel,
        out_shape=[jax.ShapeDtypeStruct(factor.shape, factor.dtype) for factor in factors],
        in_specs=[pl.BlockSpec(memory_space=pl.ANY)] + [pl.BlockSpec(memory_space=pltpu.HBM)] * 2,
        out_specs=[pl.BlockSpec(memory_space=pltpu.VMEM)] * 2,
        scratch_shapes=[pltpu.SemaphoreType.DMA((2,))],
        compiler_params=pltpu.CompilerParams(vmem_limit_bytes=8 * MIB),
        cost_estimate=pl.CostEstimate(flops=0, bytes_accessed=moved, transcendentals=0),
        name="stage_factors",
    )(requests, *in_hbm(*factors))


def gather_rows(asked, mine, paired):
    chips, _, width = asked.shape
    rows, rank = mine[0].shape[1:]

    def kernel(asked_ref, mine_b, mine_c, pair_b, pair_c, out_ref, index_ref, sem):
        copy = pltpu.make_async_copy(asked_ref, index_ref, sem)
        copy.start()
        side = lax.rem(lax.axis_index("tiles"), 2)
        copy.wait()
        for chip in range(chips):
            for mode, (own, other) in enumerate(((mine_b, pair_b), (mine_c, pair_c))):
                for which in range(width):
                    slot = index_ref[chip, 2 * mode, which]
                    block = index_ref[chip, 2 * mode + 1, 0]
                    for entry in range(1, width):
                        block = jnp.where(slot == entry, index_ref[chip, 2 * mode + 1, entry], block)
                    out_ref[chip, mode * width + which, side] = own[block]
                    out_ref[chip, mode * width + which, 1 - side] = other[block]

    return pl.pallas_call(
        kernel,
        out_shape=jax.ShapeDtypeStruct((chips, 2 * width, 2, rows, rank), mine[0].dtype),
        in_specs=[pl.BlockSpec(memory_space=pl.ANY)] + [pl.BlockSpec(memory_space=pltpu.VMEM)] * 4,
        out_specs=pl.BlockSpec(memory_space=pltpu.VMEM),
        scratch_shapes=[pltpu.SMEM(asked.shape, jnp.int32), pltpu.SemaphoreType.DMA],
        compiler_params=pltpu.CompilerParams(vmem_limit_bytes=8 * MIB),
        name="gather_rows",
    )(asked, *mine, *paired)


def contract(owners, fetched, order, tiles, groups):
    chips, wants, halves, rows, rank = fetched.shape
    count, inner, width = tiles.shape
    across = chips * halves * rows
    depth = width // across
    step = max(1, 256 // depth)

    def kernel(owners_ref, fetched_ref, tiles_ref, own_ref, send_ref, factor_ref, index_ref, sem):
        copy = pltpu.make_async_copy(owners_ref, index_ref, sem)
        copy.start()
        me = lax.axis_index("blk")
        for want in range(wants):
            for came, chip in enumerate(order):
                for half in range(halves):
                    at = (chip * halves + half) * rows
                    factor_ref[want, at : at + rows, :] = fetched_ref[came, want, half].astype(jnp.float32)
        terms = []
        for which in range(count):
            mode_three = factor_ref[count + which].astype(jnp.bfloat16)
            term = jnp.zeros((inner, rank), jnp.float32)
            for start in range(0, across, step):
                product = jnp.concatenate(
                    [
                        jnp.broadcast_to(factor_ref[which, j : j + 1, :], (depth, rank)).astype(jnp.bfloat16)
                        * mode_three
                        for j in range(start, start + step)
                    ],
                    axis=0,
                )
                term = term + jnp.dot(
                    tiles_ref[which, :, start * depth : (start + step) * depth],
                    product,
                    preferred_element_type=jnp.float32,
                )
            terms.append(term)
        copy.wait()
        for shift in range(groups):
            group = lax.rem(me + shift, groups)
            total = jnp.zeros((inner, rank), jnp.float32)
            for which in range(count):
                total = total + jnp.where(index_ref[0, which] == group, terms[which], 0.0)
            rounded = total.astype(jnp.bfloat16)
            if shift == 0:
                own_ref[...] = rounded
            else:
                send_ref[shift - 1] = rounded

    return pl.pallas_call(
        kernel,
        out_shape=(
            jax.ShapeDtypeStruct((inner, rank), jnp.bfloat16),
            jax.ShapeDtypeStruct((groups - 1, inner, rank), jnp.bfloat16),
        ),
        in_specs=[
            pl.BlockSpec(memory_space=pltpu.HBM),
            pl.BlockSpec(memory_space=pltpu.VMEM),
            pl.BlockSpec(memory_space=pltpu.VMEM),
        ],
        out_specs=(pl.BlockSpec(memory_space=pltpu.VMEM), pl.BlockSpec(memory_space=pltpu.VMEM)),
        scratch_shapes=[
            pltpu.VMEM((wants, across, rank), jnp.float32),
            pltpu.SMEM(owners.shape, jnp.int32),
            pltpu.SemaphoreType.DMA,
        ],
        compiler_params=pltpu.CompilerParams(vmem_limit_bytes=16 * MIB),
        name="contract",
    )(*in_hbm(owners), fetched, tiles)


def per_device(
    tensor_tiles, tile_iblock, tile_jslot, tile_kslot, block_jlist, block_klist, factor_b, factor_c
):
    groups = lax.axis_size("blk")
    size = lax.axis_size("tiles")
    chips = size // 2
    order = [(chip + chips // 2) % chips for chip in range(chips)]
    sides = [[2 * chip + (side + (chip == order[0])) % 2 for chip in order] for side in range(2)]

    def exchange(array):
        return lax.all_to_all(array, "tiles", split_axis=0, concat_axis=0, tiled=True, axis_index_groups=sides)

    paired = [
        lax.ppermute(factor, "tiles", [(at, at ^ 1) for at in range(size)]) for factor in (factor_b, factor_c)
    ]
    requests = make_requests(chips, tile_jslot, block_jlist, tile_kslot, block_klist)
    asked = exchange(requests)
    mine = stage_factors(requests, factor_b, factor_c)
    fetched = exchange(gather_rows(asked, mine, paired))
    own, send = contract(tile_iblock, fetched, order, tensor_tiles[0], groups)
    total = own.astype(jnp.float32)
    for shift in range(1, groups):
        arrived = lax.ppermute(
            send[shift - 1], "blk", [(i, (i + shift) % groups) for i in range(groups)]
        )
        total = total + arrived.astype(jnp.float32)
    return total


def solution(mesh):
    placed = (
        P("blk", "tiles", None, None),
        P("blk", "tiles"),
        P("blk", "tiles"),
        P("blk", "tiles"),
        P("blk", "tiles"),
        P("blk", "tiles"),
        P(None, "tiles", None),
        P(None, "tiles", None),
    )
    return jax.shard_map(
        per_device, mesh=mesh, in_specs=placed, out_specs=P(("blk", "tiles"), None), check_vma=False
    )
```

```python
import jax
import jax.numpy as jnp
from jax import lax
from jax.experimental import pallas as pl
from jax.experimental.pallas import tpu as pltpu
from jax.sharding import PartitionSpec as P

MIB = 1024 * 1024
LANES = 128


def in_hbm(*arrays):
    return [pltpu.with_memory_space_constraint(array, pltpu.HBM) for array in arrays]


def make_requests(chips, *small):
    count, listed = small[0].shape[1], small[1].shape[1]

    def kernel(*refs):
        sources, out_ref, held, sem = refs[:4], refs[4], refs[5:9], refs[9]
        copies = [
            pltpu.make_async_copy(source, target, sem.at[at]) for at, (source, target) in enumerate(zip(sources, held))
        ]
        for copy in copies:
            copy.start()
        out_ref[...] = jnp.zeros(out_ref.shape, jnp.int32)
        for copy in copies:
            copy.wait()
        for mode in range(2):
            slots, table = held[2 * mode][...], held[2 * mode + 1][...]
            blocks = jnp.broadcast_to(table[:, 0:1], slots.shape)
            for entry in range(1, listed):
                blocks = jnp.where(slots == entry, jnp.broadcast_to(table[:, entry : entry + 1], slots.shape), blocks)
            for chip in range(chips):
                out_ref[chip, mode : mode + 1, 0:count] = blocks

    return pl.pallas_call(
        kernel,
        out_shape=jax.ShapeDtypeStruct((chips, 2, LANES), jnp.int32),
        in_specs=[pl.BlockSpec(memory_space=pltpu.HBM)] * 4,
        out_specs=pl.BlockSpec(memory_space=pltpu.VMEM),
        scratch_shapes=[pltpu.VMEM(array.shape, jnp.int32) for array in small] + [pltpu.SemaphoreType.DMA((4,))],
        compiler_params=pltpu.CompilerParams(vmem_limit_bytes=8 * MIB),
        name="make_requests",
    )(*in_hbm(*small))


def stage_factors(requests, *factors):
    def kernel(requests_ref, *refs):
        sources, outs, sem = refs[:2], refs[2:4], refs[4]
        copies = [
            pltpu.make_async_copy(source, target, sem.at[at]) for at, (source, target) in enumerate(zip(sources, outs))
        ]
        for copy in copies:
            copy.start()
        for copy in copies:
            copy.wait()

    moved = 2 * sum(factor.size * factor.dtype.itemsize for factor in factors)
    return pl.pallas_call(
        kernel,
        out_shape=[jax.ShapeDtypeStruct(factor.shape, factor.dtype) for factor in factors],
        in_specs=[pl.BlockSpec(memory_space=pl.ANY)] + [pl.BlockSpec(memory_space=pltpu.HBM)] * 2,
        out_specs=[pl.BlockSpec(memory_space=pltpu.VMEM)] * 2,
        scratch_shapes=[pltpu.SemaphoreType.DMA((2,))],
        compiler_params=pltpu.CompilerParams(vmem_limit_bytes=8 * MIB),
        cost_estimate=pl.CostEstimate(flops=0, bytes_accessed=moved, transcendentals=0),
        name="stage_factors",
    )(requests, *in_hbm(*factors))


def gather_rows(asked, count, mine, paired):
    chips = asked.shape[0]
    rows, rank = mine[0].shape[1:]

    def kernel(asked_ref, mine_b, mine_c, pair_b, pair_c, out_ref, index_ref, sem):
        copy = pltpu.make_async_copy(asked_ref, index_ref, sem)
        copy.start()
        side = lax.rem(lax.axis_index("tiles"), 2)
        copy.wait()
        for chip in range(chips):
            for mode, (own, other) in enumerate(((mine_b, pair_b), (mine_c, pair_c))):
                for which in range(count):
                    block = index_ref[chip, mode, which]
                    out_ref[chip, mode * count + which, side] = own[block]
                    out_ref[chip, mode * count + which, 1 - side] = other[block]

    return pl.pallas_call(
        kernel,
        out_shape=jax.ShapeDtypeStruct((chips, 2 * count, 2, rows, rank), mine[0].dtype),
        in_specs=[pl.BlockSpec(memory_space=pl.ANY)] + [pl.BlockSpec(memory_space=pltpu.VMEM)] * 4,
        out_specs=pl.BlockSpec(memory_space=pltpu.VMEM),
        scratch_shapes=[pltpu.SMEM(asked.shape, jnp.int32), pltpu.SemaphoreType.DMA],
        compiler_params=pltpu.CompilerParams(vmem_limit_bytes=8 * MIB),
        name="gather_rows",
    )(asked, *mine, *paired)


def contract(owners, fetched, order, tiles, groups):
    chips, wants, halves, rows, rank = fetched.shape
    count, inner, width = tiles.shape
    across = chips * halves * rows
    depth = width // across
    step = max(1, 256 // depth)

    def kernel(owners_ref, fetched_ref, tiles_ref, own_ref, send_ref, factor_ref, index_ref, sem):
        copy = pltpu.make_async_copy(owners_ref, index_ref, sem)
        copy.start()
        me = lax.axis_index("blk")
        for want in range(wants):
            for came, chip in enumerate(order):
                for half in range(halves):
                    at = (chip * halves + half) * rows
                    factor_ref[want, at : at + rows, :] = fetched_ref[came, want, half].astype(jnp.float32)
        terms = []
        for which in range(count):
            mode_three = factor_ref[count + which].astype(jnp.bfloat16)
            term = jnp.zeros((inner, rank), jnp.float32)
            for start in range(0, across, step):
                product = jnp.concatenate(
                    [
                        jnp.broadcast_to(factor_ref[which, j : j + 1, :], (depth, rank)).astype(jnp.bfloat16)
                        * mode_three
                        for j in range(start, start + step)
                    ],
                    axis=0,
                )
                term = term + jnp.dot(
                    tiles_ref[which, :, start * depth : (start + step) * depth],
                    product,
                    preferred_element_type=jnp.float32,
                )
            terms.append(term)
        copy.wait()
        for shift in range(groups):
            group = lax.rem(me + shift, groups)
            total = jnp.zeros((inner, rank), jnp.float32)
            for which in range(count):
                total = total + jnp.where(index_ref[0, which] == group, terms[which], 0.0)
            rounded = total.astype(jnp.bfloat16)
            if shift == 0:
                own_ref[...] = rounded
            else:
                send_ref[shift - 1] = rounded

    return pl.pallas_call(
        kernel,
        out_shape=(
            jax.ShapeDtypeStruct((inner, rank), jnp.bfloat16),
            jax.ShapeDtypeStruct((groups - 1, inner, rank), jnp.bfloat16),
        ),
        in_specs=[
            pl.BlockSpec(memory_space=pltpu.HBM),
            pl.BlockSpec(memory_space=pltpu.VMEM),
            pl.BlockSpec(memory_space=pltpu.VMEM),
        ],
        out_specs=(pl.BlockSpec(memory_space=pltpu.VMEM), pl.BlockSpec(memory_space=pltpu.VMEM)),
        scratch_shapes=[
            pltpu.VMEM((wants, across, rank), jnp.float32),
            pltpu.SMEM(owners.shape, jnp.int32),
            pltpu.SemaphoreType.DMA,
        ],
        compiler_params=pltpu.CompilerParams(vmem_limit_bytes=16 * MIB),
        name="contract",
    )(*in_hbm(owners), fetched, tiles)


def per_device(
    tensor_tiles, tile_iblock, tile_jslot, tile_kslot, block_jlist, block_klist, factor_b, factor_c
):
    groups = lax.axis_size("blk")
    size = lax.axis_size("tiles")
    chips = size // 2
    order = [(chip + chips // 2) % chips for chip in range(chips)]
    sides = [[2 * chip + side for chip in order] for side in range(2)]

    def exchange(array):
        return lax.all_to_all(array, "tiles", split_axis=0, concat_axis=0, tiled=True, axis_index_groups=sides)

    paired = [
        lax.ppermute(factor, "tiles", [(at, at ^ 1) for at in range(size)]) for factor in (factor_b, factor_c)
    ]
    requests = make_requests(chips, tile_jslot, block_jlist, tile_kslot, block_klist)
    asked = exchange(requests)
    mine = stage_factors(requests, factor_b, factor_c)
    fetched = exchange(gather_rows(asked, tile_jslot.shape[1], mine, paired))
    own, send = contract(tile_iblock, fetched, order, tensor_tiles[0], groups)
    total = own.astype(jnp.float32)
    for shift in range(1, groups):
        arrived = lax.ppermute(
            send[shift - 1], "blk", [(i, (i + shift) % groups) for i in range(groups)]
        )
        total = total + arrived.astype(jnp.float32)
    return total


def solution(mesh):
    placed = (
        P("blk", "tiles", None, None),
        P("blk", "tiles"),
        P("blk", "tiles"),
        P("blk", "tiles"),
        P("blk", "tiles"),
        P("blk", "tiles"),
        P(None, "tiles", None),
        P(None, "tiles", None),
    )
    return jax.shard_map(
        per_device, mesh=mesh, in_specs=placed, out_specs=P(("blk", "tiles"), None), check_vma=False
    )
```

```python
import jax
import jax.numpy as jnp
from jax import lax
from jax.experimental import pallas as pl
from jax.experimental.pallas import tpu as pltpu
from jax.sharding import PartitionSpec as P

MIB = 1024 * 1024
LANES = 128
BLOCKS_PER_COPY = 32


def in_hbm(*arrays):
    return [pltpu.with_memory_space_constraint(array, pltpu.HBM) for array in arrays]


def make_requests(chips, small, factors):
    many = [max(1, factor.shape[0] // BLOCKS_PER_COPY) for factor in factors]

    def kernel(*refs):
        sources, whole, out_ref, staged = refs[:4], refs[4:6], refs[6], refs[7:9]
        held, sem, whole_sem = refs[9:13], refs[13], refs[14]
        copies = [
            pltpu.make_async_copy(source, target, sem.at[at]) for at, (source, target) in enumerate(zip(sources, held))
        ]
        for copy in copies:
            copy.start()
        staging = []
        for source, target, parts in zip(whole, staged, many):
            size = source.shape[0] // parts
            for part in range(parts):
                piece = pl.ds(part * size, size)
                staging.append(
                    pltpu.make_async_copy(source.at[piece], target.at[piece], whole_sem.at[len(staging)])
                )
                staging[-1].start()
        out_ref[...] = jnp.zeros(out_ref.shape, jnp.int32)
        for at, copy in enumerate(copies):
            copy.wait()
            row = held[at][...]
            for chip in range(chips):
                out_ref[chip, at : at + 1, 0 : row.shape[1]] = row
        for copy in staging:
            copy.wait()

    return pl.pallas_call(
        kernel,
        out_shape=[jax.ShapeDtypeStruct((chips, 4, LANES), jnp.int32)]
        + [jax.ShapeDtypeStruct(factor.shape, factor.dtype) for factor in factors],
        in_specs=[pl.BlockSpec(memory_space=pltpu.HBM)] * 6,
        out_specs=[pl.BlockSpec(memory_space=pltpu.VMEM)] * 3,
        scratch_shapes=[pltpu.VMEM(array.shape, jnp.int32) for array in small]
        + [pltpu.SemaphoreType.DMA((4,)), pltpu.SemaphoreType.DMA((sum(many),))],
        compiler_params=pltpu.CompilerParams(vmem_limit_bytes=8 * MIB),
        name="make_requests",
    )(*in_hbm(*small, *factors))


def gather_rows(asked, count, mine, paired):
    chips = asked.shape[0]
    rows, rank = mine[0].shape[1:]

    def kernel(asked_ref, mine_b, mine_c, pair_b, pair_c, out_ref, index_ref, sem):
        copy = pltpu.make_async_copy(asked_ref, index_ref, sem)
        copy.start()
        side = lax.rem(lax.axis_index("tiles"), 2)
        copy.wait()
        for chip in range(chips):
            for mode, (own, other) in enumerate(((mine_b, pair_b), (mine_c, pair_c))):
                for which in range(count):
                    block = index_ref[chip, 2 * mode + 1, index_ref[chip, 2 * mode, which]]
                    out_ref[chip, mode * count + which, side] = own[block]
                    out_ref[chip, mode * count + which, 1 - side] = other[block]

    return pl.pallas_call(
        kernel,
        out_shape=jax.ShapeDtypeStruct((chips, 2 * count, 2, rows, rank), mine[0].dtype),
        in_specs=[pl.BlockSpec(memory_space=pl.ANY)] + [pl.BlockSpec(memory_space=pltpu.VMEM)] * 4,
        out_specs=pl.BlockSpec(memory_space=pltpu.VMEM),
        scratch_shapes=[pltpu.SMEM(asked.shape, jnp.int32), pltpu.SemaphoreType.DMA],
        compiler_params=pltpu.CompilerParams(vmem_limit_bytes=8 * MIB),
        name="gather_rows",
    )(asked, *mine, *paired)


def contract(owners, fetched, order, tiles, groups):
    chips, wants, halves, rows, rank = fetched.shape
    count, inner, width = tiles.shape
    across = chips * halves * rows
    depth = width // across
    step = max(1, 256 // depth)

    def kernel(owners_ref, fetched_ref, tiles_ref, own_ref, send_ref, factor_ref, index_ref, sem):
        copy = pltpu.make_async_copy(owners_ref, index_ref, sem)
        copy.start()
        me = lax.axis_index("blk")
        for want in range(wants):
            for came, chip in enumerate(order):
                for half in range(halves):
                    at = (chip * halves + half) * rows
                    factor_ref[want, at : at + rows, :] = fetched_ref[came, want, half].astype(jnp.float32)
        terms = []
        for which in range(count):
            mode_three = factor_ref[count + which].astype(jnp.bfloat16)
            term = jnp.zeros((inner, rank), jnp.float32)
            for start in range(0, across, step):
                product = jnp.concatenate(
                    [
                        jnp.broadcast_to(factor_ref[which, j : j + 1, :], (depth, rank)).astype(jnp.bfloat16)
                        * mode_three
                        for j in range(start, start + step)
                    ],
                    axis=0,
                )
                term = term + jnp.dot(
                    tiles_ref[which, :, start * depth : (start + step) * depth],
                    product,
                    preferred_element_type=jnp.float32,
                )
            terms.append(term)
        copy.wait()
        for shift in range(groups):
            group = lax.rem(me + shift, groups)
            total = jnp.zeros((inner, rank), jnp.float32)
            for which in range(count):
                total = total + jnp.where(index_ref[0, which] == group, terms[which], 0.0)
            rounded = total.astype(jnp.bfloat16)
            if shift == 0:
                own_ref[...] = rounded
            else:
                send_ref[shift - 1] = rounded

    return pl.pallas_call(
        kernel,
        out_shape=(
            jax.ShapeDtypeStruct((inner, rank), jnp.bfloat16),
            jax.ShapeDtypeStruct((groups - 1, inner, rank), jnp.bfloat16),
        ),
        in_specs=[
            pl.BlockSpec(memory_space=pltpu.HBM),
            pl.BlockSpec(memory_space=pltpu.VMEM),
            pl.BlockSpec(memory_space=pltpu.VMEM),
        ],
        out_specs=(pl.BlockSpec(memory_space=pltpu.VMEM), pl.BlockSpec(memory_space=pltpu.VMEM)),
        scratch_shapes=[
            pltpu.VMEM((wants, across, rank), jnp.float32),
            pltpu.SMEM(owners.shape, jnp.int32),
            pltpu.SemaphoreType.DMA,
        ],
        compiler_params=pltpu.CompilerParams(vmem_limit_bytes=16 * MIB),
        name="contract",
    )(*in_hbm(owners), fetched, tiles)


def per_device(
    tensor_tiles, tile_iblock, tile_jslot, tile_kslot, block_jlist, block_klist, factor_b, factor_c
):
    groups = lax.axis_size("blk")
    size = lax.axis_size("tiles")
    chips = size // 2
    order = [(chip + chips // 2) % chips for chip in range(chips)]
    sides = [[2 * chip + side for chip in order] for side in range(2)]

    def exchange(array):
        return lax.all_to_all(array, "tiles", split_axis=0, concat_axis=0, tiled=True, axis_index_groups=sides)

    factors = (factor_b, factor_c)
    paired = [lax.ppermute(factor, "tiles", [(at, at ^ 1) for at in range(size)]) for factor in factors]
    requests, *mine = make_requests(chips, (tile_jslot, block_jlist, tile_kslot, block_klist), factors)
    asked = exchange(requests)
    fetched = exchange(gather_rows(asked, tile_jslot.shape[1], mine, paired))
    own, send = contract(tile_iblock, fetched, order, tensor_tiles[0], groups)
    total = own.astype(jnp.float32)
    for shift in range(1, groups):
        arrived = lax.ppermute(
            send[shift - 1], "blk", [(i, (i + shift) % groups) for i in range(groups)]
        )
        total = total + arrived.astype(jnp.float32)
    return total


def solution(mesh):
    placed = (
        P("blk", "tiles", None, None),
        P("blk", "tiles"),
        P("blk", "tiles"),
        P("blk", "tiles"),
        P("blk", "tiles"),
        P("blk", "tiles"),
        P(None, "tiles", None),
        P(None, "tiles", None),
    )
    return jax.shard_map(
        per_device, mesh=mesh, in_specs=placed, out_specs=P(("blk", "tiles"), None), check_vma=False
    )
```

```python
import jax
import jax.numpy as jnp
from jax import lax
from jax.experimental import pallas as pl
from jax.experimental.pallas import tpu as pltpu
from jax.sharding import PartitionSpec as P

MIB = 1024 * 1024
LANES = 128


def in_hbm(*arrays):
    return [pltpu.with_memory_space_constraint(array, pltpu.HBM) for array in arrays]


def make_requests(chips, owners, slots_two, slots_three, list_two, list_three, factor_b, factor_c):
    count = owners.shape[1]
    listed = list_two.shape[1]
    small = (owners, slots_two, slots_three, list_two, list_three)
    factors = (factor_b, factor_c)

    def kernel(*refs):
        sources, outs, held, sem = refs[:7], refs[7:10], refs[10:15], refs[15]
        copies = [
            pltpu.make_async_copy(source, target, sem.at[at])
            for at, (source, target) in enumerate(zip(sources, (*held, *outs[1:])))
        ]
        for copy in copies:
            copy.start()
        for copy in copies[:5]:
            copy.wait()
        own, slot_two, slot_three, two, three = held
        words = []
        for slot, table in ((slot_two, two), (slot_three, three)):
            for which in range(count):
                word = table[0, 0]
                for entry in range(1, listed):
                    word = jnp.where(slot[0, which] == entry, table[0, entry], word)
                words.append(word)
        words.extend(own[0, which] for which in range(count))
        lane = lax.broadcasted_iota(jnp.int32, (1, LANES), 1)
        row = jnp.zeros((1, LANES), jnp.int32)
        for at, word in enumerate(words):
            row = jnp.where(lane == at, word, row)
        for chip in range(chips):
            outs[0][chip] = row
        for copy in copies[5:]:
            copy.wait()

    return pl.pallas_call(
        kernel,
        out_shape=[jax.ShapeDtypeStruct((chips, 1, LANES), jnp.int32)]
        + [jax.ShapeDtypeStruct(factor.shape, factor.dtype) for factor in factors],
        in_specs=[pl.BlockSpec(memory_space=pltpu.HBM)] * 7,
        out_specs=[pl.BlockSpec(memory_space=pltpu.VMEM)] * 3,
        scratch_shapes=[pltpu.SMEM(array.shape, jnp.int32) for array in small] + [pltpu.SemaphoreType.DMA((7,))],
        compiler_params=pltpu.CompilerParams(vmem_limit_bytes=8 * MIB),
        name="make_requests",
    )(*in_hbm(*small, *factors))


def gather_rows(asked, count, mine, paired):
    chips = asked.shape[0]
    wants = 2 * count
    rows, rank = mine[0].shape[1:]

    def kernel(asked_ref, mine_b, mine_c, pair_b, pair_c, out_ref, index_ref, sem):
        copy = pltpu.make_async_copy(asked_ref, index_ref, sem)
        copy.start()
        side = lax.rem(lax.axis_index("tiles"), 2)
        copy.wait()
        for chip in range(chips):
            for want in range(wants):
                own, other = (mine_b, pair_b) if want < count else (mine_c, pair_c)
                block = index_ref[chip, 0, want]
                out_ref[chip, want, side] = own[block]
                out_ref[chip, want, 1 - side] = other[block]

    return pl.pallas_call(
        kernel,
        out_shape=jax.ShapeDtypeStruct((chips, wants, 2, rows, rank), mine[0].dtype),
        in_specs=[pl.BlockSpec(memory_space=pl.ANY)] + [pl.BlockSpec(memory_space=pltpu.VMEM)] * 4,
        out_specs=pl.BlockSpec(memory_space=pltpu.VMEM),
        scratch_shapes=[pltpu.SMEM(asked.shape, jnp.int32), pltpu.SemaphoreType.DMA],
        compiler_params=pltpu.CompilerParams(vmem_limit_bytes=8 * MIB),
        name="gather_rows",
    )(asked, *mine, *paired)


def contract(requests, fetched, order, tiles, groups):
    chips, wants, halves, rows, rank = fetched.shape
    count, inner, width = tiles.shape
    across = chips * halves * rows
    depth = width // across
    step = max(1, 256 // depth)

    def kernel(requests_ref, fetched_ref, tiles_ref, own_ref, send_ref, factor_ref, index_ref, sem):
        copy = pltpu.make_async_copy(requests_ref.at[0], index_ref, sem)
        copy.start()
        me = lax.axis_index("blk")
        for want in range(wants):
            for came, chip in enumerate(order):
                for half in range(halves):
                    at = (chip * halves + half) * rows
                    factor_ref[want, at : at + rows, :] = fetched_ref[came, want, half].astype(jnp.float32)
        terms = []
        for which in range(count):
            mode_three = factor_ref[count + which].astype(jnp.bfloat16)
            term = jnp.zeros((inner, rank), jnp.float32)
            for start in range(0, across, step):
                product = jnp.concatenate(
                    [
                        jnp.broadcast_to(factor_ref[which, j : j + 1, :], (depth, rank)).astype(jnp.bfloat16)
                        * mode_three
                        for j in range(start, start + step)
                    ],
                    axis=0,
                )
                term = term + jnp.dot(
                    tiles_ref[which, :, start * depth : (start + step) * depth],
                    product,
                    preferred_element_type=jnp.float32,
                )
            terms.append(term)
        copy.wait()
        for shift in range(groups):
            group = lax.rem(me + shift, groups)
            total = jnp.zeros((inner, rank), jnp.float32)
            for which in range(count):
                total = total + jnp.where(index_ref[0, 2 * count + which] == group, terms[which], 0.0)
            rounded = total.astype(jnp.bfloat16)
            if shift == 0:
                own_ref[...] = rounded
            else:
                send_ref[shift - 1] = rounded

    return pl.pallas_call(
        kernel,
        out_shape=(
            jax.ShapeDtypeStruct((inner, rank), jnp.bfloat16),
            jax.ShapeDtypeStruct((groups - 1, inner, rank), jnp.bfloat16),
        ),
        in_specs=[
            pl.BlockSpec(memory_space=pl.ANY),
            pl.BlockSpec(memory_space=pltpu.VMEM),
            pl.BlockSpec(memory_space=pltpu.VMEM),
        ],
        out_specs=(pl.BlockSpec(memory_space=pltpu.VMEM), pl.BlockSpec(memory_space=pltpu.VMEM)),
        scratch_shapes=[
            pltpu.VMEM((wants, across, rank), jnp.float32),
            pltpu.SMEM((1, LANES), jnp.int32),
            pltpu.SemaphoreType.DMA,
        ],
        compiler_params=pltpu.CompilerParams(vmem_limit_bytes=16 * MIB),
        name="contract",
    )(requests, fetched, tiles)


def per_device(
    tensor_tiles, tile_iblock, tile_jslot, tile_kslot, block_jlist, block_klist, factor_b, factor_c
):
    groups = lax.axis_size("blk")
    size = lax.axis_size("tiles")
    chips = size // 2
    order = [(chip + chips // 2 + 1) % chips for chip in range(chips)]
    same_side = [[2 * chip + side for chip in order] for side in range(2)]
    count = tensor_tiles.shape[1]

    def exchange(array):
        return lax.all_to_all(
            array, "tiles", split_axis=0, concat_axis=0, tiled=True, axis_index_groups=same_side
        )

    requests, *mine = make_requests(
        chips, tile_iblock, tile_jslot, tile_kslot, block_jlist, block_klist, factor_b, factor_c
    )
    paired = [lax.ppermute(factor, "tiles", [(at, at ^ 1) for at in range(size)]) for factor in mine]
    rows = gather_rows(exchange(requests), count, mine, paired)
    fetched = exchange(rows)
    own, send = contract(requests, fetched, order, tensor_tiles[0], groups)
    total = own.astype(jnp.float32)
    for shift in range(1, groups):
        arrived = lax.ppermute(
            send[shift - 1], "blk", [(i, (i + shift) % groups) for i in range(groups)]
        )
        total = total + arrived.astype(jnp.float32)
    return total


def solution(mesh):
    placed = (
        P("blk", "tiles", None, None),
        P("blk", "tiles"),
        P("blk", "tiles"),
        P("blk", "tiles"),
        P("blk", "tiles"),
        P("blk", "tiles"),
        P(None, "tiles", None),
        P(None, "tiles", None),
    )
    return jax.shard_map(
        per_device, mesh=mesh, in_specs=placed, out_specs=P(("blk", "tiles"), None), check_vma=False
    )
```

```python
import jax
import jax.numpy as jnp
from jax import lax
from jax.experimental import pallas as pl
from jax.experimental.pallas import tpu as pltpu
from jax.sharding import PartitionSpec as P

MIB = 1024 * 1024
LANES = 128


def in_hbm(*arrays):
    return [pltpu.with_memory_space_constraint(array, pltpu.HBM) for array in arrays]


def make_requests(chips, *small):
    def kernel(*refs):
        sources, out_ref, held, sem = refs[:4], refs[4], refs[5:9], refs[9]
        copies = [
            pltpu.make_async_copy(source, target, sem.at[at]) for at, (source, target) in enumerate(zip(sources, held))
        ]
        for copy in copies:
            copy.start()
        out_ref[...] = jnp.zeros(out_ref.shape, jnp.int32)
        for at, copy in enumerate(copies):
            copy.wait()
            row = held[at][...]
            for chip in range(chips):
                out_ref[chip, at : at + 1, 0 : row.shape[1]] = row

    return pl.pallas_call(
        kernel,
        out_shape=jax.ShapeDtypeStruct((chips, 4, LANES), jnp.int32),
        in_specs=[pl.BlockSpec(memory_space=pltpu.HBM)] * 4,
        out_specs=pl.BlockSpec(memory_space=pltpu.VMEM),
        scratch_shapes=[pltpu.VMEM(array.shape, jnp.int32) for array in small] + [pltpu.SemaphoreType.DMA((4,))],
        compiler_params=pltpu.CompilerParams(vmem_limit_bytes=8 * MIB),
        name="make_requests",
    )(*in_hbm(*small))


def stage_factors(requests, *factors):
    def kernel(requests_ref, *refs):
        sources, outs, sem = refs[:2], refs[2:4], refs[4]
        copies = [
            pltpu.make_async_copy(source, target, sem.at[at]) for at, (source, target) in enumerate(zip(sources, outs))
        ]
        for copy in copies:
            copy.start()
        for copy in copies:
            copy.wait()

    moved = 2 * sum(factor.size * factor.dtype.itemsize for factor in factors)
    return pl.pallas_call(
        kernel,
        out_shape=[jax.ShapeDtypeStruct(factor.shape, factor.dtype) for factor in factors],
        in_specs=[pl.BlockSpec(memory_space=pl.ANY)] + [pl.BlockSpec(memory_space=pltpu.HBM)] * 2,
        out_specs=[pl.BlockSpec(memory_space=pltpu.VMEM)] * 2,
        scratch_shapes=[pltpu.SemaphoreType.DMA((2,))],
        compiler_params=pltpu.CompilerParams(vmem_limit_bytes=8 * MIB),
        cost_estimate=pl.CostEstimate(flops=0, bytes_accessed=moved, transcendentals=0),
        name="stage_factors",
    )(requests, *in_hbm(*factors))


def gather_rows(asked, count, mine, paired):
    chips = asked.shape[0]
    rows, rank = mine[0].shape[1:]

    def kernel(asked_ref, mine_b, mine_c, pair_b, pair_c, out_ref, index_ref, sem):
        copy = pltpu.make_async_copy(asked_ref, index_ref, sem)
        copy.start()
        side = lax.rem(lax.axis_index("tiles"), 2)
        copy.wait()
        for chip in range(chips):
            for mode, (own, other) in enumerate(((mine_b, pair_b), (mine_c, pair_c))):
                for which in range(count):
                    block = index_ref[chip, 2 * mode + 1, index_ref[chip, 2 * mode, which]]
                    out_ref[chip, mode * count + which, side] = own[block]
                    out_ref[chip, mode * count + which, 1 - side] = other[block]

    return pl.pallas_call(
        kernel,
        out_shape=jax.ShapeDtypeStruct((chips, 2 * count, 2, rows, rank), mine[0].dtype),
        in_specs=[pl.BlockSpec(memory_space=pl.ANY)] + [pl.BlockSpec(memory_space=pltpu.VMEM)] * 4,
        out_specs=pl.BlockSpec(memory_space=pltpu.VMEM),
        scratch_shapes=[pltpu.SMEM(asked.shape, jnp.int32), pltpu.SemaphoreType.DMA],
        compiler_params=pltpu.CompilerParams(vmem_limit_bytes=8 * MIB),
        name="gather_rows",
    )(asked, *mine, *paired)


def contract(owners, fetched, order, tiles, groups):
    chips, wants, halves, rows, rank = fetched.shape
    count, inner, width = tiles.shape
    across = chips * halves * rows
    depth = width // across
    step = max(1, 256 // depth)

    def kernel(owners_ref, fetched_ref, tiles_ref, own_ref, send_ref, factor_ref, index_ref, sem):
        copy = pltpu.make_async_copy(owners_ref, index_ref, sem)
        copy.start()
        me = lax.axis_index("blk")
        for want in range(wants):
            for came, chip in enumerate(order):
                for half in range(halves):
                    at = (chip * halves + half) * rows
                    factor_ref[want, at : at + rows, :] = fetched_ref[came, want, half].astype(jnp.float32)
        terms = []
        for which in range(count):
            mode_three = factor_ref[count + which].astype(jnp.bfloat16)
            term = jnp.zeros((inner, rank), jnp.float32)
            for start in range(0, across, step):
                product = jnp.concatenate(
                    [
                        jnp.broadcast_to(factor_ref[which, j : j + 1, :], (depth, rank)).astype(jnp.bfloat16)
                        * mode_three
                        for j in range(start, start + step)
                    ],
                    axis=0,
                )
                term = term + jnp.dot(
                    tiles_ref[which, :, start * depth : (start + step) * depth],
                    product,
                    preferred_element_type=jnp.float32,
                )
            terms.append(term)
        copy.wait()
        for shift in range(groups):
            group = lax.rem(me + shift, groups)
            total = jnp.zeros((inner, rank), jnp.float32)
            for which in range(count):
                total = total + jnp.where(index_ref[0, which] == group, terms[which], 0.0)
            rounded = total.astype(jnp.bfloat16)
            if shift == 0:
                own_ref[...] = rounded
            else:
                send_ref[shift - 1] = rounded

    return pl.pallas_call(
        kernel,
        out_shape=(
            jax.ShapeDtypeStruct((inner, rank), jnp.bfloat16),
            jax.ShapeDtypeStruct((groups - 1, inner, rank), jnp.bfloat16),
        ),
        in_specs=[
            pl.BlockSpec(memory_space=pltpu.HBM),
            pl.BlockSpec(memory_space=pltpu.VMEM),
            pl.BlockSpec(memory_space=pltpu.VMEM),
        ],
        out_specs=(pl.BlockSpec(memory_space=pltpu.VMEM), pl.BlockSpec(memory_space=pltpu.VMEM)),
        scratch_shapes=[
            pltpu.VMEM((wants, across, rank), jnp.float32),
            pltpu.SMEM(owners.shape, jnp.int32),
            pltpu.SemaphoreType.DMA,
        ],
        compiler_params=pltpu.CompilerParams(vmem_limit_bytes=16 * MIB),
        name="contract",
    )(*in_hbm(owners), fetched, tiles)


def per_device(
    tensor_tiles, tile_iblock, tile_jslot, tile_kslot, block_jlist, block_klist, factor_b, factor_c
):
    groups = lax.axis_size("blk")
    size = lax.axis_size("tiles")
    chips = size // 2
    order = [(chip + chips // 2 + 1) % chips for chip in range(chips)]
    same_side = [[2 * chip + side for chip in order] for side in range(2)]

    def exchange(array):
        return lax.all_to_all(
            array, "tiles", split_axis=0, concat_axis=0, tiled=True, axis_index_groups=same_side
        )

    requests = make_requests(chips, tile_jslot, block_jlist, tile_kslot, block_klist)
    asked = exchange(requests)
    mine = stage_factors(requests, factor_b, factor_c)
    paired = [lax.ppermute(factor, "tiles", [(at, at ^ 1) for at in range(size)]) for factor in mine]
    fetched = exchange(gather_rows(asked, tile_jslot.shape[1], mine, paired))
    own, send = contract(tile_iblock, fetched, order, tensor_tiles[0], groups)
    total = own.astype(jnp.float32)
    for shift in range(1, groups):
        arrived = lax.ppermute(
            send[shift - 1], "blk", [(i, (i + shift) % groups) for i in range(groups)]
        )
        total = total + arrived.astype(jnp.float32)
    return total


def solution(mesh):
    placed = (
        P("blk", "tiles", None, None),
        P("blk", "tiles"),
        P("blk", "tiles"),
        P("blk", "tiles"),
        P("blk", "tiles"),
        P("blk", "tiles"),
        P(None, "tiles", None),
        P(None, "tiles", None),
    )
    return jax.shard_map(
        per_device, mesh=mesh, in_specs=placed, out_specs=P(("blk", "tiles"), None), check_vma=False
    )
```

```python
import jax
import jax.numpy as jnp
from jax import lax
from jax.experimental import pallas as pl
from jax.experimental.pallas import tpu as pltpu
from jax.sharding import PartitionSpec as P

MIB = 1024 * 1024
LANES = 128


def in_hbm(*arrays):
    return [pltpu.with_memory_space_constraint(array, pltpu.HBM) for array in arrays]


def make_requests(chips, *small):
    def kernel(*refs):
        sources, out_ref, held, sem = refs[:4], refs[4], refs[5:9], refs[9]
        copies = [
            pltpu.make_async_copy(source, target, sem.at[at]) for at, (source, target) in enumerate(zip(sources, held))
        ]
        for copy in copies:
            copy.start()
        out_ref[...] = jnp.zeros(out_ref.shape, jnp.int32)
        for at, copy in enumerate(copies):
            copy.wait()
            row = held[at][...]
            for chip in range(chips):
                out_ref[chip, at : at + 1, 0 : row.shape[1]] = row

    return pl.pallas_call(
        kernel,
        out_shape=jax.ShapeDtypeStruct((chips, 4, LANES), jnp.int32),
        in_specs=[pl.BlockSpec(memory_space=pltpu.HBM)] * 4,
        out_specs=pl.BlockSpec(memory_space=pltpu.VMEM),
        scratch_shapes=[pltpu.VMEM(array.shape, jnp.int32) for array in small] + [pltpu.SemaphoreType.DMA((4,))],
        compiler_params=pltpu.CompilerParams(vmem_limit_bytes=8 * MIB),
        name="make_requests",
    )(*in_hbm(*small))


def stage_factors(requests, *factors):
    def kernel(requests_ref, *refs):
        sources, outs, sem = refs[:2], refs[2:4], refs[4]
        copies = [
            pltpu.make_async_copy(source, target, sem.at[at]) for at, (source, target) in enumerate(zip(sources, outs))
        ]
        for copy in copies:
            copy.start()
        for copy in copies:
            copy.wait()

    moved = 2 * sum(factor.size * factor.dtype.itemsize for factor in factors)
    return pl.pallas_call(
        kernel,
        out_shape=[jax.ShapeDtypeStruct(factor.shape, factor.dtype) for factor in factors],
        in_specs=[pl.BlockSpec(memory_space=pl.ANY)] + [pl.BlockSpec(memory_space=pltpu.HBM)] * 2,
        out_specs=[pl.BlockSpec(memory_space=pltpu.VMEM)] * 2,
        scratch_shapes=[pltpu.SemaphoreType.DMA((2,))],
        compiler_params=pltpu.CompilerParams(vmem_limit_bytes=8 * MIB),
        cost_estimate=pl.CostEstimate(flops=0, bytes_accessed=moved, transcendentals=0),
        name="stage_factors",
    )(requests, *in_hbm(*factors))


def gather_rows(asked, count, mine, paired):
    chips = asked.shape[0]
    rows, rank = mine[0].shape[1:]

    def kernel(asked_ref, mine_b, mine_c, pair_b, pair_c, out_ref, index_ref, sem):
        copy = pltpu.make_async_copy(asked_ref, index_ref, sem)
        copy.start()
        side = lax.rem(lax.axis_index("tiles"), 2)
        copy.wait()
        for chip in range(chips):
            for mode, (own, other) in enumerate(((mine_b, pair_b), (mine_c, pair_c))):
                for which in range(count):
                    block = index_ref[chip, 2 * mode + 1, index_ref[chip, 2 * mode, which]]
                    out_ref[chip, mode * count + which, side] = own[block]
                    out_ref[chip, mode * count + which, 1 - side] = other[block]

    return pl.pallas_call(
        kernel,
        out_shape=jax.ShapeDtypeStruct((chips, 2 * count, 2, rows, rank), mine[0].dtype),
        in_specs=[pl.BlockSpec(memory_space=pl.ANY)] + [pl.BlockSpec(memory_space=pltpu.VMEM)] * 4,
        out_specs=pl.BlockSpec(memory_space=pltpu.VMEM),
        scratch_shapes=[pltpu.SMEM(asked.shape, jnp.int32), pltpu.SemaphoreType.DMA],
        compiler_params=pltpu.CompilerParams(vmem_limit_bytes=8 * MIB),
        name="gather_rows",
    )(asked, *mine, *paired)


def contract(owners, fetched, order, tiles, groups):
    chips, wants, halves, rows, rank = fetched.shape
    count, inner, width = tiles.shape
    across = chips * halves * rows
    depth = width // across
    step = max(1, 256 // depth)
    columns = min(rank, 256)

    def kernel(owners_ref, fetched_ref, tiles_ref, own_ref, send_ref, factor_ref, index_ref, sem):
        copy = pltpu.make_async_copy(owners_ref, index_ref, sem)
        copy.start()
        me = lax.axis_index("blk")
        for want in range(wants):
            for came, chip in enumerate(order):
                for half in range(halves):
                    at = (chip * halves + half) * rows
                    factor_ref[want, at : at + rows, :] = fetched_ref[came, want, half].astype(jnp.float32)
        terms = []
        for which in range(count):
            sums = []
            for left in range(0, rank, columns):
                here = slice(left, left + columns)
                mode_three = factor_ref[count + which, :, here].astype(jnp.bfloat16)
                term = jnp.zeros((inner, columns), jnp.float32)
                for start in range(0, across, step):
                    product = jnp.concatenate(
                        [
                            jnp.broadcast_to(factor_ref[which, j : j + 1, here], (depth, columns)).astype(jnp.bfloat16)
                            * mode_three
                            for j in range(start, start + step)
                        ],
                        axis=0,
                    )
                    term = term + jnp.dot(
                        tiles_ref[which, :, start * depth : (start + step) * depth],
                        product,
                        preferred_element_type=jnp.float32,
                    )
                sums.append(term)
            terms.append(jnp.concatenate(sums, axis=1))
        copy.wait()
        for shift in range(groups):
            group = lax.rem(me + shift, groups)
            total = jnp.zeros((inner, rank), jnp.float32)
            for which in range(count):
                total = total + jnp.where(index_ref[0, which] == group, terms[which], 0.0)
            rounded = total.astype(jnp.bfloat16)
            if shift == 0:
                own_ref[...] = rounded
            else:
                send_ref[shift - 1] = rounded

    return pl.pallas_call(
        kernel,
        out_shape=(
            jax.ShapeDtypeStruct((inner, rank), jnp.bfloat16),
            jax.ShapeDtypeStruct((groups - 1, inner, rank), jnp.bfloat16),
        ),
        in_specs=[
            pl.BlockSpec(memory_space=pltpu.HBM),
            pl.BlockSpec(memory_space=pltpu.VMEM),
            pl.BlockSpec(memory_space=pltpu.VMEM),
        ],
        out_specs=(pl.BlockSpec(memory_space=pltpu.VMEM), pl.BlockSpec(memory_space=pltpu.VMEM)),
        scratch_shapes=[
            pltpu.VMEM((wants, across, rank), jnp.float32),
            pltpu.SMEM(owners.shape, jnp.int32),
            pltpu.SemaphoreType.DMA,
        ],
        compiler_params=pltpu.CompilerParams(vmem_limit_bytes=16 * MIB),
        name="contract",
    )(*in_hbm(owners), fetched, tiles)


def per_device(
    tensor_tiles, tile_iblock, tile_jslot, tile_kslot, block_jlist, block_klist, factor_b, factor_c
):
    groups = lax.axis_size("blk")
    size = lax.axis_size("tiles")
    chips = size // 2
    order = [(chip + chips // 2 + 1) % chips for chip in range(chips)]
    same_side = [[2 * chip + side for chip in order] for side in range(2)]

    def exchange(array):
        return lax.all_to_all(
            array, "tiles", split_axis=0, concat_axis=0, tiled=True, axis_index_groups=same_side
        )

    paired = [
        lax.ppermute(factor, "tiles", [(at, at ^ 1) for at in range(size)]) for factor in (factor_b, factor_c)
    ]
    requests = make_requests(chips, tile_jslot, block_jlist, tile_kslot, block_klist)
    asked = exchange(requests)
    mine = stage_factors(requests, factor_b, factor_c)
    fetched = exchange(gather_rows(asked, tile_jslot.shape[1], mine, paired))
    own, send = contract(tile_iblock, fetched, order, tensor_tiles[0], groups)
    total = own.astype(jnp.float32)
    for shift in range(1, groups):
        arrived = lax.ppermute(
            send[shift - 1], "blk", [(i, (i + shift) % groups) for i in range(groups)]
        )
        total = total + arrived.astype(jnp.float32)
    return total


def solution(mesh):
    placed = (
        P("blk", "tiles", None, None),
        P("blk", "tiles"),
        P("blk", "tiles"),
        P("blk", "tiles"),
        P("blk", "tiles"),
        P("blk", "tiles"),
        P(None, "tiles", None),
        P(None, "tiles", None),
    )
    return jax.shard_map(
        per_device, mesh=mesh, in_specs=placed, out_specs=P(("blk", "tiles"), None), check_vma=False
    )
```

```python
import jax
import jax.numpy as jnp
from jax import lax
from jax.experimental import pallas as pl
from jax.experimental.pallas import tpu as pltpu
from jax.sharding import PartitionSpec as P

MIB = 1024 * 1024
LANES = 128
BLOCKS_PER_COPY = 32
PACKED_ROWS = 16


def in_hbm(*arrays):
    return [pltpu.with_memory_space_constraint(array, pltpu.HBM) for array in arrays]


def make_requests(chips, owners, slots_two, slots_three, list_two, list_three, factor_b, factor_c):
    count = owners.shape[1]
    listed = list_two.shape[1]
    small = (owners, slots_two, slots_three, list_two, list_three)
    factors = (factor_b, factor_c)
    many = [max(1, factor.shape[0] // BLOCKS_PER_COPY) for factor in factors]

    def kernel(*refs):
        sources, outs, landed, held = refs[:7], refs[7:10], refs[10:15], refs[15:20]
        sem, held_sem, factor_sem = refs[20:]
        copies = [
            pltpu.make_async_copy(source, target, sem.at[at]) for at, (source, target) in enumerate(zip(sources, landed))
        ]
        for copy in copies:
            copy.start()
        staging = []
        for source, target, parts in zip(sources[5:], outs[1:], many):
            size = source.shape[0] // parts
            for part in range(parts):
                piece = pl.ds(part * size, size)
                staging.append(pltpu.make_async_copy(source.at[piece], target.at[piece], factor_sem.at[len(staging)]))
                staging[-1].start()
        moves = [
            pltpu.make_async_copy(source, target, held_sem.at[at]) for at, (source, target) in enumerate(zip(landed, held))
        ]
        for copy, move in zip(copies, moves):
            copy.wait()
            move.start()
        for move in moves:
            move.wait()
        own, slot_two, slot_three, two, three = held
        words = []
        for slot, table in ((slot_two, two), (slot_three, three)):
            for which in range(count):
                word = table[0, 0]
                for entry in range(1, listed):
                    word = jnp.where(slot[0, which] == entry, table[0, entry], word)
                words.append(word)
        words.extend(own[0, which] for which in range(count))
        lane = lax.broadcasted_iota(jnp.int32, (1, LANES), 1)
        row = jnp.zeros((1, LANES), jnp.int32)
        for at, word in enumerate(words):
            row = jnp.where(lane == at, word, row)
        for chip in range(chips):
            outs[0][chip] = row
        for copy in staging:
            copy.wait()

    return pl.pallas_call(
        kernel,
        out_shape=[jax.ShapeDtypeStruct((chips, 1, LANES), jnp.int32)]
        + [jax.ShapeDtypeStruct(factor.shape, factor.dtype) for factor in factors],
        in_specs=[pl.BlockSpec(memory_space=pltpu.HBM)] * 7,
        out_specs=[pl.BlockSpec(memory_space=pltpu.VMEM)] * 3,
        scratch_shapes=[pltpu.VMEM(array.shape, jnp.int32) for array in small]
        + [pltpu.SMEM(array.shape, jnp.int32) for array in small]
        + [pltpu.SemaphoreType.DMA((parts,)) for parts in (5, 5, sum(many))],
        compiler_params=pltpu.CompilerParams(vmem_limit_bytes=8 * MIB),
        name="make_requests",
    )(*in_hbm(*small, *factors))


def gather_rows(asked, count, mine, paired):
    chips = asked.shape[0]
    wants = 2 * count
    rows, rank = mine[0].shape[1:]

    def kernel(asked_ref, mine_b, mine_c, pair_b, pair_c, out_ref, index_ref, sem):
        copy = pltpu.make_async_copy(asked_ref, index_ref, sem)
        copy.start()
        side = lax.rem(lax.axis_index("tiles"), 2)
        copy.wait()
        for chip in range(chips):
            for want in range(wants):
                own, other = (mine_b, pair_b) if want < count else (mine_c, pair_c)
                block = index_ref[chip, 0, want]
                out_ref[chip, want, side] = own[block]
                out_ref[chip, want, 1 - side] = other[block]

    return pl.pallas_call(
        kernel,
        out_shape=jax.ShapeDtypeStruct((chips, wants, 2, rows, rank), mine[0].dtype),
        in_specs=[pl.BlockSpec(memory_space=pl.ANY)] + [pl.BlockSpec(memory_space=pltpu.VMEM)] * 4,
        out_specs=pl.BlockSpec(memory_space=pltpu.VMEM),
        scratch_shapes=[pltpu.SMEM(asked.shape, jnp.int32), pltpu.SemaphoreType.DMA],
        compiler_params=pltpu.CompilerParams(vmem_limit_bytes=8 * MIB),
        name="gather_rows",
    )(asked, *mine, *paired)


def contract(requests, fetched, order, tiles, groups):
    chips, wants, halves, rows, rank = fetched.shape
    count, inner, width = tiles.shape
    across = chips * halves * rows
    depth = width // across
    step = max(1, 256 // depth)

    def kernel(requests_ref, fetched_ref, tiles_ref, own_ref, send_ref, factor_ref, index_ref, sem):
        copy = pltpu.make_async_copy(requests_ref.at[0], index_ref, sem)
        copy.start()
        me = lax.axis_index("blk")
        for want in range(wants):
            for came, chip in enumerate(order):
                for half in range(halves):
                    at = (chip * halves + half) * rows
                    factor_ref[want, at : at + rows, :] = fetched_ref[came, want, half].astype(jnp.float32)
        terms = []
        for which in range(count):
            mode_three = factor_ref[count + which].astype(jnp.bfloat16)
            term = jnp.zeros((inner, rank), jnp.float32)
            for start in range(0, across, step):
                parts = []
                for j in range(start, start + step):
                    row = jnp.broadcast_to(factor_ref[which, j : j + 1, :], (PACKED_ROWS, rank)).astype(jnp.bfloat16)
                    parts.extend(row * mode_three[k : k + PACKED_ROWS] for k in range(0, depth, PACKED_ROWS))
                product = jnp.concatenate(parts, axis=0)
                term = term + jnp.dot(
                    tiles_ref[which, :, start * depth : (start + step) * depth],
                    product,
                    preferred_element_type=jnp.float32,
                )
            terms.append(term)
        copy.wait()
        for shift in range(groups):
            group = lax.rem(me + shift, groups)
            total = jnp.zeros((inner, rank), jnp.float32)
            for which in range(count):
                total = total + jnp.where(index_ref[0, 2 * count + which] == group, terms[which], 0.0)
            rounded = total.astype(jnp.bfloat16)
            if shift == 0:
                own_ref[...] = rounded
            else:
                send_ref[shift - 1] = rounded

    return pl.pallas_call(
        kernel,
        out_shape=(
            jax.ShapeDtypeStruct((inner, rank), jnp.bfloat16),
            jax.ShapeDtypeStruct((groups - 1, inner, rank), jnp.bfloat16),
        ),
        in_specs=[
            pl.BlockSpec(memory_space=pl.ANY),
            pl.BlockSpec(memory_space=pltpu.VMEM),
            pl.BlockSpec(memory_space=pltpu.VMEM),
        ],
        out_specs=(pl.BlockSpec(memory_space=pltpu.VMEM), pl.BlockSpec(memory_space=pltpu.VMEM)),
        scratch_shapes=[
            pltpu.VMEM((wants, across, rank), jnp.float32),
            pltpu.SMEM((1, LANES), jnp.int32),
            pltpu.SemaphoreType.DMA,
        ],
        compiler_params=pltpu.CompilerParams(vmem_limit_bytes=16 * MIB),
        name="contract",
    )(requests, fetched, tiles)


def per_device(
    tensor_tiles, tile_iblock, tile_jslot, tile_kslot, block_jlist, block_klist, factor_b, factor_c
):
    groups = lax.axis_size("blk")
    size = lax.axis_size("tiles")
    chips = size // 2
    order = [(chip + chips // 2 + 1) % chips for chip in range(chips)]
    same_side = [[2 * chip + side for chip in order] for side in range(2)]
    count = tensor_tiles.shape[1]

    def exchange(array):
        return lax.all_to_all(
            array, "tiles", split_axis=0, concat_axis=0, tiled=True, axis_index_groups=same_side
        )

    requests, *mine = make_requests(
        chips, tile_iblock, tile_jslot, tile_kslot, block_jlist, block_klist, factor_b, factor_c
    )
    paired = [lax.ppermute(factor, "tiles", [(at, at ^ 1) for at in range(size)]) for factor in mine]
    rows = gather_rows(exchange(requests), count, mine, paired)
    fetched = exchange(rows)
    own, send = contract(requests, fetched, order, tensor_tiles[0], groups)
    total = own.astype(jnp.float32)
    for shift in range(1, groups):
        arrived = lax.ppermute(
            send[shift - 1], "blk", [(i, (i + shift) % groups) for i in range(groups)]
        )
        total = total + arrived.astype(jnp.float32)
    return total


def solution(mesh):
    placed = (
        P("blk", "tiles", None, None),
        P("blk", "tiles"),
        P("blk", "tiles"),
        P("blk", "tiles"),
        P("blk", "tiles"),
        P("blk", "tiles"),
        P(None, "tiles", None),
        P(None, "tiles", None),
    )
    return jax.shard_map(
        per_device, mesh=mesh, in_specs=placed, out_specs=P(("blk", "tiles"), None), check_vma=False
    )
```

```python
import jax
import jax.numpy as jnp
from jax import lax
from jax.experimental import pallas as pl
from jax.experimental.pallas import tpu as pltpu
from jax.sharding import PartitionSpec as P

MIB = 1024 * 1024
LANES = 128


def in_hbm(*arrays):
    return [pltpu.with_memory_space_constraint(array, pltpu.HBM) for array in arrays]


def make_requests(chips, owners, slots_two, slots_three, list_two, list_three, factor_b, factor_c):
    count = owners.shape[1]
    listed = list_two.shape[1]
    small = (owners, slots_two, slots_three, list_two, list_three)
    factors = (factor_b, factor_c)

    def kernel(*refs):
        sources, outs, held, sem = refs[:7], refs[7:10], refs[10:15], refs[15]
        copies = [
            pltpu.make_async_copy(source, target, sem.at[at])
            for at, (source, target) in enumerate(zip(sources, (*held, *outs[1:])))
        ]
        for copy in copies:
            copy.start()
        for copy in copies[:5]:
            copy.wait()
        own, slot_two, slot_three, two, three = held
        words = []
        for slot, table in ((slot_two, two), (slot_three, three)):
            for which in range(count):
                word = table[0, 0]
                for entry in range(1, listed):
                    word = jnp.where(slot[0, which] == entry, table[0, entry], word)
                words.append(word)
        words.extend(own[0, which] for which in range(count))
        lane = lax.broadcasted_iota(jnp.int32, (1, LANES), 1)
        row = jnp.zeros((1, LANES), jnp.int32)
        for at, word in enumerate(words):
            row = jnp.where(lane == at, word, row)
        for chip in range(chips):
            outs[0][chip] = row
        for copy in copies[5:]:
            copy.wait()

    return pl.pallas_call(
        kernel,
        out_shape=[jax.ShapeDtypeStruct((chips, 1, LANES), jnp.int32)]
        + [jax.ShapeDtypeStruct(factor.shape, factor.dtype) for factor in factors],
        in_specs=[pl.BlockSpec(memory_space=pltpu.HBM)] * 7,
        out_specs=[pl.BlockSpec(memory_space=pltpu.VMEM)] * 3,
        scratch_shapes=[pltpu.SMEM(array.shape, jnp.int32) for array in small] + [pltpu.SemaphoreType.DMA((7,))],
        compiler_params=pltpu.CompilerParams(vmem_limit_bytes=8 * MIB),
        name="make_requests",
    )(*in_hbm(*small, *factors))


def gather_rows(asked, count, mine, paired):
    chips = asked.shape[0]
    wants = 2 * count
    rows, rank = mine[0].shape[1:]

    def kernel(asked_ref, mine_b, mine_c, pair_b, pair_c, out_ref):
        side = lax.rem(lax.axis_index("tiles"), 2)
        for chip in range(chips):
            words = asked_ref[chip]
            for want in range(wants):
                own, other = (mine_b, pair_b) if want < count else (mine_c, pair_c)
                block = words[0, want]
                out_ref[chip, want, side] = own[block]
                out_ref[chip, want, 1 - side] = other[block]

    return pl.pallas_call(
        kernel,
        out_shape=jax.ShapeDtypeStruct((chips, wants, 2, rows, rank), mine[0].dtype),
        in_specs=[pl.BlockSpec(memory_space=pltpu.VMEM)] * 5,
        out_specs=pl.BlockSpec(memory_space=pltpu.VMEM),
        compiler_params=pltpu.CompilerParams(vmem_limit_bytes=8 * MIB),
        name="gather_rows",
    )(asked, *mine, *paired)


def contract(requests, fetched, order, tiles, groups):
    chips, wants, halves, rows, rank = fetched.shape
    count, inner, width = tiles.shape
    across = chips * halves * rows
    depth = width // across
    step = max(1, 1024 // depth)

    def kernel(requests_ref, fetched_ref, tiles_ref, own_ref, send_ref, factor_ref, index_ref, sem):
        copy = pltpu.make_async_copy(requests_ref.at[0], index_ref, sem)
        copy.start()
        me = lax.axis_index("blk")
        for want in range(wants):
            for came, chip in enumerate(order):
                for half in range(halves):
                    at = (chip * halves + half) * rows
                    factor_ref[want, at : at + rows, :] = fetched_ref[came, want, half].astype(jnp.float32)
        terms = []
        for which in range(count):
            mode_three = factor_ref[count + which].astype(jnp.bfloat16)
            term = jnp.zeros((inner, rank), jnp.float32)
            for start in range(0, across, step):
                product = jnp.concatenate(
                    [
                        jnp.broadcast_to(factor_ref[which, j : j + 1, :], (depth, rank)).astype(jnp.bfloat16)
                        * mode_three
                        for j in range(start, start + step)
                    ],
                    axis=0,
                )
                term = term + jnp.dot(
                    tiles_ref[which, :, start * depth : (start + step) * depth],
                    product,
                    preferred_element_type=jnp.float32,
                )
            terms.append(term)
        copy.wait()
        for shift in range(groups):
            group = lax.rem(me + shift, groups)
            total = jnp.zeros((inner, rank), jnp.float32)
            for which in range(count):
                total = total + jnp.where(index_ref[0, 2 * count + which] == group, terms[which], 0.0)
            rounded = total.astype(jnp.bfloat16)
            if shift == 0:
                own_ref[...] = rounded
            else:
                send_ref[shift - 1] = rounded

    return pl.pallas_call(
        kernel,
        out_shape=(
            jax.ShapeDtypeStruct((inner, rank), jnp.bfloat16),
            jax.ShapeDtypeStruct((groups - 1, inner, rank), jnp.bfloat16),
        ),
        in_specs=[
            pl.BlockSpec(memory_space=pl.ANY),
            pl.BlockSpec(memory_space=pltpu.VMEM),
            pl.BlockSpec(memory_space=pltpu.VMEM),
        ],
        out_specs=(pl.BlockSpec(memory_space=pltpu.VMEM), pl.BlockSpec(memory_space=pltpu.VMEM)),
        scratch_shapes=[
            pltpu.VMEM((wants, across, rank), jnp.float32),
            pltpu.SMEM((1, LANES), jnp.int32),
            pltpu.SemaphoreType.DMA,
        ],
        compiler_params=pltpu.CompilerParams(vmem_limit_bytes=16 * MIB),
        name="contract",
    )(requests, fetched, tiles)


def per_device(
    tensor_tiles, tile_iblock, tile_jslot, tile_kslot, block_jlist, block_klist, factor_b, factor_c
):
    groups = lax.axis_size("blk")
    size = lax.axis_size("tiles")
    chips = size // 2
    order = [(chip + chips // 2 + 1) % chips for chip in range(chips)]
    same_side = [[2 * chip + side for chip in order] for side in range(2)]
    count = tensor_tiles.shape[1]

    def exchange(array):
        return lax.all_to_all(
            array, "tiles", split_axis=0, concat_axis=0, tiled=True, axis_index_groups=same_side
        )

    requests, *mine = make_requests(
        chips, tile_iblock, tile_jslot, tile_kslot, block_jlist, block_klist, factor_b, factor_c
    )
    paired = [lax.ppermute(factor, "tiles", [(at, at ^ 1) for at in range(size)]) for factor in mine]
    rows = gather_rows(exchange(requests), count, mine, paired)
    fetched = exchange(rows)
    own, send = contract(requests, fetched, order, tensor_tiles[0], groups)
    total = own.astype(jnp.float32)
    for shift in range(1, groups):
        arrived = lax.ppermute(
            send[shift - 1], "blk", [(i, (i + shift) % groups) for i in range(groups)]
        )
        total = total + arrived.astype(jnp.float32)
    return total


def solution(mesh):
    placed = (
        P("blk", "tiles", None, None),
        P("blk", "tiles"),
        P("blk", "tiles"),
        P("blk", "tiles"),
        P("blk", "tiles"),
        P("blk", "tiles"),
        P(None, "tiles", None),
        P(None, "tiles", None),
    )
    return jax.shard_map(
        per_device, mesh=mesh, in_specs=placed, out_specs=P(("blk", "tiles"), None), check_vma=False
    )
```

```python
import jax
import jax.numpy as jnp
from jax import lax
from jax.experimental import pallas as pl
from jax.experimental.pallas import tpu as pltpu
from jax.sharding import PartitionSpec as P

MIB = 1024 * 1024
LANES = 128
BLOCKS_PER_COPY = 32


def in_hbm(*arrays):
    return [pltpu.with_memory_space_constraint(array, pltpu.HBM) for array in arrays]


def make_requests(chips, owners, slots_two, slots_three, list_two, list_three, factor_b, factor_c):
    count = owners.shape[1]
    listed = list_two.shape[1]
    small = (owners, slots_two, slots_three, list_two, list_three)
    factors = (factor_b, factor_c)
    many = [max(1, factor.shape[0] // BLOCKS_PER_COPY) for factor in factors]
    blocks = sum(factor.shape[0] for factor in factors)

    def kernel(*refs):
        sources, wide, out_ref, staged_ref = refs[:5], refs[5:7], refs[7], refs[8]
        held, sem, wide_sem = refs[9:14], refs[14], refs[15]
        copies = [
            pltpu.make_async_copy(source, target, sem.at[at]) for at, (source, target) in enumerate(zip(sources, held))
        ]
        for copy in copies:
            copy.start()
        staging, first = [], 0
        for source, parts in zip(wide, many):
            size = source.shape[0] // parts
            for part in range(parts):
                staging.append(
                    pltpu.make_async_copy(
                        source.at[pl.ds(part * size, size)],
                        staged_ref.at[pl.ds(first + part * size, size)],
                        wide_sem.at[len(staging)],
                    )
                )
                staging[-1].start()
            first += source.shape[0]
        for copy in copies:
            copy.wait()
        own, slot_two, slot_three, two, three = (ref[...] for ref in held)
        words = []
        for slot, table in ((slot_two, two), (slot_three, three)):
            for which in range(count):
                word = table[0, 0]
                for entry in range(1, listed):
                    word = jnp.where(slot[0, which] == entry, table[0, entry], word)
                words.append(word)
        words.extend(own[0, which] for which in range(count))
        lane = lax.broadcasted_iota(jnp.int32, (1, LANES), 1)
        row = jnp.zeros((1, LANES), jnp.int32)
        for at, word in enumerate(words):
            row = jnp.where(lane == at, word, row)
        for chip in range(chips):
            out_ref[chip] = row
        for copy in staging:
            copy.wait()

    return pl.pallas_call(
        kernel,
        out_shape=[
            jax.ShapeDtypeStruct((chips, 1, LANES), jnp.int32),
            jax.ShapeDtypeStruct((blocks, *factor_b.shape[1:]), factor_b.dtype),
        ],
        in_specs=[pl.BlockSpec(memory_space=pltpu.HBM)] * 7,
        out_specs=[pl.BlockSpec(memory_space=pltpu.VMEM)] * 2,
        scratch_shapes=[pltpu.VMEM(array.shape, jnp.int32) for array in small]
        + [pltpu.SemaphoreType.DMA((5,)), pltpu.SemaphoreType.DMA((sum(many),))],
        compiler_params=pltpu.CompilerParams(vmem_limit_bytes=8 * MIB),
        name="make_requests",
    )(*in_hbm(*small, *factors))


def gather_rows(asked, count, first_three, mine, paired):
    chips = asked.shape[0]
    wants = 2 * count
    rows, rank = mine.shape[1:]

    def kernel(asked_ref, mine_ref, paired_ref, out_ref):
        side = lax.rem(lax.axis_index("tiles"), 2)
        for chip in range(chips):
            words = asked_ref[chip]
            for want in range(wants):
                block = words[0, want] + (0 if want < count else first_three)
                out_ref[chip, want, side] = mine_ref[block]
                out_ref[chip, want, 1 - side] = paired_ref[block]

    return pl.pallas_call(
        kernel,
        out_shape=jax.ShapeDtypeStruct((chips, wants, 2, rows, rank), mine.dtype),
        in_specs=[pl.BlockSpec(memory_space=pltpu.VMEM)] * 3,
        out_specs=pl.BlockSpec(memory_space=pltpu.VMEM),
        compiler_params=pltpu.CompilerParams(vmem_limit_bytes=8 * MIB),
        name="gather_rows",
    )(asked, mine, paired)


def contract(requests, fetched, order, tiles, groups):
    chips, wants, halves, rows, rank = fetched.shape
    count, inner, width = tiles.shape
    across = chips * halves * rows
    depth = width // across
    step = max(1, 256 // depth)

    def kernel(requests_ref, fetched_ref, tiles_ref, own_ref, send_ref, factor_ref, index_ref, sem):
        copy = pltpu.make_async_copy(requests_ref.at[0], index_ref, sem)
        copy.start()
        me = lax.axis_index("blk")
        for want in range(wants):
            for came, chip in enumerate(order):
                for half in range(halves):
                    at = (chip * halves + half) * rows
                    factor_ref[want, at : at + rows, :] = fetched_ref[came, want, half].astype(jnp.float32)
        terms = []
        for which in range(count):
            mode_three = factor_ref[count + which].astype(jnp.bfloat16)
            term = jnp.zeros((inner, rank), jnp.float32)
            for start in range(0, across, step):
                product = jnp.concatenate(
                    [
                        jnp.broadcast_to(factor_ref[which, j : j + 1, :], (depth, rank)).astype(jnp.bfloat16)
                        * mode_three
                        for j in range(start, start + step)
                    ],
                    axis=0,
                )
                term = term + jnp.dot(
                    tiles_ref[which, :, start * depth : (start + step) * depth],
                    product,
                    preferred_element_type=jnp.float32,
                )
            terms.append(term)
        copy.wait()
        for shift in range(groups):
            group = lax.rem(me + shift, groups)
            total = jnp.zeros((inner, rank), jnp.float32)
            for which in range(count):
                total = total + jnp.where(index_ref[0, 2 * count + which] == group, terms[which], 0.0)
            rounded = total.astype(jnp.bfloat16)
            if shift == 0:
                own_ref[...] = rounded
            else:
                send_ref[shift - 1] = rounded

    return pl.pallas_call(
        kernel,
        out_shape=(
            jax.ShapeDtypeStruct((inner, rank), jnp.bfloat16),
            jax.ShapeDtypeStruct((groups - 1, inner, rank), jnp.bfloat16),
        ),
        in_specs=[
            pl.BlockSpec(memory_space=pl.ANY),
            pl.BlockSpec(memory_space=pltpu.VMEM),
            pl.BlockSpec(memory_space=pltpu.VMEM),
        ],
        out_specs=(pl.BlockSpec(memory_space=pltpu.VMEM), pl.BlockSpec(memory_space=pltpu.VMEM)),
        scratch_shapes=[
            pltpu.VMEM((wants, across, rank), jnp.float32),
            pltpu.SMEM((1, LANES), jnp.int32),
            pltpu.SemaphoreType.DMA,
        ],
        compiler_params=pltpu.CompilerParams(vmem_limit_bytes=16 * MIB),
        name="contract",
    )(requests, fetched, tiles)


def per_device(
    tensor_tiles, tile_iblock, tile_jslot, tile_kslot, block_jlist, block_klist, factor_b, factor_c
):
    groups = lax.axis_size("blk")
    size = lax.axis_size("tiles")
    chips = size // 2
    order = [(chip + chips // 2 + 1) % chips for chip in range(chips)]
    same_side = [[2 * chip + side for chip in order] for side in range(2)]
    count = tensor_tiles.shape[1]

    def exchange(array):
        return lax.all_to_all(
            array, "tiles", split_axis=0, concat_axis=0, tiled=True, axis_index_groups=same_side
        )

    requests, mine = make_requests(
        chips, tile_iblock, tile_jslot, tile_kslot, block_jlist, block_klist, factor_b, factor_c
    )
    paired = lax.ppermute(mine, "tiles", [(at, at ^ 1) for at in range(size)])
    rows = gather_rows(exchange(requests), count, factor_b.shape[0], mine, paired)
    fetched = exchange(rows)
    own, send = contract(requests, fetched, order, tensor_tiles[0], groups)
    total = own.astype(jnp.float32)
    for shift in range(1, groups):
        arrived = lax.ppermute(
            send[shift - 1], "blk", [(i, (i + shift) % groups) for i in range(groups)]
        )
        total = total + arrived.astype(jnp.float32)
    return total


def solution(mesh):
    placed = (
        P("blk", "tiles", None, None),
        P("blk", "tiles"),
        P("blk", "tiles"),
        P("blk", "tiles"),
        P("blk", "tiles"),
        P("blk", "tiles"),
        P(None, "tiles", None),
        P(None, "tiles", None),
    )
    return jax.shard_map(
        per_device, mesh=mesh, in_specs=placed, out_specs=P(("blk", "tiles"), None), check_vma=False
    )
```

```python
import jax
import jax.numpy as jnp
from jax import lax
from jax.experimental import pallas as pl
from jax.experimental.pallas import tpu as pltpu
from jax.sharding import PartitionSpec as P

MIB = 1024 * 1024
LANES = 128
BLOCKS_PER_COPY = 256


def in_hbm(*arrays):
    return [pltpu.with_memory_space_constraint(array, pltpu.HBM) for array in arrays]


def make_requests(chips, owners, slots_two, slots_three, list_two, list_three, factor_b, factor_c):
    count = owners.shape[1]
    listed = list_two.shape[1]
    small = (owners, slots_two, slots_three, list_two, list_three)
    factors = (factor_b, factor_c)
    many = [max(1, factor.shape[0] // BLOCKS_PER_COPY) for factor in factors]
    blocks = sum(factor.shape[0] for factor in factors)

    def kernel(*refs):
        sources, wide, out_ref, staged_ref = refs[:5], refs[5:7], refs[7], refs[8]
        held, sem, wide_sem = refs[9:14], refs[14], refs[15]
        copies = [
            pltpu.make_async_copy(source, target, sem.at[at]) for at, (source, target) in enumerate(zip(sources, held))
        ]
        for copy in copies:
            copy.start()
        staging, first = [], 0
        for source, parts in zip(wide, many):
            size = source.shape[0] // parts
            for part in range(parts):
                staging.append(
                    pltpu.make_async_copy(
                        source.at[pl.ds(part * size, size)],
                        staged_ref.at[pl.ds(first + part * size, size)],
                        wide_sem.at[len(staging)],
                    )
                )
                staging[-1].start()
            first += source.shape[0]
        for copy in copies:
            copy.wait()
        own, slot_two, slot_three, two, three = (ref[...] for ref in held)
        words = []
        for slot, table in ((slot_two, two), (slot_three, three)):
            for which in range(count):
                word = table[0, 0]
                for entry in range(1, listed):
                    word = jnp.where(slot[0, which] == entry, table[0, entry], word)
                words.append(word)
        words.extend(own[0, which] for which in range(count))
        lane = lax.broadcasted_iota(jnp.int32, (1, LANES), 1)
        row = jnp.zeros((1, LANES), jnp.int32)
        for at, word in enumerate(words):
            row = jnp.where(lane == at, word, row)
        for chip in range(chips):
            out_ref[chip] = row
        for copy in staging:
            copy.wait()

    return pl.pallas_call(
        kernel,
        out_shape=[
            jax.ShapeDtypeStruct((chips, 1, LANES), jnp.int32),
            jax.ShapeDtypeStruct((blocks, *factor_b.shape[1:]), factor_b.dtype),
        ],
        in_specs=[pl.BlockSpec(memory_space=pltpu.HBM)] * 7,
        out_specs=[pl.BlockSpec(memory_space=pltpu.VMEM)] * 2,
        scratch_shapes=[pltpu.VMEM(array.shape, jnp.int32) for array in small]
        + [pltpu.SemaphoreType.DMA((5,)), pltpu.SemaphoreType.DMA((sum(many),))],
        compiler_params=pltpu.CompilerParams(vmem_limit_bytes=8 * MIB),
        name="make_requests",
    )(*in_hbm(*small, *factors))


def gather_rows(asked, count, first_three, mine, paired):
    chips = asked.shape[0]
    wants = 2 * count
    rows, rank = mine.shape[1:]

    def kernel(asked_ref, mine_ref, paired_ref, out_ref):
        side = lax.rem(lax.axis_index("tiles"), 2)
        for chip in range(chips):
            words = asked_ref[chip]
            for want in range(wants):
                block = words[0, want] + (0 if want < count else first_three)
                out_ref[chip, want, side] = mine_ref[block]
                out_ref[chip, want, 1 - side] = paired_ref[block]

    return pl.pallas_call(
        kernel,
        out_shape=jax.ShapeDtypeStruct((chips, wants, 2, rows, rank), mine.dtype),
        in_specs=[pl.BlockSpec(memory_space=pltpu.VMEM)] * 3,
        out_specs=pl.BlockSpec(memory_space=pltpu.VMEM),
        compiler_params=pltpu.CompilerParams(vmem_limit_bytes=8 * MIB),
        name="gather_rows",
    )(asked, mine, paired)


def contract(requests, fetched, order, tiles, groups):
    chips, wants, halves, rows, rank = fetched.shape
    count, inner, width = tiles.shape
    across = chips * halves * rows
    depth = width // across
    step = max(1, 256 // depth)

    def kernel(requests_ref, fetched_ref, tiles_ref, own_ref, send_ref, factor_ref, index_ref, sem):
        copy = pltpu.make_async_copy(requests_ref.at[0], index_ref, sem)
        copy.start()
        me = lax.axis_index("blk")
        for want in range(wants):
            for came, chip in enumerate(order):
                for half in range(halves):
                    at = (chip * halves + half) * rows
                    factor_ref[want, at : at + rows, :] = fetched_ref[came, want, half].astype(jnp.float32)
        terms = []
        for which in range(count):
            mode_three = factor_ref[count + which].astype(jnp.bfloat16)
            term = jnp.zeros((inner, rank), jnp.float32)
            for start in range(0, across, step):
                product = jnp.concatenate(
                    [
                        jnp.broadcast_to(factor_ref[which, j : j + 1, :], (depth, rank)).astype(jnp.bfloat16)
                        * mode_three
                        for j in range(start, start + step)
                    ],
                    axis=0,
                )
                term = term + jnp.dot(
                    tiles_ref[which, :, start * depth : (start + step) * depth],
                    product,
                    preferred_element_type=jnp.float32,
                )
            terms.append(term)
        copy.wait()
        for shift in range(groups):
            group = lax.rem(me + shift, groups)
            total = jnp.zeros((inner, rank), jnp.float32)
            for which in range(count):
                total = total + jnp.where(index_ref[0, 2 * count + which] == group, terms[which], 0.0)
            rounded = total.astype(jnp.bfloat16)
            if shift == 0:
                own_ref[...] = rounded
            else:
                send_ref[shift - 1] = rounded

    return pl.pallas_call(
        kernel,
        out_shape=(
            jax.ShapeDtypeStruct((inner, rank), jnp.bfloat16),
            jax.ShapeDtypeStruct((groups - 1, inner, rank), jnp.bfloat16),
        ),
        in_specs=[
            pl.BlockSpec(memory_space=pl.ANY),
            pl.BlockSpec(memory_space=pltpu.VMEM),
            pl.BlockSpec(memory_space=pltpu.VMEM),
        ],
        out_specs=(pl.BlockSpec(memory_space=pltpu.VMEM), pl.BlockSpec(memory_space=pltpu.VMEM)),
        scratch_shapes=[
            pltpu.VMEM((wants, across, rank), jnp.float32),
            pltpu.SMEM((1, LANES), jnp.int32),
            pltpu.SemaphoreType.DMA,
        ],
        compiler_params=pltpu.CompilerParams(vmem_limit_bytes=16 * MIB),
        name="contract",
    )(requests, fetched, tiles)


def per_device(
    tensor_tiles, tile_iblock, tile_jslot, tile_kslot, block_jlist, block_klist, factor_b, factor_c
):
    groups = lax.axis_size("blk")
    size = lax.axis_size("tiles")
    chips = size // 2
    order = [(chip + chips // 2 + 1) % chips for chip in range(chips)]
    same_side = [[2 * chip + side for chip in order] for side in range(2)]
    count = tensor_tiles.shape[1]

    def exchange(array):
        return lax.all_to_all(
            array, "tiles", split_axis=0, concat_axis=0, tiled=True, axis_index_groups=same_side
        )

    requests, mine = make_requests(
        chips, tile_iblock, tile_jslot, tile_kslot, block_jlist, block_klist, factor_b, factor_c
    )
    paired = lax.ppermute(mine, "tiles", [(at, at ^ 1) for at in range(size)])
    rows = gather_rows(exchange(requests), count, factor_b.shape[0], mine, paired)
    fetched = exchange(rows)
    own, send = contract(requests, fetched, order, tensor_tiles[0], groups)
    total = own.astype(jnp.float32)
    for shift in range(1, groups):
        arrived = lax.ppermute(
            send[shift - 1], "blk", [(i, (i + shift) % groups) for i in range(groups)]
        )
        total = total + arrived.astype(jnp.float32)
    return total


def solution(mesh):
    placed = (
        P("blk", "tiles", None, None),
        P("blk", "tiles"),
        P("blk", "tiles"),
        P("blk", "tiles"),
        P("blk", "tiles"),
        P("blk", "tiles"),
        P(None, "tiles", None),
        P(None, "tiles", None),
    )
    return jax.shard_map(
        per_device, mesh=mesh, in_specs=placed, out_specs=P(("blk", "tiles"), None), check_vma=False
    )
```

```python
import jax
import jax.numpy as jnp
from jax import lax
from jax.experimental import pallas as pl
from jax.experimental.pallas import tpu as pltpu
from jax.sharding import PartitionSpec as P

MIB = 1024 * 1024
LANES = 128
BLOCKS_PER_COPY = 256


def in_hbm(*arrays):
    return [pltpu.with_memory_space_constraint(array, pltpu.HBM) for array in arrays]


def make_requests(chips, owners, slots_two, slots_three, list_two, list_three, factor_b, factor_c):
    count = owners.shape[1]
    listed = list_two.shape[1]
    small = (owners, slots_two, slots_three, list_two, list_three)
    factors = (factor_b, factor_c)
    many = [max(1, factor.shape[0] // BLOCKS_PER_COPY) for factor in factors]
    blocks = sum(factor.shape[0] for factor in factors)

    def kernel(*refs):
        sources, wide, out_ref, staged_ref = refs[:5], refs[5:7], refs[7], refs[8]
        held, sem, wide_sem = refs[9:14], refs[14], refs[15]
        copies = [
            pltpu.make_async_copy(source, target, sem.at[at]) for at, (source, target) in enumerate(zip(sources, held))
        ]
        for copy in copies:
            copy.start()
        staging, first = [], 0
        for source, parts in zip(wide, many):
            size = source.shape[0] // parts
            for part in range(parts):
                staging.append(
                    pltpu.make_async_copy(
                        source.at[pl.ds(part * size, size)],
                        staged_ref.at[pl.ds(first + part * size, size)],
                        wide_sem.at[len(staging)],
                    )
                )
                staging[-1].start()
            first += source.shape[0]
        for copy in copies:
            copy.wait()
        own, slot_two, slot_three, two, three = (ref[...] for ref in held)
        words = []
        for slot, table in ((slot_two, two), (slot_three, three)):
            for which in range(count):
                word = table[0, 0]
                for entry in range(1, listed):
                    word = jnp.where(slot[0, which] == entry, table[0, entry], word)
                words.append(word)
        words.extend(own[0, which] for which in range(count))
        lane = lax.broadcasted_iota(jnp.int32, (1, LANES), 1)
        row = jnp.zeros((1, LANES), jnp.int32)
        for at, word in enumerate(words):
            row = jnp.where(lane == at, word, row)
        for chip in range(chips):
            out_ref[chip] = row
        for copy in staging:
            copy.wait()

    return pl.pallas_call(
        kernel,
        out_shape=[
            jax.ShapeDtypeStruct((chips, 1, LANES), jnp.int32),
            jax.ShapeDtypeStruct((blocks, *factor_b.shape[1:]), factor_b.dtype),
        ],
        in_specs=[pl.BlockSpec(memory_space=pltpu.HBM)] * 7,
        out_specs=[pl.BlockSpec(memory_space=pltpu.VMEM)] * 2,
        scratch_shapes=[pltpu.VMEM(array.shape, jnp.int32) for array in small]
        + [pltpu.SemaphoreType.DMA((5,)), pltpu.SemaphoreType.DMA((sum(many),))],
        compiler_params=pltpu.CompilerParams(vmem_limit_bytes=8 * MIB),
        name="make_requests",
    )(*in_hbm(*small, *factors))


def gather_rows(asked, count, first_three, mine, paired):
    chips = asked.shape[0]
    wants = 2 * count
    rows, rank = mine.shape[1:]

    def kernel(asked_ref, mine_ref, paired_ref, out_ref):
        side = lax.rem(lax.axis_index("tiles"), 2)
        for chip in range(chips):
            words = asked_ref[chip]
            for want in range(wants):
                block = words[0, want] + (0 if want < count else first_three)
                out_ref[chip, want, side] = mine_ref[block]
                out_ref[chip, want, 1 - side] = paired_ref[block]

    return pl.pallas_call(
        kernel,
        out_shape=jax.ShapeDtypeStruct((chips, wants, 2, rows, rank), mine.dtype),
        in_specs=[pl.BlockSpec(memory_space=pltpu.VMEM)] * 3,
        out_specs=pl.BlockSpec(memory_space=pltpu.VMEM),
        compiler_params=pltpu.CompilerParams(vmem_limit_bytes=8 * MIB),
        name="gather_rows",
    )(asked, mine, paired)


def contract(requests, fetched, order, tiles, groups):
    chips, wants, halves, rows, rank = fetched.shape
    count, inner, width = tiles.shape
    across = chips * halves * rows
    depth = width // across
    step = max(1, 256 // depth)

    def kernel(requests_ref, fetched_ref, tiles_ref, own_ref, send_ref, factor_ref, index_ref, sem):
        copy = pltpu.make_async_copy(requests_ref.at[0], index_ref, sem)
        copy.start()
        me = lax.axis_index("blk")
        for want in range(wants):
            for came, chip in enumerate(order):
                for half in range(halves):
                    at = (chip * halves + half) * rows
                    factor_ref[want, at : at + rows, :] = fetched_ref[came, want, half].astype(jnp.float32)
        terms = []
        for which in range(count):
            mode_three = factor_ref[count + which].astype(jnp.bfloat16)
            term = jnp.zeros((inner, rank), jnp.float32)
            for start in range(0, across, step):
                product = jnp.concatenate(
                    [
                        jnp.broadcast_to(factor_ref[which, j : j + 1, :], (depth, rank)).astype(jnp.bfloat16)
                        * mode_three
                        for j in range(start, start + step)
                    ],
                    axis=0,
                )
                term = term + jnp.dot(
                    tiles_ref[which, :, start * depth : (start + step) * depth],
                    product,
                    preferred_element_type=jnp.float32,
                )
            terms.append(term)
        copy.wait()
        for shift in range(groups):
            group = lax.rem(me + shift, groups)
            total = jnp.zeros((inner, rank), jnp.float32)
            for which in range(count):
                total = total + jnp.where(index_ref[0, 2 * count + which] == group, terms[which], 0.0)
            rounded = total.astype(jnp.bfloat16)
            if shift == 0:
                own_ref[...] = rounded
            else:
                send_ref[shift - 1] = rounded

    return pl.pallas_call(
        kernel,
        out_shape=(
            jax.ShapeDtypeStruct((inner, rank), jnp.bfloat16),
            jax.ShapeDtypeStruct((groups - 1, inner, rank), jnp.bfloat16),
        ),
        in_specs=[
            pl.BlockSpec(memory_space=pl.ANY),
            pl.BlockSpec(memory_space=pltpu.VMEM),
            pl.BlockSpec(memory_space=pltpu.VMEM),
        ],
        out_specs=(pl.BlockSpec(memory_space=pltpu.VMEM), pl.BlockSpec(memory_space=pltpu.VMEM)),
        scratch_shapes=[
            pltpu.VMEM((wants, across, rank), jnp.float32),
            pltpu.SMEM((1, LANES), jnp.int32),
            pltpu.SemaphoreType.DMA,
        ],
        compiler_params=pltpu.CompilerParams(vmem_limit_bytes=16 * MIB),
        name="contract",
    )(requests, fetched, tiles)


def per_device(
    tensor_tiles, tile_iblock, tile_jslot, tile_kslot, block_jlist, block_klist, factor_b, factor_c
):
    groups = lax.axis_size("blk")
    size = lax.axis_size("tiles")
    chips = size // 2
    half = chips // 2
    upper = [half + (1 + 2 * at) % half for at in range(half // 2)] + [half + 2 * at % half for at in range(half // 2)]
    lower = [2 * at for at in range(half // 2)] + [1 + 2 * at for at in range(half // 2)]
    order = [chip for both in zip(upper, lower) for chip in both]
    same_side = [[2 * chip + side for chip in order] for side in range(2)]
    count = tensor_tiles.shape[1]

    def exchange(array):
        return lax.all_to_all(
            array, "tiles", split_axis=0, concat_axis=0, tiled=True, axis_index_groups=same_side
        )

    requests, mine = make_requests(
        chips, tile_iblock, tile_jslot, tile_kslot, block_jlist, block_klist, factor_b, factor_c
    )
    paired = lax.ppermute(mine, "tiles", [(at, at ^ 1) for at in range(size)])
    rows = gather_rows(exchange(requests), count, factor_b.shape[0], mine, paired)
    fetched = exchange(rows)
    own, send = contract(requests, fetched, order, tensor_tiles[0], groups)
    total = own.astype(jnp.float32)
    for shift in range(1, groups):
        arrived = lax.ppermute(
            send[shift - 1], "blk", [(i, (i + shift) % groups) for i in range(groups)]
        )
        total = total + arrived.astype(jnp.float32)
    return total


def solution(mesh):
    placed = (
        P("blk", "tiles", None, None),
        P("blk", "tiles"),
        P("blk", "tiles"),
        P("blk", "tiles"),
        P("blk", "tiles"),
        P("blk", "tiles"),
        P(None, "tiles", None),
        P(None, "tiles", None),
    )
    return jax.shard_map(
        per_device, mesh=mesh, in_specs=placed, out_specs=P(("blk", "tiles"), None), check_vma=False
    )
```

```python
import jax
import jax.numpy as jnp
from jax import lax
from jax.experimental import pallas as pl
from jax.experimental.pallas import tpu as pltpu
from jax.sharding import PartitionSpec as P

MIB = 1024 * 1024
LANES = 128
BLOCKS_PER_COPY = 256


def in_hbm(*arrays):
    return [pltpu.with_memory_space_constraint(array, pltpu.HBM) for array in arrays]


def make_requests(chips, owners, slots_two, slots_three, list_two, list_three, factor_b, factor_c):
    count = owners.shape[1]
    listed = list_two.shape[1]
    small = (owners, slots_two, slots_three, list_two, list_three)
    factors = (factor_b, factor_c)
    many = [max(1, factor.shape[0] // BLOCKS_PER_COPY) for factor in factors]
    blocks = sum(factor.shape[0] for factor in factors)

    def kernel(*refs):
        sources, wide, out_ref, staged_ref = refs[:5], refs[5:7], refs[7], refs[8]
        held, sem, wide_sem = refs[9:14], refs[14], refs[15]
        copies = [
            pltpu.make_async_copy(source, target, sem.at[at]) for at, (source, target) in enumerate(zip(sources, held))
        ]
        for copy in copies:
            copy.start()
        staging, first = [], 0
        for source, parts in zip(wide, many):
            size = source.shape[0] // parts
            for part in range(parts):
                staging.append(
                    pltpu.make_async_copy(
                        source.at[pl.ds(part * size, size)],
                        staged_ref.at[pl.ds(first + part * size, size)],
                        wide_sem.at[len(staging)],
                    )
                )
                staging[-1].start()
            first += source.shape[0]
        for copy in copies:
            copy.wait()
        own, slot_two, slot_three, two, three = (ref[...] for ref in held)
        words = []
        for slot, table in ((slot_two, two), (slot_three, three)):
            for which in range(count):
                word = table[0, 0]
                for entry in range(1, listed):
                    word = jnp.where(slot[0, which] == entry, table[0, entry], word)
                words.append(word)
        words.extend(own[0, which] for which in range(count))
        lane = lax.broadcasted_iota(jnp.int32, (1, LANES), 1)
        row = jnp.zeros((1, LANES), jnp.int32)
        for at, word in enumerate(words):
            row = jnp.where(lane == at, word, row)
        for chip in range(chips):
            out_ref[chip] = row
        for copy in staging:
            copy.wait()

    return pl.pallas_call(
        kernel,
        out_shape=[
            jax.ShapeDtypeStruct((chips, 1, LANES), jnp.int32),
            jax.ShapeDtypeStruct((blocks, *factor_b.shape[1:]), factor_b.dtype),
        ],
        in_specs=[pl.BlockSpec(memory_space=pltpu.HBM)] * 7,
        out_specs=[pl.BlockSpec(memory_space=pltpu.VMEM)] * 2,
        scratch_shapes=[pltpu.VMEM(array.shape, jnp.int32) for array in small]
        + [pltpu.SemaphoreType.DMA((5,)), pltpu.SemaphoreType.DMA((sum(many),))],
        compiler_params=pltpu.CompilerParams(vmem_limit_bytes=8 * MIB),
        name="make_requests",
    )(*in_hbm(*small, *factors))


def gather_rows(asked, count, first_three, mine, paired):
    chips = asked.shape[0]
    wants = 2 * count
    rows, rank = mine.shape[1:]

    def kernel(asked_ref, mine_ref, paired_ref, out_ref):
        side = lax.rem(lax.axis_index("tiles"), 2)
        for chip in range(chips):
            words = asked_ref[chip]
            for want in range(wants):
                block = words[0, want] + (0 if want < count else first_three)
                out_ref[chip, want, side] = mine_ref[block]
                out_ref[chip, want, 1 - side] = paired_ref[block]

    return pl.pallas_call(
        kernel,
        out_shape=jax.ShapeDtypeStruct((chips, wants, 2, rows, rank), mine.dtype),
        in_specs=[pl.BlockSpec(memory_space=pltpu.VMEM)] * 3,
        out_specs=pl.BlockSpec(memory_space=pltpu.VMEM),
        compiler_params=pltpu.CompilerParams(vmem_limit_bytes=8 * MIB),
        name="gather_rows",
    )(asked, mine, paired)


def contract(requests, fetched, order, tiles, groups):
    chips, wants, halves, rows, rank = fetched.shape
    count, inner, width = tiles.shape
    across = chips * halves * rows
    depth = width // across
    step = max(1, 256 // depth)

    def kernel(requests_ref, fetched_ref, tiles_ref, own_ref, send_ref, factor_ref, index_ref, sem):
        copy = pltpu.make_async_copy(requests_ref.at[0], index_ref, sem)
        copy.start()
        me = lax.axis_index("blk")
        for want in range(wants):
            for came, chip in enumerate(order):
                for half in range(halves):
                    at = (chip * halves + half) * rows
                    factor_ref[want, at : at + rows, :] = fetched_ref[came, want, half].astype(jnp.float32)
        terms = []
        for which in range(count):
            mode_three = factor_ref[count + which].astype(jnp.bfloat16)
            term = jnp.zeros((inner, rank), jnp.float32)
            for start in range(0, across, step):
                product = jnp.concatenate(
                    [
                        jnp.broadcast_to(factor_ref[which, j : j + 1, :], (depth, rank)).astype(jnp.bfloat16)
                        * mode_three
                        for j in range(start, start + step)
                    ],
                    axis=0,
                )
                term = term + jnp.dot(
                    tiles_ref[which, :, start * depth : (start + step) * depth],
                    product,
                    preferred_element_type=jnp.float32,
                )
            terms.append(term)
        copy.wait()
        for shift in range(groups):
            group = lax.rem(me + shift, groups)
            total = jnp.zeros((inner, rank), jnp.float32)
            for which in range(count):
                total = total + jnp.where(index_ref[0, 2 * count + which] == group, terms[which], 0.0)
            rounded = total.astype(jnp.bfloat16)
            if shift == 0:
                own_ref[...] = rounded
            else:
                send_ref[shift - 1] = rounded

    return pl.pallas_call(
        kernel,
        out_shape=(
            jax.ShapeDtypeStruct((inner, rank), jnp.bfloat16),
            jax.ShapeDtypeStruct((groups - 1, inner, rank), jnp.bfloat16),
        ),
        in_specs=[
            pl.BlockSpec(memory_space=pl.ANY),
            pl.BlockSpec(memory_space=pltpu.VMEM),
            pl.BlockSpec(memory_space=pltpu.VMEM),
        ],
        out_specs=(pl.BlockSpec(memory_space=pltpu.VMEM), pl.BlockSpec(memory_space=pltpu.VMEM)),
        scratch_shapes=[
            pltpu.VMEM((wants, across, rank), jnp.float32),
            pltpu.SMEM((1, LANES), jnp.int32),
            pltpu.SemaphoreType.DMA,
        ],
        compiler_params=pltpu.CompilerParams(vmem_limit_bytes=16 * MIB),
        name="contract",
    )(requests, fetched, tiles)


def per_device(
    tensor_tiles, tile_iblock, tile_jslot, tile_kslot, block_jlist, block_klist, factor_b, factor_c
):
    groups = lax.axis_size("blk")
    size = lax.axis_size("tiles")
    chips = size // 2
    half = chips // 2
    upper = sorted(range(half, chips), key=lambda chip: (chip != half + 1, chip))
    lower = list(range(half))[::-1]
    order = [chip for both in zip(upper, lower) for chip in both]
    same_side = [[2 * chip + side for chip in order] for side in range(2)]
    count = tensor_tiles.shape[1]

    def exchange(array):
        return lax.all_to_all(
            array, "tiles", split_axis=0, concat_axis=0, tiled=True, axis_index_groups=same_side
        )

    requests, mine = make_requests(
        chips, tile_iblock, tile_jslot, tile_kslot, block_jlist, block_klist, factor_b, factor_c
    )
    paired = lax.ppermute(mine, "tiles", [(at, at ^ 1) for at in range(size)])
    rows = gather_rows(exchange(requests), count, factor_b.shape[0], mine, paired)
    fetched = exchange(rows)
    own, send = contract(requests, fetched, order, tensor_tiles[0], groups)
    total = own.astype(jnp.float32)
    for shift in range(1, groups):
        arrived = lax.ppermute(
            send[shift - 1], "blk", [(i, (i + shift) % groups) for i in range(groups)]
        )
        total = total + arrived.astype(jnp.float32)
    return total


def solution(mesh):
    placed = (
        P("blk", "tiles", None, None),
        P("blk", "tiles"),
        P("blk", "tiles"),
        P("blk", "tiles"),
        P("blk", "tiles"),
        P("blk", "tiles"),
        P(None, "tiles", None),
        P(None, "tiles", None),
    )
    return jax.shard_map(
        per_device, mesh=mesh, in_specs=placed, out_specs=P(("blk", "tiles"), None), check_vma=False
    )
```

```python
import jax
import jax.numpy as jnp
from jax import lax
from jax.experimental import pallas as pl
from jax.experimental.pallas import tpu as pltpu
from jax.sharding import PartitionSpec as P

MIB = 1024 * 1024
LANES = 128
BLOCKS_PER_COPY = 256


def in_hbm(*arrays):
    return [pltpu.with_memory_space_constraint(array, pltpu.HBM) for array in arrays]


def make_requests(chips, owners, slots_two, slots_three, list_two, list_three, factor_b, factor_c):
    count = owners.shape[1]
    listed = list_two.shape[1]
    small = (owners, slots_two, slots_three, list_two, list_three)
    factors = (factor_b, factor_c)
    many = [max(1, factor.shape[0] // BLOCKS_PER_COPY) for factor in factors]
    blocks = sum(factor.shape[0] for factor in factors)

    def kernel(*refs):
        sources, wide, out_ref, staged_ref = refs[:5], refs[5:7], refs[7], refs[8]
        held, sem, wide_sem = refs[9:14], refs[14], refs[15]
        copies = [
            pltpu.make_async_copy(source, target, sem.at[at]) for at, (source, target) in enumerate(zip(sources, held))
        ]
        for copy in copies:
            copy.start()
        staging, first = [], 0
        for source, parts in zip(wide, many):
            size = source.shape[0] // parts
            for part in range(parts):
                staging.append(
                    pltpu.make_async_copy(
                        source.at[pl.ds(part * size, size)],
                        staged_ref.at[pl.ds(first + part * size, size)],
                        wide_sem.at[len(staging)],
                    )
                )
                staging[-1].start()
            first += source.shape[0]
        for copy in copies:
            copy.wait()
        own, slot_two, slot_three, two, three = (ref[...] for ref in held)
        words = []
        for slot, table in ((slot_two, two), (slot_three, three)):
            for which in range(count):
                word = table[0, 0]
                for entry in range(1, listed):
                    word = jnp.where(slot[0, which] == entry, table[0, entry], word)
                words.append(word)
        words.extend(own[0, which] for which in range(count))
        lane = lax.broadcasted_iota(jnp.int32, (1, LANES), 1)
        row = jnp.zeros((1, LANES), jnp.int32)
        for at, word in enumerate(words):
            row = jnp.where(lane == at, word, row)
        for chip in range(chips):
            out_ref[chip] = row
        for copy in staging:
            copy.wait()

    return pl.pallas_call(
        kernel,
        out_shape=[
            jax.ShapeDtypeStruct((chips, 1, LANES), jnp.int32),
            jax.ShapeDtypeStruct((blocks, *factor_b.shape[1:]), factor_b.dtype),
        ],
        in_specs=[pl.BlockSpec(memory_space=pltpu.HBM)] * 7,
        out_specs=[pl.BlockSpec(memory_space=pltpu.VMEM)] * 2,
        scratch_shapes=[pltpu.VMEM(array.shape, jnp.int32) for array in small]
        + [pltpu.SemaphoreType.DMA((5,)), pltpu.SemaphoreType.DMA((sum(many),))],
        compiler_params=pltpu.CompilerParams(vmem_limit_bytes=8 * MIB),
        name="make_requests",
    )(*in_hbm(*small, *factors))


def gather_rows(asked, count, first_three, mine, paired):
    chips = asked.shape[0]
    wants = 2 * count
    rows, rank = mine.shape[1:]

    def kernel(asked_ref, mine_ref, paired_ref, out_ref):
        side = lax.rem(lax.axis_index("tiles"), 2)
        for chip in range(chips):
            words = asked_ref[chip]
            for want in range(wants):
                block = words[0, want] + (0 if want < count else first_three)
                out_ref[chip, want, side] = mine_ref[block]
                out_ref[chip, want, 1 - side] = paired_ref[block]

    return pl.pallas_call(
        kernel,
        out_shape=jax.ShapeDtypeStruct((chips, wants, 2, rows, rank), mine.dtype),
        in_specs=[pl.BlockSpec(memory_space=pltpu.VMEM)] * 3,
        out_specs=pl.BlockSpec(memory_space=pltpu.VMEM),
        compiler_params=pltpu.CompilerParams(vmem_limit_bytes=8 * MIB),
        name="gather_rows",
    )(asked, mine, paired)


def contract(requests, fetched, order, tiles, groups):
    chips, wants, halves, rows, rank = fetched.shape
    count, inner, width = tiles.shape
    across = chips * halves * rows
    depth = width // across
    step = max(1, 256 // depth)

    def kernel(requests_ref, fetched_ref, tiles_ref, own_ref, send_ref, factor_ref):
        words = requests_ref[0]
        me = lax.axis_index("blk")
        for want in range(wants):
            for came, chip in enumerate(order):
                for half in range(halves):
                    at = (chip * halves + half) * rows
                    factor_ref[want, at : at + rows, :] = fetched_ref[came, want, half].astype(jnp.float32)
        terms = []
        for which in range(count):
            mode_three = factor_ref[count + which].astype(jnp.bfloat16)
            term = jnp.zeros((inner, rank), jnp.float32)
            for start in range(0, across, step):
                product = jnp.concatenate(
                    [
                        jnp.broadcast_to(factor_ref[which, j : j + 1, :], (depth, rank)).astype(jnp.bfloat16)
                        * mode_three
                        for j in range(start, start + step)
                    ],
                    axis=0,
                )
                term = term + jnp.dot(
                    tiles_ref[which, :, start * depth : (start + step) * depth],
                    product,
                    preferred_element_type=jnp.float32,
                )
            terms.append(term)
        for shift in range(groups):
            group = lax.rem(me + shift, groups)
            total = jnp.zeros((inner, rank), jnp.float32)
            for which in range(count):
                total = total + jnp.where(words[0, 2 * count + which] == group, terms[which], 0.0)
            rounded = total.astype(jnp.bfloat16)
            if shift == 0:
                own_ref[...] = rounded
            else:
                send_ref[shift - 1] = rounded

    return pl.pallas_call(
        kernel,
        out_shape=(
            jax.ShapeDtypeStruct((inner, rank), jnp.bfloat16),
            jax.ShapeDtypeStruct((groups - 1, inner, rank), jnp.bfloat16),
        ),
        in_specs=[pl.BlockSpec(memory_space=pltpu.VMEM)] * 3,
        out_specs=(pl.BlockSpec(memory_space=pltpu.VMEM), pl.BlockSpec(memory_space=pltpu.VMEM)),
        scratch_shapes=[pltpu.VMEM((wants, across, rank), jnp.float32)],
        compiler_params=pltpu.CompilerParams(vmem_limit_bytes=16 * MIB),
        name="contract",
    )(requests, fetched, tiles)


def per_device(
    tensor_tiles, tile_iblock, tile_jslot, tile_kslot, block_jlist, block_klist, factor_b, factor_c
):
    groups = lax.axis_size("blk")
    size = lax.axis_size("tiles")
    chips = size // 2
    half = chips // 2
    upper = [half + (1 + 2 * at) % half for at in range(half // 2)] + [half + 2 * at % half for at in range(half // 2)]
    lower = [2 * at for at in range(half // 2)] + [1 + 2 * at for at in range(half // 2)]
    order = [chip for both in zip(upper, lower) for chip in both]
    same_side = [[2 * chip + side for chip in order] for side in range(2)]
    count = tensor_tiles.shape[1]

    def exchange(array):
        return lax.all_to_all(
            array, "tiles", split_axis=0, concat_axis=0, tiled=True, axis_index_groups=same_side
        )

    requests, mine = make_requests(
        chips, tile_iblock, tile_jslot, tile_kslot, block_jlist, block_klist, factor_b, factor_c
    )
    paired = lax.ppermute(mine, "tiles", [(at, at ^ 1) for at in range(size)])
    rows = gather_rows(exchange(requests), count, factor_b.shape[0], mine, paired)
    fetched = exchange(rows)
    own, send = contract(requests, fetched, order, tensor_tiles[0], groups)
    total = own.astype(jnp.float32)
    for shift in range(1, groups):
        arrived = lax.ppermute(
            send[shift - 1], "blk", [(i, (i + shift) % groups) for i in range(groups)]
        )
        total = total + arrived.astype(jnp.float32)
    return total


def solution(mesh):
    placed = (
        P("blk", "tiles", None, None),
        P("blk", "tiles"),
        P("blk", "tiles"),
        P("blk", "tiles"),
        P("blk", "tiles"),
        P("blk", "tiles"),
        P(None, "tiles", None),
        P(None, "tiles", None),
    )
    return jax.shard_map(
        per_device, mesh=mesh, in_specs=placed, out_specs=P(("blk", "tiles"), None), check_vma=False
    )
```

```python
import jax
import jax.numpy as jnp
from jax import lax
from jax.experimental import pallas as pl
from jax.experimental.pallas import tpu as pltpu
from jax.sharding import PartitionSpec as P

MIB = 1024 * 1024
LANES = 128


def in_hbm(*arrays):
    return [pltpu.with_memory_space_constraint(array, pltpu.HBM) for array in arrays]


def make_requests(chips, *small):
    count, listed = small[0].shape[1], small[3].shape[1]

    def kernel(*refs):
        sources, out_ref, held, sem = refs[:5], refs[5], refs[6:11], refs[11]
        copies = [
            pltpu.make_async_copy(source, target, sem.at[at]) for at, (source, target) in enumerate(zip(sources, held))
        ]
        for copy in copies:
            copy.start()
        for copy in copies:
            copy.wait()
        own, slot_two, slot_three, two, three = (ref[...] for ref in held)
        words = []
        for slot, table in ((slot_two, two), (slot_three, three)):
            for which in range(count):
                word = table[0, 0]
                for entry in range(1, listed):
                    word = jnp.where(slot[0, which] == entry, table[0, entry], word)
                words.append(word)
        words.extend(own[0, which] for which in range(count))
        lane = lax.broadcasted_iota(jnp.int32, (1, LANES), 1)
        row = jnp.zeros((1, LANES), jnp.int32)
        for at, word in enumerate(words):
            row = jnp.where(lane == at, word, row)
        for chip in range(chips):
            out_ref[chip] = row

    return pl.pallas_call(
        kernel,
        out_shape=jax.ShapeDtypeStruct((chips, 1, LANES), jnp.int32),
        in_specs=[pl.BlockSpec(memory_space=pltpu.HBM)] * 5,
        out_specs=pl.BlockSpec(memory_space=pltpu.VMEM),
        scratch_shapes=[pltpu.VMEM(array.shape, jnp.int32) for array in small] + [pltpu.SemaphoreType.DMA((5,))],
        compiler_params=pltpu.CompilerParams(vmem_limit_bytes=8 * MIB),
        name="make_requests",
    )(*in_hbm(*small))


def stage_factors(requests, *factors):
    def kernel(requests_ref, *refs):
        sources, outs, sem = refs[:2], refs[2:4], refs[4]
        copies = [
            pltpu.make_async_copy(source, target, sem.at[at]) for at, (source, target) in enumerate(zip(sources, outs))
        ]
        for copy in copies:
            copy.start()
        for copy in copies:
            copy.wait()

    moved = 2 * sum(factor.size * factor.dtype.itemsize for factor in factors)
    return pl.pallas_call(
        kernel,
        out_shape=[jax.ShapeDtypeStruct(factor.shape, factor.dtype) for factor in factors],
        in_specs=[pl.BlockSpec(memory_space=pl.ANY)] + [pl.BlockSpec(memory_space=pltpu.HBM)] * 2,
        out_specs=[pl.BlockSpec(memory_space=pltpu.VMEM)] * 2,
        scratch_shapes=[pltpu.SemaphoreType.DMA((2,))],
        compiler_params=pltpu.CompilerParams(vmem_limit_bytes=8 * MIB),
        cost_estimate=pl.CostEstimate(flops=0, bytes_accessed=moved, transcendentals=0),
        name="stage_factors",
    )(requests, *in_hbm(*factors))


def gather_rows(asked, count, mine, paired):
    chips = asked.shape[0]
    wants = 2 * count
    rows, rank = mine[0].shape[1:]

    def kernel(asked_ref, mine_b, mine_c, pair_b, pair_c, out_ref):
        side = lax.rem(lax.axis_index("tiles"), 2)
        for chip in range(chips):
            words = asked_ref[chip]
            for want in range(wants):
                own, other = (mine_b, pair_b) if want < count else (mine_c, pair_c)
                block = words[0, want]
                out_ref[chip, want, side] = own[block]
                out_ref[chip, want, 1 - side] = other[block]

    return pl.pallas_call(
        kernel,
        out_shape=jax.ShapeDtypeStruct((chips, wants, 2, rows, rank), mine[0].dtype),
        in_specs=[pl.BlockSpec(memory_space=pltpu.VMEM)] * 5,
        out_specs=pl.BlockSpec(memory_space=pltpu.VMEM),
        compiler_params=pltpu.CompilerParams(vmem_limit_bytes=8 * MIB),
        name="gather_rows",
    )(asked, *mine, *paired)


def contract(requests, fetched, order, tiles, groups):
    chips, wants, halves, rows, rank = fetched.shape
    count, inner, width = tiles.shape
    across = chips * halves * rows
    depth = width // across
    step = max(1, 256 // depth)

    def kernel(requests_ref, fetched_ref, tiles_ref, own_ref, send_ref, factor_ref):
        words = requests_ref[0]
        me = lax.axis_index("blk")
        for want in range(wants):
            for came, chip in enumerate(order):
                for half in range(halves):
                    at = (chip * halves + half) * rows
                    factor_ref[want, at : at + rows, :] = fetched_ref[came, want, half].astype(jnp.float32)
        terms = []
        for which in range(count):
            mode_three = factor_ref[count + which].astype(jnp.bfloat16)
            term = jnp.zeros((inner, rank), jnp.float32)
            for start in range(0, across, step):
                product = jnp.concatenate(
                    [
                        jnp.broadcast_to(factor_ref[which, j : j + 1, :], (depth, rank)).astype(jnp.bfloat16)
                        * mode_three
                        for j in range(start, start + step)
                    ],
                    axis=0,
                )
                term = term + jnp.dot(
                    tiles_ref[which, :, start * depth : (start + step) * depth],
                    product,
                    preferred_element_type=jnp.float32,
                )
            terms.append(term)
        for shift in range(groups):
            group = lax.rem(me + shift, groups)
            total = jnp.zeros((inner, rank), jnp.float32)
            for which in range(count):
                total = total + jnp.where(words[0, 2 * count + which] == group, terms[which], 0.0)
            rounded = total.astype(jnp.bfloat16)
            if shift == 0:
                own_ref[...] = rounded
            else:
                send_ref[shift - 1] = rounded

    return pl.pallas_call(
        kernel,
        out_shape=(
            jax.ShapeDtypeStruct((inner, rank), jnp.bfloat16),
            jax.ShapeDtypeStruct((groups - 1, inner, rank), jnp.bfloat16),
        ),
        in_specs=[pl.BlockSpec(memory_space=pltpu.VMEM)] * 3,
        out_specs=(pl.BlockSpec(memory_space=pltpu.VMEM), pl.BlockSpec(memory_space=pltpu.VMEM)),
        scratch_shapes=[pltpu.VMEM((wants, across, rank), jnp.float32)],
        compiler_params=pltpu.CompilerParams(vmem_limit_bytes=16 * MIB),
        name="contract",
    )(requests, fetched, tiles)


def per_device(
    tensor_tiles, tile_iblock, tile_jslot, tile_kslot, block_jlist, block_klist, factor_b, factor_c
):
    groups = lax.axis_size("blk")
    size = lax.axis_size("tiles")
    chips = size // 2
    half = chips // 2
    upper = [half + (1 + 2 * at) % half for at in range(half // 2)] + [half + 2 * at % half for at in range(half // 2)]
    lower = [2 * at for at in range(half // 2)] + [1 + 2 * at for at in range(half // 2)]
    order = [chip for both in zip(upper, lower) for chip in both]
    same_side = [[2 * chip + side for chip in order] for side in range(2)]
    count = tensor_tiles.shape[1]

    def exchange(array):
        return lax.all_to_all(
            array, "tiles", split_axis=0, concat_axis=0, tiled=True, axis_index_groups=same_side
        )

    requests = make_requests(chips, tile_iblock, tile_jslot, tile_kslot, block_jlist, block_klist)
    requests, *later = lax.optimization_barrier((requests, factor_b, factor_c))
    paired = [lax.ppermute(factor, "tiles", [(at, at ^ 1) for at in range(size)]) for factor in later]
    asked = exchange(requests)
    mine = stage_factors(requests, factor_b, factor_c)
    rows = gather_rows(asked, count, mine, paired)
    fetched = exchange(rows)
    own, send = contract(requests, fetched, order, tensor_tiles[0], groups)
    total = own.astype(jnp.float32)
    for shift in range(1, groups):
        arrived = lax.ppermute(
            send[shift - 1], "blk", [(i, (i + shift) % groups) for i in range(groups)]
        )
        total = total + arrived.astype(jnp.float32)
    return total


def solution(mesh):
    placed = (
        P("blk", "tiles", None, None),
        P("blk", "tiles"),
        P("blk", "tiles"),
        P("blk", "tiles"),
        P("blk", "tiles"),
        P("blk", "tiles"),
        P(None, "tiles", None),
        P(None, "tiles", None),
    )
    return jax.shard_map(
        per_device, mesh=mesh, in_specs=placed, out_specs=P(("blk", "tiles"), None), check_vma=False
    )
```

```python
import jax
import jax.numpy as jnp
from jax import lax
from jax.experimental import pallas as pl
from jax.experimental.pallas import tpu as pltpu
from jax.sharding import PartitionSpec as P

MIB = 1024 * 1024
LANES = 128
BLOCKS_PER_COPY = 256


def in_hbm(*arrays):
    return [pltpu.with_memory_space_constraint(array, pltpu.HBM) for array in arrays]


def make_requests(chips, owners, slots_two, slots_three, list_two, list_three, factor_b, factor_c):
    count = owners.shape[1]
    listed = list_two.shape[1]
    small = (owners, slots_two, slots_three, list_two, list_three)
    factors = (factor_b, factor_c)
    many = [max(1, factor.shape[0] // BLOCKS_PER_COPY) for factor in factors]
    blocks = sum(factor.shape[0] for factor in factors)

    def kernel(*refs):
        sources, wide, out_ref, staged_ref = refs[:5], refs[5:7], refs[7], refs[8]
        held, sem, wide_sem = refs[9:14], refs[14], refs[15]
        copies = [
            pltpu.make_async_copy(source, target, sem.at[at]) for at, (source, target) in enumerate(zip(sources, held))
        ]
        for copy in copies:
            copy.start()
        staging, first = [], 0
        for source, parts in zip(wide, many):
            size = source.shape[0] // parts
            for part in range(parts):
                staging.append(
                    pltpu.make_async_copy(
                        source.at[pl.ds(part * size, size)],
                        staged_ref.at[pl.ds(first + part * size, size)],
                        wide_sem.at[len(staging)],
                    )
                )
                staging[-1].start()
            first += source.shape[0]
        for copy in copies:
            copy.wait()
        own, slot_two, slot_three, two, three = (ref[...] for ref in held)
        words = []
        for slot, table in ((slot_two, two), (slot_three, three)):
            for which in range(count):
                word = table[0, 0]
                for entry in range(1, listed):
                    word = jnp.where(slot[0, which] == entry, table[0, entry], word)
                words.append(word)
        words.extend(own[0, which] for which in range(count))
        lane = lax.broadcasted_iota(jnp.int32, (1, LANES), 1)
        row = jnp.zeros((1, LANES), jnp.int32)
        for at, word in enumerate(words):
            row = jnp.where(lane == at, word, row)
        for chip in range(chips):
            out_ref[chip] = row
        for copy in staging:
            copy.wait()

    return pl.pallas_call(
        kernel,
        out_shape=[
            jax.ShapeDtypeStruct((chips, 1, LANES), jnp.int32),
            jax.ShapeDtypeStruct((blocks, *factor_b.shape[1:]), factor_b.dtype),
        ],
        in_specs=[pl.BlockSpec(memory_space=pltpu.HBM)] * 7,
        out_specs=[pl.BlockSpec(memory_space=pltpu.VMEM)] * 2,
        scratch_shapes=[pltpu.VMEM(array.shape, jnp.int32) for array in small]
        + [pltpu.SemaphoreType.DMA((5,)), pltpu.SemaphoreType.DMA((sum(many),))],
        compiler_params=pltpu.CompilerParams(vmem_limit_bytes=8 * MIB),
        name="make_requests",
    )(*in_hbm(*small, *factors))


def gather_rows(asked, count, first_three, mine, paired):
    chips = asked.shape[0]
    wants = 2 * count
    rows, rank = mine.shape[1:]

    def kernel(asked_ref, mine_ref, paired_ref, out_ref):
        side = lax.rem(lax.axis_index("tiles"), 2)
        for chip in range(chips):
            words = asked_ref[chip]
            for want in range(wants):
                block = words[0, want] + (0 if want < count else first_three)
                out_ref[chip, want, side] = mine_ref[block]
                out_ref[chip, want, 1 - side] = paired_ref[block]

    return pl.pallas_call(
        kernel,
        out_shape=jax.ShapeDtypeStruct((chips, wants, 2, rows, rank), mine.dtype),
        in_specs=[pl.BlockSpec(memory_space=pltpu.VMEM)] * 3,
        out_specs=pl.BlockSpec(memory_space=pltpu.VMEM),
        compiler_params=pltpu.CompilerParams(vmem_limit_bytes=8 * MIB),
        name="gather_rows",
    )(asked, mine, paired)


def contract(requests, fetched, order, tiles, groups):
    chips, wants, halves, rows, rank = fetched.shape
    count, inner, width = tiles.shape
    across = chips * halves * rows
    depth = width // across
    step = max(1, 256 // depth)

    def kernel(requests_ref, fetched_ref, tiles_ref, own_ref, send_ref, factor_ref):
        words = requests_ref[0]
        me = lax.axis_index("blk")
        for want in range(wants):
            for came, chip in enumerate(order):
                for half in range(halves):
                    at = (chip * halves + half) * rows
                    factor_ref[want, at : at + rows, :] = fetched_ref[came, want, half].astype(jnp.float32)
        mode_three = [factor_ref[count + which].astype(jnp.bfloat16) for which in range(count)]
        terms = [jnp.zeros((inner, rank), jnp.float32)] * count
        for start in range(0, across, step):
            for which in range(count):
                product = jnp.concatenate(
                    [
                        jnp.broadcast_to(factor_ref[which, j : j + 1, :], (depth, rank)).astype(jnp.bfloat16)
                        * mode_three[which]
                        for j in range(start, start + step)
                    ],
                    axis=0,
                )
                terms[which] = terms[which] + jnp.dot(
                    tiles_ref[which, :, start * depth : (start + step) * depth],
                    product,
                    preferred_element_type=jnp.float32,
                )
        for shift in range(groups):
            group = lax.rem(me + shift, groups)
            total = jnp.zeros((inner, rank), jnp.float32)
            for which in range(count):
                total = total + jnp.where(words[0, 2 * count + which] == group, terms[which], 0.0)
            rounded = total.astype(jnp.bfloat16)
            if shift == 0:
                own_ref[...] = rounded
            else:
                send_ref[shift - 1] = rounded

    return pl.pallas_call(
        kernel,
        out_shape=(
            jax.ShapeDtypeStruct((inner, rank), jnp.bfloat16),
            jax.ShapeDtypeStruct((groups - 1, inner, rank), jnp.bfloat16),
        ),
        in_specs=[pl.BlockSpec(memory_space=pltpu.VMEM)] * 3,
        out_specs=(pl.BlockSpec(memory_space=pltpu.VMEM), pl.BlockSpec(memory_space=pltpu.VMEM)),
        scratch_shapes=[pltpu.VMEM((wants, across, rank), jnp.float32)],
        compiler_params=pltpu.CompilerParams(vmem_limit_bytes=16 * MIB),
        name="contract",
    )(requests, fetched, tiles)


def per_device(
    tensor_tiles, tile_iblock, tile_jslot, tile_kslot, block_jlist, block_klist, factor_b, factor_c
):
    groups = lax.axis_size("blk")
    size = lax.axis_size("tiles")
    chips = size // 2
    half = chips // 2
    upper = [half + (1 + 2 * at) % half for at in range(half // 2)] + [half + 2 * at % half for at in range(half // 2)]
    lower = [2 * at for at in range(half // 2)] + [1 + 2 * at for at in range(half // 2)]
    order = [chip for both in zip(upper, lower) for chip in both]
    same_side = [[2 * chip + side for chip in order] for side in range(2)]
    count = tensor_tiles.shape[1]

    def exchange(array):
        return lax.all_to_all(
            array, "tiles", split_axis=0, concat_axis=0, tiled=True, axis_index_groups=same_side
        )

    requests, mine = make_requests(
        chips, tile_iblock, tile_jslot, tile_kslot, block_jlist, block_klist, factor_b, factor_c
    )
    paired = lax.ppermute(mine, "tiles", [(at, at ^ 1) for at in range(size)])
    rows = gather_rows(exchange(requests), count, factor_b.shape[0], mine, paired)
    fetched = exchange(rows)
    own, send = contract(requests, fetched, order, tensor_tiles[0], groups)
    total = own.astype(jnp.float32)
    for shift in range(1, groups):
        arrived = lax.ppermute(
            send[shift - 1], "blk", [(i, (i + shift) % groups) for i in range(groups)]
        )
        total = total + arrived.astype(jnp.float32)
    return total


def solution(mesh):
    placed = (
        P("blk", "tiles", None, None),
        P("blk", "tiles"),
        P("blk", "tiles"),
        P("blk", "tiles"),
        P("blk", "tiles"),
        P("blk", "tiles"),
        P(None, "tiles", None),
        P(None, "tiles", None),
    )
    return jax.shard_map(
        per_device, mesh=mesh, in_specs=placed, out_specs=P(("blk", "tiles"), None), check_vma=False
    )
```

```python
import jax
import jax.numpy as jnp
from jax import lax
from jax.experimental import pallas as pl
from jax.experimental.pallas import tpu as pltpu
from jax.sharding import PartitionSpec as P

MIB = 1024 * 1024
LANES = 128
BLOCKS_PER_COPY = 256


def in_hbm(*arrays):
    return [pltpu.with_memory_space_constraint(array, pltpu.HBM) for array in arrays]


def make_requests(chips, owners, slots_two, slots_three, list_two, list_three, factor_b, factor_c):
    count = owners.shape[1]
    listed = list_two.shape[1]
    small = (owners, slots_two, slots_three, list_two, list_three)
    factors = (factor_b, factor_c)
    many = [max(1, factor.shape[0] // BLOCKS_PER_COPY) for factor in factors]
    blocks = sum(factor.shape[0] for factor in factors)

    def kernel(*refs):
        sources, wide, out_ref, staged_ref = refs[:5], refs[5:7], refs[7], refs[8]
        held, sem, wide_sem = refs[9:14], refs[14], refs[15]
        copies = [
            pltpu.make_async_copy(source, target, sem.at[at]) for at, (source, target) in enumerate(zip(sources, held))
        ]
        for copy in copies:
            copy.start()
        staging, first = [], 0
        for source, parts in zip(wide, many):
            size = source.shape[0] // parts
            for part in range(parts):
                staging.append(
                    pltpu.make_async_copy(
                        source.at[pl.ds(part * size, size)],
                        staged_ref.at[pl.ds(first + part * size, size)],
                        wide_sem.at[len(staging)],
                    )
                )
                staging[-1].start()
            first += source.shape[0]
        for copy in copies:
            copy.wait()
        own, slot_two, slot_three, two, three = (ref[...] for ref in held)
        words = []
        for slot, table in ((slot_two, two), (slot_three, three)):
            for which in range(count):
                word = table[0, 0]
                for entry in range(1, listed):
                    word = jnp.where(slot[0, which] == entry, table[0, entry], word)
                words.append(word)
        words.extend(own[0, which] for which in range(count))
        lane = lax.broadcasted_iota(jnp.int32, (1, LANES), 1)
        row = jnp.zeros((1, LANES), jnp.int32)
        for at, word in enumerate(words):
            row = jnp.where(lane == at, word, row)
        for chip in range(chips):
            out_ref[chip] = row
        for copy in staging:
            copy.wait()

    return pl.pallas_call(
        kernel,
        out_shape=[
            jax.ShapeDtypeStruct((chips, 1, LANES), jnp.int32),
            jax.ShapeDtypeStruct((blocks, *factor_b.shape[1:]), factor_b.dtype),
        ],
        in_specs=[pl.BlockSpec(memory_space=pltpu.HBM)] * 7,
        out_specs=[pl.BlockSpec(memory_space=pltpu.VMEM)] * 2,
        scratch_shapes=[pltpu.VMEM(array.shape, jnp.int32) for array in small]
        + [pltpu.SemaphoreType.DMA((5,)), pltpu.SemaphoreType.DMA((sum(many),))],
        compiler_params=pltpu.CompilerParams(vmem_limit_bytes=8 * MIB),
        name="make_requests",
    )(*in_hbm(*small, *factors))


def gather_rows(asked, turn, count, first_three, mine, paired):
    chips = asked.shape[0]
    wants = 2 * count
    rows, rank = mine.shape[1:]

    def kernel(asked_ref, mine_ref, paired_ref, out_ref):
        side = lax.rem(lax.axis_index("tiles"), 2)
        for chip in range(chips):
            words = asked_ref[(chip - turn) % chips]
            for want in range(wants):
                block = words[0, want] + (0 if want < count else first_three)
                out_ref[chip, want, side] = mine_ref[block]
                out_ref[chip, want, 1 - side] = paired_ref[block]

    return pl.pallas_call(
        kernel,
        out_shape=jax.ShapeDtypeStruct((chips, wants, 2, rows, rank), mine.dtype),
        in_specs=[pl.BlockSpec(memory_space=pltpu.VMEM)] * 3,
        out_specs=pl.BlockSpec(memory_space=pltpu.VMEM),
        compiler_params=pltpu.CompilerParams(vmem_limit_bytes=8 * MIB),
        name="gather_rows",
    )(asked, mine, paired)


def contract(requests, fetched, order, tiles, groups):
    chips, wants, halves, rows, rank = fetched.shape
    count, inner, width = tiles.shape
    across = chips * halves * rows
    depth = width // across
    step = max(1, 256 // depth)

    def kernel(requests_ref, fetched_ref, tiles_ref, own_ref, send_ref, factor_ref):
        words = requests_ref[0]
        me = lax.axis_index("blk")
        for want in range(wants):
            for came, chip in enumerate(order):
                for half in range(halves):
                    at = (chip * halves + half) * rows
                    factor_ref[want, at : at + rows, :] = fetched_ref[came, want, half].astype(jnp.float32)
        terms = []
        for which in range(count):
            mode_three = factor_ref[count + which].astype(jnp.bfloat16)
            term = jnp.zeros((inner, rank), jnp.float32)
            for start in range(0, across, step):
                product = jnp.concatenate(
                    [
                        jnp.broadcast_to(factor_ref[which, j : j + 1, :], (depth, rank)).astype(jnp.bfloat16)
                        * mode_three
                        for j in range(start, start + step)
                    ],
                    axis=0,
                )
                term = term + jnp.dot(
                    tiles_ref[which, :, start * depth : (start + step) * depth],
                    product,
                    preferred_element_type=jnp.float32,
                )
            terms.append(term)
        for shift in range(groups):
            group = lax.rem(me + shift, groups)
            total = jnp.zeros((inner, rank), jnp.float32)
            for which in range(count):
                total = total + jnp.where(words[0, 2 * count + which] == group, terms[which], 0.0)
            rounded = total.astype(jnp.bfloat16)
            if shift == 0:
                own_ref[...] = rounded
            else:
                send_ref[shift - 1] = rounded

    return pl.pallas_call(
        kernel,
        out_shape=(
            jax.ShapeDtypeStruct((inner, rank), jnp.bfloat16),
            jax.ShapeDtypeStruct((groups - 1, inner, rank), jnp.bfloat16),
        ),
        in_specs=[pl.BlockSpec(memory_space=pltpu.VMEM)] * 3,
        out_specs=(pl.BlockSpec(memory_space=pltpu.VMEM), pl.BlockSpec(memory_space=pltpu.VMEM)),
        scratch_shapes=[pltpu.VMEM((wants, across, rank), jnp.float32)],
        compiler_params=pltpu.CompilerParams(vmem_limit_bytes=16 * MIB),
        name="contract",
    )(requests, fetched, tiles)


def per_device(
    tensor_tiles, tile_iblock, tile_jslot, tile_kslot, block_jlist, block_klist, factor_b, factor_c
):
    groups = lax.axis_size("blk")
    size = lax.axis_size("tiles")
    chips = size // 2
    half = chips // 2
    upper = [half + (1 + 2 * at) % half for at in range(half // 2)] + [half + 2 * at % half for at in range(half // 2)]
    lower = [2 * at for at in range(half // 2)] + [1 + 2 * at for at in range(half // 2)]
    order = [chip for both in zip(upper, lower) for chip in both]
    same_side = [[2 * chip + side for chip in order] for side in range(2)]
    count = tensor_tiles.shape[1]

    turn = order.index(chips - 1)

    def exchange(array, turned=0):
        members = [side[turned:] + side[:turned] for side in same_side]
        return lax.all_to_all(
            array, "tiles", split_axis=0, concat_axis=0, tiled=True, axis_index_groups=members
        )

    requests, mine = make_requests(
        chips, tile_iblock, tile_jslot, tile_kslot, block_jlist, block_klist, factor_b, factor_c
    )
    paired = lax.ppermute(mine, "tiles", [(at, at ^ 1) for at in range(size)])
    rows = gather_rows(exchange(requests, turn), turn, count, factor_b.shape[0], mine, paired)
    fetched = exchange(rows)
    own, send = contract(requests, fetched, order, tensor_tiles[0], groups)
    total = own.astype(jnp.float32)
    for shift in range(1, groups):
        arrived = lax.ppermute(
            send[shift - 1], "blk", [(i, (i + shift) % groups) for i in range(groups)]
        )
        total = total + arrived.astype(jnp.float32)
    return total


def solution(mesh):
    placed = (
        P("blk", "tiles", None, None),
        P("blk", "tiles"),
        P("blk", "tiles"),
        P("blk", "tiles"),
        P("blk", "tiles"),
        P("blk", "tiles"),
        P(None, "tiles", None),
        P(None, "tiles", None),
    )
    return jax.shard_map(
        per_device, mesh=mesh, in_specs=placed, out_specs=P(("blk", "tiles"), None), check_vma=False
    )
```
